128 devices in a mesh: ctx: 8 (over z_lo, y), rec: 16 (over z_hi, x, core).
Axes of the slice: x: 4, y: 4, z: 4 (z_hi: 2, z_lo: 2; z = z_hi * 2 + z_lo), core: 2. Of those that a mesh axis runs over, the one named last changes fastest.
Arguments:
- layer_in: bfloat16 [16, 2048, 1024], P('rec', 'ctx'), may hold values from -6 to 6
- queries: bfloat16 [16, 2048, 1024], P('rec', 'ctx'), may hold values from -6 to 6, as said below
- keys: bfloat16 [16, 2048, 1024], P('rec', 'ctx'), may hold values from -6 to 6, as said below
- values: bfloat16 [16, 2048, 1024], P('rec', 'ctx'), may hold values from -6 to 6
- lengths: int32 [16], P('rec'), may hold values from 512 to 2048, as said below
- w_qkv: bfloat16 [1024, 3072], replicated, may hold values from -0.1875 to 0.1875
- w_out: bfloat16 [1024, 1024], replicated, may hold values from -0.1875 to 0.1875
- conv_kernel: float32 [9, 1024], replicated, may hold values from -2.5 to 2.5
- grad_out: bfloat16 [16, 2048, 1024], P('rec', 'ctx'), may hold values from -6 to 6
Outputs:
- d_input: bfloat16 [16, 2048, 1024], P('rec', 'ctx')
- d_w_qkv: float32 [1024, 3072], P(('ctx', 'rec'))
- d_w_out: float32 [1024, 1024], P(('ctx', 'rec'))
- d_kernel: float32 [9, 1024], replicated
The draws below stay inside these ranges and needn't reach their ends.
Inputs may be any that keep to these rules, and one draw needn't show every extreme that they name: `queries`: entries of order one. `keys`: entries of order one. `lengths`: some recording has all 2048 frames valid.
All inputs are finite; a program needn't handle non-finite values.
Results may differ from the reference program's by a relative error of at most 0.013.
Values may be sent and summed in bfloat16 or wider, within the bound.
A program may use at most 128 MiB of HBM per device.

```python
import math
import jax
import jax.numpy as jnp
from jax import lax

D = 1024
HEAD_DIM = 128
KW = 9
FRAMES = 2048
REC = 16


def draw_queries(key, part):
    key = jax.random.fold_in(key, 11)
    base = jnp.clip(jax.random.normal(key, (REC, FRAMES, D), jnp.float32), -6.0, 6.0)
    return base.astype(jnp.bfloat16)


def draw_keys(key, part):
    key = jax.random.fold_in(key, 23)
    base = jnp.clip(jax.random.normal(key, (REC, FRAMES, D), jnp.float32), -6.0, 6.0)
    return base.astype(jnp.bfloat16)


def draw_lengths(key, part):
    key = jax.random.fold_in(key, 37)
    key_len, key_full = jax.random.split(key)
    drawn = jax.random.randint(key_len, (REC,), FRAMES // 4, FRAMES + 1)
    full_index = jax.random.randint(key_full, (), 0, REC)
    return jnp.where(jnp.arange(REC) == full_index, FRAMES, drawn).astype(jnp.int32)


def raised(values, key, source, target, parts, factor):
    def block_of(dim):
        return (jnp.arange(values.shape[dim]) // (values.shape[dim] // parts)).reshape((-1,) + (1,) * (values.ndim - 1 - dim))

    one_side = jax.random.permutation(key, parts)[block_of(target)]
    far = (block_of(target) + parts // 2) % parts
    return jnp.where((block_of(source) == one_side) | (block_of(source) == far), factor * values, values)


def level_of(own_key, dims, cuts, smallest, largest):
    def one(dim, parts):
        heights = jax.random.uniform(jax.random.fold_in(jax.random.fold_in(own_key, 6), dim), (parts,), jnp.float32, smallest / len(cuts), largest / len(cuts))
        return jnp.repeat(jnp.exp(heights), dims[dim] // parts).reshape((-1,) + (1,) * (len(dims) - dim - 1))

    loudness = one(*cuts[0])
    for cut in cuts[1:]:
        loudness = loudness * one(*cut)
    return loudness


def bell_draw(rng, dims, width, most, cuts=(), held_as=jnp.bfloat16):
    result = width * jax.random.normal(rng, dims, jnp.float32)
    if cuts:
        result = result * level_of(rng, dims, cuts, -0.22, 0.18)
    return jnp.clip(result, -most, most).astype(held_as)


def gaussian_with(own_key, dims, deviation, limit, shards, heavy, kind=jnp.bfloat16):
    values = deviation * jax.random.normal(own_key, dims, jnp.float32)
    if shards:
        values = values * level_of(own_key, dims, shards, -0.22, 0.18)
    return jnp.clip(raised(values, jax.random.fold_in(own_key, 3), *heavy), -limit, limit).astype(kind)


def setup_inputs(seed: int = 0) -> dict:
    key_of = jax.random.split(jax.random.key(seed), 10)
    layer_in = gaussian_with(key_of[0], (REC, FRAMES, D), 1.0, 6.0, ((0, 16), (1, 8)), (1, 2, 8, 2.0))
    queries = draw_queries(jax.random.fold_in(key_of[9], 71), 0)
    keys = draw_keys(jax.random.fold_in(key_of[9], 71), 0)
    values = bell_draw(key_of[3], (REC, FRAMES, D), 1.0, 6.0, ((0, 16), (1, 8)))
    lengths = draw_lengths(jax.random.fold_in(key_of[9], 71), 0)
    w_qkv = bell_draw(key_of[5], (D, 3 * D), D ** -0.5, 0.1875)
    w_out = bell_draw(key_of[6], (D, D), D ** -0.5, 0.1875)
    conv_kernel = bell_draw(key_of[7], (KW, D), 0.3, 2.5, (), jnp.float32)
    grad_out = bell_draw(key_of[8], (REC, FRAMES, D), 1.0, 6.0, ((0, 16), (1, 8)))
    return dict(layer_in=layer_in, queries=queries, keys=keys, values=values, lengths=lengths, w_qkv=w_qkv, w_out=w_out, conv_kernel=conv_kernel, grad_out=grad_out)


def one_recording(inputs, w_qkv, w_out, conv_kernel):
    layer_in, queries, keys, values, length, grad_out = inputs
    n_frames, model_width = layer_in.shape
    n_heads = model_width // HEAD_DIM
    inv_root = 1.0 / math.sqrt(HEAD_DIM)
    reach = KW // 2
    q_heads = queries.astype(jnp.float32).reshape(n_frames, n_heads, HEAD_DIM)
    k_heads = keys.astype(jnp.float32).reshape(n_frames, n_heads, HEAD_DIM)
    v_heads = values.astype(jnp.float32).reshape(n_frames, n_heads, HEAD_DIM)
    valid = jnp.arange(n_frames) < length
    scores = jnp.einsum('ihe,jhe->hij', q_heads, k_heads) * inv_root
    scores = jnp.where(valid[None, None, :], scores, -jnp.inf)
    row_max = lax.optimization_barrier(jnp.max(scores, axis=-1, keepdims=True))
    log_total = row_max + jnp.log(lax.optimization_barrier(jnp.sum(jnp.exp(scores - row_max), axis=-1, keepdims=True)))
    attn_probs = jnp.exp(scores - log_total).astype(jnp.bfloat16)
    probs_f = attn_probs.astype(jnp.float32)
    attended = jnp.einsum('hij,jhe->ihe', probs_f, v_heads).reshape(n_frames, model_width).astype(jnp.bfloat16)
    sublayer = jnp.dot(attended, w_out, preferred_element_type=jnp.float32).astype(jnp.bfloat16)
    grad_f = grad_out.astype(jnp.float32)
    grad_pad = jnp.pad(grad_f, ((reach, reach), (0, 0)))
    sub_pad = jnp.pad(sublayer.astype(jnp.float32), ((reach, reach), (0, 0)))
    d_sub = grad_f
    kernel_rows = []
    for offset in range(KW):
        start = 2 * reach - offset
        d_sub = d_sub + conv_kernel[offset][None, :] * grad_pad[start:start + n_frames]
        kernel_rows.append(lax.optimization_barrier(jnp.sum(grad_f * sub_pad[offset:offset + n_frames], axis=0)))
    kernel_term = jnp.stack(kernel_rows)
    d_sub_bf = d_sub.astype(jnp.bfloat16)
    w_out_term = jnp.dot(attended.T, d_sub_bf, preferred_element_type=jnp.float32)
    d_att = jnp.dot(d_sub_bf, w_out.T, preferred_element_type=jnp.float32).astype(jnp.bfloat16)
    d_att_heads = d_att.astype(jnp.float32).reshape(n_frames, n_heads, HEAD_DIM)
    row_delta = lax.optimization_barrier(jnp.sum(d_att_heads * attended.astype(jnp.float32).reshape(n_frames, n_heads, HEAD_DIM), axis=-1)).T
    d_probs = jnp.einsum('ihe,jhe->hij', d_att_heads, v_heads)
    d_scores = (probs_f * (d_probs - row_delta[:, :, None])).astype(jnp.bfloat16).astype(jnp.float32)
    d_query = (jnp.einsum('hij,jhe->ihe', d_scores, k_heads) * inv_root).reshape(n_frames, model_width).astype(jnp.bfloat16)
    d_key = (jnp.einsum('hij,ihe->jhe', d_scores, q_heads) * inv_root).reshape(n_frames, model_width).astype(jnp.bfloat16)
    d_value = jnp.einsum('hij,ihe->jhe', probs_f, d_att_heads).reshape(n_frames, model_width).astype(jnp.bfloat16)
    qkv_grads = jnp.concatenate([d_query, d_key, d_value], axis=1)
    d_input = jnp.dot(qkv_grads, w_qkv.T, preferred_element_type=jnp.float32).astype(jnp.bfloat16)
    qkv_term = jnp.dot(layer_in.T, qkv_grads, preferred_element_type=jnp.float32)
    return (d_input, qkv_term, w_out_term, kernel_term)

def reference(layer_in, queries, keys, values, lengths, w_qkv, w_out, conv_kernel, grad_out):

    def step(inputs):
        return one_recording(inputs, w_qkv, w_out, conv_kernel)
    d_input, qkv_terms, out_terms, kernel_terms = lax.map(step, (layer_in, queries, keys, values, lengths, grad_out))
    return (d_input, lax.optimization_barrier(jnp.sum(qkv_terms, axis=0)), lax.optimization_barrier(jnp.sum(out_terms, axis=0)), lax.optimization_barrier(jnp.sum(kernel_terms, axis=0)))
```

```python
import math

import jax
import jax.numpy as jnp
from jax import lax
from jax.experimental import pallas as pl
from jax.experimental.pallas import tpu as pltpu
from jax.sharding import PartitionSpec as P

HD = 128
KW = 9
NC = 8
BF = 256
T = NC * BF
D = 1024
F32 = jnp.float32
BF16 = jnp.bfloat16
MESH = pl.DeviceIdType.MESH
KB = 512
NEG = -1e30
NT = (((1,), (1,)), ((), ()))
ANY = pl.BlockSpec(memory_space=pl.ANY)
VM = pl.BlockSpec(memory_space=pltpu.VMEM)

TQ, TK, TV, TD, BA, BQ, BK, BV = range(8)


def mult(value, of):
    return pl.multiple_of(value, of)


def dot(a, b):
    return jnp.dot(a, b, preferred_element_type=F32)


def dot_nt(a, b):
    return lax.dot_general(a, b, NT, preferred_element_type=F32)


def attention_kernel(
    len_ref, q_ref, k_ref, v_ref, g_ref, conv_ref, wout_ref,
    att_out, dsub_out, dqkv_out, dker_out,
    q_aug, k_aug, v_aug, do_in, do_aug, k_t, v_t, s_ref, e_ref, ds_ref,
    att_s, linv_s, dq_s, dk_s, dv_s, dat_s, att_fr, dq_fr, dk_fr, dv_fr,
    g_vm, gp, halo_lo, halo_hi, wout_vm,
    send_sem, recv_sem, halo_send, halo_recv, local_sem,
):
    me = lax.axis_index("ctx")
    rec = lax.axis_index("rec")
    z, y = lax.div(me, 4), lax.rem(me, 4)
    inv_root = 1.0 / math.sqrt(HD)
    c_exp = math.log2(math.e) / math.sqrt(HD)

    def peer(d):
        return lax.rem(z + lax.div(d, 4), 2) * 4 + lax.rem(y + lax.rem(d, 4), 4)

    def origin(d):
        return lax.rem(z + 2 - lax.div(d, 4), 2) * 4 + lax.rem(y + 4 - lax.rem(d, 4), 4)

    def head_cols(h):
        return pl.ds(mult(h * HD, HD), HD)

    def slot(d):
        return pl.ds(mult(d * BF, BF), BF)

    fwd_src = {TQ: q_ref, TK: k_ref, TV: v_ref}
    fwd_dst = {TQ: q_aug, TK: k_aug, TV: v_aug, TD: do_in}
    back_src = {BA: att_s, BQ: dq_s, BK: dk_s, BV: dv_s}
    back_dst = {BA: att_fr, BQ: dq_fr, BK: dk_fr, BV: dv_fr}

    def ends(t, d):
        if t <= TD:
            p = peer(d)
            src = dat_s.at[d] if t == TD else fwd_src[t].at[:, head_cols(p)]
            dst = fwd_dst[t].at[slot(d), pl.ds(0, HD)]
        else:
            p = origin(d)
            src = back_src[t].at[d]
            dst = back_dst[t].at[:, head_cols(me)]
        return p, src, dst

    def remote(t, d):
        p, src, dst = ends(t, d)
        return pltpu.make_async_remote_copy(
            src_ref=src, dst_ref=dst, send_sem=send_sem.at[t, d], recv_sem=recv_sem.at[t, d],
            device_id=(p, rec), device_id_type=MESH,
        )

    def local(t):
        _, src, dst = ends(t, 0)
        return pltpu.make_async_copy(src, dst, recv_sem.at[t, 0])

    def each_peer(body):
        def step(d, carry):
            body(d)
            return carry

        lax.fori_loop(1, NC, step, 0)

    def each_slot(body):
        def step(d, carry):
            body(d)
            return carry

        lax.fori_loop(0, NC, step, 0)

    get_g = pltpu.make_async_copy(g_ref, g_vm, local_sem.at[0])
    get_w = pltpu.make_async_copy(wout_ref, wout_vm, local_sem.at[1])
    get_g.start()
    get_w.start()
    for t in (TK, TQ, TV):
        local(t).start()

    barrier = pltpu.get_barrier_semaphore()
    each_peer(
        lambda d: pl.semaphore_signal(barrier, inc=1, device_id=(peer(d), rec), device_id_type=MESH)
    )
    pl.semaphore_wait(barrier, NC - 1)

    right, left = lax.rem(me + 1, NC), lax.rem(me + NC - 1, NC)
    to_right = pltpu.make_async_remote_copy(
        src_ref=g_ref.at[pl.ds(BF - 16, 16), :], dst_ref=halo_lo, send_sem=halo_send.at[0],
        recv_sem=halo_recv.at[0], device_id=(right, rec), device_id_type=MESH,
    )
    to_left = pltpu.make_async_remote_copy(
        src_ref=g_ref.at[pl.ds(0, 16), :], dst_ref=halo_hi, send_sem=halo_send.at[1],
        recv_sem=halo_recv.at[1], device_id=(left, rec), device_id_type=MESH,
    )
    to_right.start()
    to_left.start()
    for t in (TK, TQ, TV):
        each_peer(lambda d: remote(t, d).start())

    length = len_ref[0]
    lane = lax.broadcasted_iota(jnp.int32, (BF, HD), 1)
    row = lax.broadcasted_iota(jnp.int32, (BF, HD), 0)

    def extra(d):
        masked = (lane == 0) & (row + origin(d) * BF >= length)
        k_aug[slot(d), pl.ds(HD, HD)] = jnp.where(masked, NEG, 0.0).astype(BF16)
        q_aug[slot(d), pl.ds(HD, HD)] = jnp.where(lane == 0, 1.0, 0.0).astype(BF16)
        v_aug[slot(d), pl.ds(HD, HD)] = jnp.where(lane < 2, 1.0, 0.0).astype(BF16)

    each_slot(extra)
    first = lax.broadcasted_iota(jnp.int32, (16, T), 0) == 0
    v_t[pl.ds(HD, 16), :] = jnp.where(first, 1.0, 0.0).astype(BF16)

    get_g.wait()
    gp[pl.ds(8, BF), :] = g_vm[...].astype(F32)
    to_right.wait_recv()
    to_left.wait_recv()
    low = halo_lo[...].astype(F32)[8:16, :]
    gp[pl.ds(0, 8), :] = jnp.where(me > 0, low, 0.0)
    high = halo_hi[...].astype(F32)[0:8, :]
    gp[pl.ds(8 + BF, 8), :] = jnp.where(me < NC - 1, high, 0.0)

    def conv_grad(n):
        cols = pl.ds(mult(n * HD, HD), HD)
        total = gp[pl.ds(8, BF), cols]
        for t in range(KW):
            total = total + conv_ref[pl.ds(t, 1), cols] * gp[pl.ds(12 - t, BF), cols]
        dsub_out[:, cols] = total.astype(BF16)

    each_slot(conv_grad)

    get_w.wait()

    def datt(d):
        rows = pl.ds(mult(peer(d) * HD, HD), HD)
        dat_s[d] = dot_nt(dsub_out[...], wout_vm[rows, :]).astype(BF16)

        @pl.when(d > 0)
        def _():
            remote(TD, d).start()

    each_slot(datt)
    local(TD).start()

    for t in (TK, TV):
        local(t).wait()
        each_peer(lambda d: remote(t, d).wait_recv())

    def turn(d):
        k_t[:, slot(d)] = k_aug[slot(d), pl.ds(0, HD)].T
        v_t[pl.ds(0, HD), slot(d)] = v_aug[slot(d), pl.ds(0, HD)].T

    each_slot(turn)
    local(TQ).wait()

    def forward(d):
        @pl.when(d > 0)
        def _():
            remote(TQ, d).wait_recv()

        qd = q_aug[slot(d), :]
        top = None
        for b in range(T // KB):
            rows = pl.ds(b * KB, KB)
            s = dot_nt(k_aug[rows, :], qd)
            s_ref[rows, :] = s
            m = jnp.max(s, axis=0, keepdims=True)
            top = m if top is None else jnp.maximum(top, m)
        acc = jnp.zeros((HD + 16, BF), F32)
        for b in range(T // KB):
            rows = pl.ds(b * KB, KB)
            e = jnp.exp2((s_ref[rows, :] - top) * c_exp).astype(BF16)
            e_ref[rows, slot(d)] = e
            acc = acc + dot(v_t[:, rows], e)
        inv = 1.0 / acc[HD : HD + 1, :]
        att_s[d] = (acc[:HD, :] * inv).T.astype(BF16)
        linv_s[d] = jnp.broadcast_to(inv, (HD, BF)).T

        @pl.when(d > 0)
        def _():
            remote(BA, d).start()

    each_slot(forward)
    local(BA).start()

    local(TD).wait()

    def backward_in(d):
        @pl.when(d > 0)
        def _():
            remote(TD, d).wait_recv()

        do = (do_in[slot(d), :].astype(F32) * linv_s[d]).astype(BF16)
        delta = -jnp.sum(do.astype(F32) * att_s[d].astype(F32), axis=1, keepdims=True)
        hi = delta.astype(BF16).astype(F32)
        do_aug[slot(d), pl.ds(0, HD)] = do
        do_aug[slot(d), pl.ds(HD, HD)] = jnp.where(
            lane == 0, hi, jnp.where(lane == 1, delta - hi, 0.0)
        ).astype(BF16)

    each_slot(backward_in)

    def d_value(j):
        dv_s[j] = dot(e_ref[slot(j), :], do_aug[:, pl.ds(0, HD)]).astype(BF16)

        @pl.when(j > 0)
        def _():
            remote(BV, j).start()

    each_slot(d_value)
    local(BV).start()

    def d_query(d):
        dod = do_aug[slot(d), :]
        acc = jnp.zeros((HD, BF), F32)
        for b in range(T // KB):
            rows = pl.ds(b * KB, KB)
            dp = dot_nt(v_aug[rows, :], dod)
            ds = (e_ref[rows, slot(d)].astype(F32) * dp).astype(BF16)
            ds_ref[rows, slot(d)] = ds
            acc = acc + dot(k_t[:, rows], ds)
        dq_s[d] = (acc * inv_root).T.astype(BF16)

        @pl.when(d > 0)
        def _():
            remote(BQ, d).start()

    each_slot(d_query)
    local(BQ).start()

    def d_key(j):
        dk = dot(ds_ref[slot(j), :], q_aug[:, pl.ds(0, HD)])
        dk_s[j] = (dk * inv_root).astype(BF16)

        @pl.when(j > 0)
        def _():
            remote(BK, j).start()

    each_slot(d_key)
    local(BK).start()

    local(BA).wait()
    each_peer(lambda d: remote(BA, d).wait_recv())
    att_out[...] = att_fr[...]

    def taps(n):
        cols = pl.ds(mult(n * BF, BF), BF)
        sub = dot(att_fr[...], wout_vm[:, cols]).astype(BF16).astype(F32)
        for t in range(KW):
            dker_out[pl.ds(t, 1), cols] = jnp.sum(
                sub * gp[pl.ds(12 - t, BF), cols], axis=0, keepdims=True
            )

    dker_out[...] = jnp.zeros_like(dker_out)
    lax.fori_loop(0, D // BF, lambda n, c: (taps(n), c)[1], 0)

    for part, (t, ref) in enumerate(((BQ, dq_fr), (BK, dk_fr), (BV, dv_fr))):
        local(t).wait()
        each_peer(lambda d: remote(t, d).wait_recv())
        dqkv_out[:, pl.ds(part * D, D)] = ref[...]

    to_right.wait_send()
    to_left.wait_send()
    for t in range(8):
        each_peer(lambda d: remote(t, d).wait_send())


def attention(lengths, q, k, v, g, conv, wout):
    def vm(shape, dtype=BF16):
        return pltpu.VMEM(shape, dtype)

    return pl.pallas_call(
        attention_kernel,
        out_shape=(
            jax.ShapeDtypeStruct((BF, D), BF16),
            jax.ShapeDtypeStruct((BF, D), BF16),
            jax.ShapeDtypeStruct((BF, 3 * D), BF16),
            jax.ShapeDtypeStruct((16, D), F32),
        ),
        in_specs=[pl.BlockSpec(memory_space=pltpu.SMEM), ANY, ANY, ANY, ANY, VM, ANY],
        out_specs=(VM, VM, VM, VM),
        scratch_shapes=[
            vm((T, 2 * HD)), vm((T, 2 * HD)), vm((T, 2 * HD)), vm((T, HD)), vm((T, 2 * HD)),
            vm((HD, T)), vm((HD + 16, T)), vm((T, BF), F32), vm((T, T)), vm((T, T)),
            vm((NC, BF, HD)), vm((NC, BF, HD), F32), vm((NC, BF, HD)), vm((NC, BF, HD)),
            vm((NC, BF, HD)), vm((NC, BF, HD)), vm((BF, D)), vm((BF, D)), vm((BF, D)), vm((BF, D)),
            vm((BF, D)), vm((BF + 16, D), F32), vm((16, D)), vm((16, D)), vm((D, D)),
            pltpu.SemaphoreType.DMA((8, NC)), pltpu.SemaphoreType.DMA((8, NC)),
            pltpu.SemaphoreType.DMA((2,)), pltpu.SemaphoreType.DMA((2,)), pltpu.SemaphoreType.DMA((2,)),
        ],
        compiler_params=pltpu.CompilerParams(
            collective_id=0, has_side_effects=True, vmem_limit_bytes=56 * 1024 * 1024
        ),
    )(lengths, q, k, v, g, conv, wout)


HALF = 512
CW = 4 * HALF
PARTS = (
    (0, 384, 768, ("x", "y", "z")),
    (768, 384, 640, ("y", "z", "x")),
    (1408, 384, 640, ("z", "x", "y")),
)
LEFT = {"x": 0, "y": 1, "z": 2}


def weights_kernel(
    li_ref, dqkv_ref, att_ref, dsub_ref, dker_ref, wqkv_ref,
    din_out, dwq_out, dwo_out, dk_out,
    li2, att2, r2, li_t, att_t, grads, fin, fin_x, taps_c, taps_a, *rest,
):
    bufs = rest[:36]
    core_send, core_recv, ring_send, ring_recv, taps_send, taps_recv = rest[36:]
    ctx = lax.axis_index("ctx")
    rec = lax.axis_index("rec")
    core = lax.rem(rec, 2)
    other = 1 - core
    at = {
        "x": lax.rem(lax.div(rec, 2), 4),
        "y": lax.rem(ctx, 4),
        "z": lax.div(rec, 8) * 2 + lax.div(ctx, 4),
    }

    def device(moved, to, on_core=core):
        p = {**at, **({moved: to} if moved else {})}
        return (
            lax.rem(p["z"], 2) * 4 + p["y"],
            lax.div(p["z"], 2) * 8 + p["x"] * 2 + on_core,
        )

    def off(axis, by):
        return lax.rem(at[axis] + by, 4)

    partner = device(None, None, other)

    barrier = pltpu.get_barrier_semaphore()
    greet = [partner] + [device(a, off(a, by)) for a in "xyz" for by in (1, 2, 3)]
    for who in greet:
        pl.semaphore_signal(barrier, inc=1, device_id=who, device_id_type=MESH)
    pl.semaphore_wait(barrier, len(greet))

    def to_partner(n, src, dst):
        return pltpu.make_async_remote_copy(
            src_ref=src, dst_ref=dst, send_sem=core_send.at[n], recv_sem=core_recv.at[n],
            device_id=partner, device_id_type=MESH,
        )

    def half(ref, base, c):
        return ref.at[:, pl.ds(mult(base + c * HALF, HALF), HALF)]

    theirs = pl.ds(BF, BF)
    swaps = [
        to_partner(0, li_ref, li2.at[theirs, :]),
        to_partner(1, half(dqkv_ref, 0, other), r2.at[theirs, pl.ds(0, HALF)]),
        to_partner(2, half(dqkv_ref, D, other), r2.at[theirs, pl.ds(HALF, HALF)]),
        to_partner(3, half(dqkv_ref, 2 * D, other), r2.at[theirs, pl.ds(2 * HALF, HALF)]),
        to_partner(4, att_ref, att2.at[theirs, :]),
        to_partner(5, half(dsub_ref, 0, other), r2.at[theirs, pl.ds(3 * HALF, HALF)]),
        to_partner(6, dker_ref, taps_c.at[core]),
    ]
    for swap in swaps:
        swap.start()
    mine = pl.ds(0, BF)
    li2[mine, :] = li_ref[...]
    att2[mine, :] = att_ref[...]
    for n in range(3):
        r2[mine, pl.ds(n * HALF, HALF)] = dqkv_ref[:, pl.ds(mult(n * D + core * HALF, HALF), HALF)]
    r2[mine, pl.ds(3 * HALF, HALF)] = dsub_ref[:, pl.ds(mult(core * HALF, HALF), HALF)]
    taps_c[core] = dker_ref[...]
    for swap in swaps:
        swap.wait_recv()

    def turn(n, carry):
        cols = pl.ds(mult(n * BF, BF), BF)
        li_t[cols, :] = li2[:, cols].T
        att_t[cols, :] = att2[:, cols].T
        return carry

    lax.fori_loop(0, 4, turn, 0)

    def product(lhs, start, width):
        def step(b, carry):
            rows = pl.ds(mult(b * HD, HD), HD)
            g = dot(lhs[rows, :], r2[:, pl.ds(start, width)]).astype(BF16)
            grads[lax.div(b, 4), lax.rem(b, 4), :, :, :, pl.ds(start, width)] = g.reshape(
                2, 4, 16, width
            )
            return carry

        lax.fori_loop(0, 8, step, 0)

    def region(fixed, start, width):
        zl = zh = slice(None)
        if "z" in fixed:
            zl, zh = lax.rem(fixed["z"], 2), lax.div(fixed["z"], 2)
        return grads.at[
            zl, fixed.get("y", slice(None)), zh, fixed.get("x", slice(None)), :, pl.ds(start, width)
        ]

    class Ring:
        def __init__(self, part, stage):
            self.start, self.wide_a, self.width, order = PARTS[part]
            self.wide_b = self.width - self.wide_a
            self.axis = order[stage]
            self.fixed = {a: at[a] for a in order[:stage]}
            base = (part * 3 + stage) * 4
            self.ra, self.rb, self.low, self.high = bufs[base : base + 4]
            self.sems = (part * 3 + stage) * 6
            self.stage = stage
            a = self.wide_a
            lead = len(self.low.shape) - 1

            def cols(ref, half_b):
                pick = pl.ds(a, self.wide_b) if half_b else pl.ds(0, a)
                return ref.at[(slice(None),) * lead + (pick,)]

            self.cols = cols
            low, high = self.low, self.high
            self.copies = [
                self.copy(0, self.piece(2, 0), self.ra, 1),
                self.copy(1, self.piece(2, 1), self.rb, 3),
                self.copy(2, self.piece(1, 1), cols(low, 1), 1),
                self.copy(3, self.piece(3, 0), cols(high, 0), 3),
                self.copy(4, self.piece(1, 0), cols(low, 0), 1),
                self.copy(5, self.piece(3, 1), cols(high, 1), 3),
            ]

        def piece(self, by, half_b=None):
            start, width = self.start, self.width
            if half_b is not None:
                start, width = (
                    (start + self.wide_a, self.wide_b) if half_b else (start, self.wide_a)
                )
            return region({**self.fixed, self.axis: off(self.axis, by)}, start, width)

        def copy(self, n, src, dst, by):
            return pltpu.make_async_remote_copy(
                src_ref=src, dst_ref=dst, send_sem=ring_send.at[self.sems + n],
                recv_sem=ring_recv.at[self.sems + n],
                device_id=device(self.axis, off(self.axis, by)), device_id_type=MESH,
            )

        def begin(self):
            for c in self.copies[:4]:
                c.start()

        def relay(self):
            for n, by, buf, half_b in ((0, 1, self.ra, 0), (1, 3, self.rb, 1)):
                self.copies[n].wait_recv()
                here = self.piece(by, half_b)
                here[...] = (here[...].astype(F32) + buf[...].astype(F32)).astype(BF16)
                self.copies[4 + n].start()

        def end(self):
            for n in (2, 3, 4, 5):
                self.copies[n].wait_recv()
            here = self.piece(0)
            total = here[...].astype(F32) + self.low[...].astype(F32) + self.high[...].astype(F32)
            if self.stage < 2:
                here[...] = total.astype(BF16)
            else:
                fin[:, pl.ds(self.start, self.width)] = total

        def sent(self):
            for c in self.copies:
                c.wait_send()

    rings = [[Ring(p, s) for s in range(3)] for p in range(3)]

    product(li_t, 0, 768)
    rings[0][0].begin()
    product(li_t, 768, 640)
    rings[1][0].begin()
    product(li_t, 1408, 128)
    product(att_t, 1536, 512)
    rings[2][0].begin()

    taps_copies = []

    def taps_send_on(n, axis, value):
        taps_a[n, at[axis]] = value
        for by in (1, 2, 3):
            c = pltpu.make_async_remote_copy(
                src_ref=taps_a.at[n, at[axis]], dst_ref=taps_a.at[n, at[axis]],
                send_sem=taps_send.at[n * 3 + by - 1], recv_sem=taps_recv.at[n * 3 + by - 1],
                device_id=device(axis, off(axis, by)), device_id_type=MESH,
            )
            c.start()
            taps_copies.append(c)

    def taps_sum(n):
        for c in taps_copies[n * 3 :]:
            c.wait_recv()
        return (taps_a[n, 0] + taps_a[n, 1]) + (taps_a[n, 2] + taps_a[n, 3])

    taps_send_on(0, "x", taps_c[0] + taps_c[1])

    def d_input(n, carry):
        cols = pl.ds(mult(n * BF, BF), BF)
        din_out[:, cols] = dot_nt(dqkv_ref[...], wqkv_ref[cols, :]).astype(BF16)
        return carry

    lax.fori_loop(0, 2, d_input, 0)
    for r in rings:
        r[0].relay()
    taps_send_on(1, "y", taps_sum(0))
    lax.fori_loop(2, 4, d_input, 0)
    for stage in (0, 1):
        for r in rings:
            r[stage].end()
            r[stage + 1].begin()
        if stage == 0:
            taps_send_on(2, "z", taps_sum(1))
        for r in rings:
            r[stage + 1].relay()
    dk_out[...] = taps_sum(2)
    for r in rings:
        r[2].end()

    last = to_partner(7, fin.at[pl.ds(mult(other * 8, 8), 8), :], fin_x)
    last.start()
    for who, ref in ((core, fin), (other, fin_x)):
        if ref is fin_x:
            last.wait_recv()
            block = fin_x[...]
        else:
            block = fin[pl.ds(mult(core * 8, 8), 8), :]
        for n in range(3):
            dwq_out[:, pl.ds(mult(n * D + who * HALF, HALF), HALF)] = block[
                :, n * HALF : (n + 1) * HALF
            ]
        dwo_out[:, pl.ds(mult(who * HALF, HALF), HALF)] = block[:, 3 * HALF :]

    last.wait_send()
    for swap in swaps:
        swap.wait_send()
    for c in taps_copies:
        c.wait_send()
    for r in rings:
        for ring in r:
            ring.sent()


def weights(layer_in, dqkv, att, dsub, dker, wqkv):
    def vm(shape, dtype=BF16):
        return pltpu.VMEM(shape, dtype)

    buffers = []
    for start, wide_a, width, order in PARTS:
        for stage in range(3):
            lead = []
            for axis, sizes in (("zl", 2), ("y", 4), ("zh", 2), ("x", 4)):
                if axis[0] not in order[: stage + 1]:
                    lead.append(sizes)
            for w in (wide_a, width - wide_a, width, width):
                buffers.append(vm((*lead, 16, w)))
    dma = pltpu.SemaphoreType.DMA
    return pl.pallas_call(
        weights_kernel,
        out_shape=(
            jax.ShapeDtypeStruct((BF, D), BF16),
            jax.ShapeDtypeStruct((8, 3 * D), F32),
            jax.ShapeDtypeStruct((8, D), F32),
            jax.ShapeDtypeStruct((16, D), F32),
        ),
        in_specs=[VM] * 6,
        out_specs=(VM,) * 4,
        scratch_shapes=[
            vm((2 * BF, D)), vm((2 * BF, D)), vm((2 * BF, CW)), vm((D, 2 * BF)), vm((D, 2 * BF)),
            vm((2, 4, 2, 4, 16, CW)), vm((16, CW), F32), vm((8, CW), F32),
            vm((2, 16, D), F32), vm((3, 4, 16, D), F32), *buffers,
            dma((8,)), dma((8,)), dma((54,)), dma((54,)), dma((9,)), dma((9,)),
        ],
        compiler_params=pltpu.CompilerParams(
            collective_id=1, has_side_effects=True, vmem_limit_bytes=56 * 1024 * 1024
        ),
    )(layer_in, dqkv, att, dsub, dker, wqkv)


def shards(layer_in, queries, keys, values, lengths, w_qkv, w_out, conv_kernel, grad_out):
    att, dsub, dqkv, dker = attention(
        lengths, queries[0], keys[0], values[0], grad_out[0], conv_kernel, w_out
    )
    d_input, d_wqkv, d_wout, d_kernel = weights(layer_in[0], dqkv, att, dsub, dker, w_qkv)
    return d_input[None], d_wqkv, d_wout, d_kernel[:KW]


def solution(mesh):
    frames = P("rec", "ctx", None)
    in_specs = (frames, frames, frames, frames, P("rec"), P(), P(), P(), frames)
    out_specs = (frames, P(("ctx", "rec"), None), P(("ctx", "rec"), None), P())
    return jax.shard_map(
        shards, mesh=mesh, in_specs=in_specs, out_specs=out_specs, check_vma=False
    )
```

```python
import math

import jax
import jax.numpy as jnp
from jax import lax
from jax.experimental import pallas as pl
from jax.experimental.pallas import tpu as pltpu
from jax.sharding import PartitionSpec as P

HD = 128
KW = 9
NC = 8
BF = 256
T = NC * BF
D = 1024
F32 = jnp.float32
BF16 = jnp.bfloat16
MESH = pl.DeviceIdType.MESH
KB = 512
NEG = -1e30
NT = (((1,), (1,)), ((), ()))
ANY = pl.BlockSpec(memory_space=pl.ANY)
VM = pl.BlockSpec(memory_space=pltpu.VMEM)

TQ, TK, TV, TD, BA, BQ, BK, BV = range(8)


def mult(value, of):
    return pl.multiple_of(value, of)


def dot(a, b):
    return jnp.dot(a, b, preferred_element_type=F32)


def dot_nt(a, b):
    return lax.dot_general(a, b, NT, preferred_element_type=F32)


HALF = 512
CW = 4 * HALF
OUT, VAL, QUE, KEY = range(4)
PARTS = (
    (0, 512, ("x", "y", "z")),
    (512, 512, ("x", "z", "y")),
    (1024, 256, ("y", "z", "x")),
    (1280, 256, ("z", "y", "x")),
    (1536, 256, ("y", "x", "z")),
    (1792, 256, ("z", "x", "y")),
)
NP = len(PARTS)


def backward_kernel(
    len_ref, li_ref, q_ref, k_ref, v_ref, g_ref, conv_ref, wout_ref, wqkv_ref,
    din_out, dwq_out, dwo_out, dk_out,
    q_aug, k_aug, v_aug, do_in, do_aug, k_t, v_t, s_ref, e_ref, ds_ref,
    att_s, linv_s, dq_s, dk_s, dv_s, dat_s, dqkv, din_vm,
    g_vm, gp, dsub, halo_lo, halo_hi, wout_vm, wqkv_vm,
    li2, att2, r2, li_t, att_t, grads, fin, fin_x, taps_c, taps_a, *rest,
):
    bufs = rest[: NP * 6]
    (send_sem, recv_sem, halo_send, halo_recv, local_sem, core_send, core_recv,
     ring_send, ring_recv, step_send, step_recv, taps_send, taps_recv) = rest[NP * 6 :]
    me = lax.axis_index("ctx")
    rec = lax.axis_index("rec")
    z, y = lax.div(me, 4), lax.rem(me, 4)
    inv_root = 1.0 / math.sqrt(HD)
    c_exp = math.log2(math.e) / math.sqrt(HD)

    def peer(d):
        return lax.rem(z + lax.div(d, 4), 2) * 4 + lax.rem(y + lax.rem(d, 4), 4)

    def origin(d):
        return lax.rem(z + 2 - lax.div(d, 4), 2) * 4 + lax.rem(y + 4 - lax.rem(d, 4), 4)

    def head_cols(h):
        return pl.ds(mult(h * HD, HD), HD)

    def slot(d):
        return pl.ds(mult(d * BF, BF), BF)

    fwd_src = {TQ: q_ref, TK: k_ref, TV: v_ref}
    fwd_dst = {TQ: q_aug, TK: k_aug, TV: v_aug, TD: do_in}
    back_src = {BA: att_s, BQ: dq_s, BK: dk_s, BV: dv_s}
    back_base = {BQ: 0, BK: D, BV: 2 * D}

    def ends(t, d):
        if t <= TD:
            p = peer(d)
            src = dat_s.at[d] if t == TD else fwd_src[t].at[:, head_cols(p)]
            dst = fwd_dst[t].at[slot(d), pl.ds(0, HD)]
        else:
            p = origin(d)
            src = back_src[t].at[d]
            if t == BA:
                dst = att2.at[pl.ds(0, BF), head_cols(me)]
            else:
                dst = dqkv.at[:, pl.ds(mult(back_base[t] + me * HD, HD), HD)]
        return p, src, dst

    def remote(t, d):
        p, src, dst = ends(t, d)
        return pltpu.make_async_remote_copy(
            src_ref=src, dst_ref=dst, send_sem=send_sem.at[t, d], recv_sem=recv_sem.at[t, d],
            device_id=(p, rec), device_id_type=MESH,
        )

    def local(t):
        _, src, dst = ends(t, 0)
        return pltpu.make_async_copy(src, dst, recv_sem.at[t, 0])

    def each_peer(body):
        def step(d, carry):
            body(d)
            return carry

        lax.fori_loop(1, NC, step, 0)

    def each_slot(body):
        def step(d, carry):
            body(d)
            return carry

        lax.fori_loop(0, NC, step, 0)

    get_g = pltpu.make_async_copy(g_ref, g_vm, local_sem.at[0])
    get_w = pltpu.make_async_copy(wout_ref, wout_vm, local_sem.at[1])
    get_g.start()
    get_w.start()
    for t in (TK, TV, TQ):
        local(t).start()
    mine, theirs = pl.ds(0, BF), pl.ds(BF, BF)
    get_li = pltpu.make_async_copy(li_ref, li2.at[mine, :], local_sem.at[2])
    get_li.start()
    get_wq = pltpu.make_async_copy(wqkv_ref, wqkv_vm, local_sem.at[3])

    core = lax.rem(rec, 2)
    other = 1 - core
    at = {"x": lax.rem(lax.div(rec, 2), 4), "y": y, "z": lax.div(rec, 8) * 2 + z}

    def device(moved, to, on_core=core):
        p = {**at, **({moved: to} if moved else {})}
        return (
            lax.rem(p["z"], 2) * 4 + p["y"],
            lax.div(p["z"], 2) * 8 + p["x"] * 2 + on_core,
        )

    def off(axis, by):
        return lax.rem(at[axis] + by, 4)

    partner = device(None, None, other)
    far = lax.rem(lax.div(rec, 8) + 1, 2)
    greet = [partner] + [device("x", off("x", by)) for by in (1, 2, 3)]
    greet += [device("z", far * 2 + zl) for zl in (0, 1)]

    barrier = pltpu.get_barrier_semaphore()
    each_peer(
        lambda d: pl.semaphore_signal(barrier, inc=1, device_id=(peer(d), rec), device_id_type=MESH)
    )
    for who in greet:
        pl.semaphore_signal(barrier, inc=1, device_id=who, device_id_type=MESH)
    pl.semaphore_wait(barrier, NC - 1 + len(greet))

    right, left = lax.rem(me + 1, NC), lax.rem(me + NC - 1, NC)
    to_right = pltpu.make_async_remote_copy(
        src_ref=g_ref.at[pl.ds(BF - 16, 16), :], dst_ref=halo_lo, send_sem=halo_send.at[0],
        recv_sem=halo_recv.at[0], device_id=(right, rec), device_id_type=MESH,
    )
    to_left = pltpu.make_async_remote_copy(
        src_ref=g_ref.at[pl.ds(0, 16), :], dst_ref=halo_hi, send_sem=halo_send.at[1],
        recv_sem=halo_recv.at[1], device_id=(left, rec), device_id_type=MESH,
    )
    to_right.start()
    to_left.start()
    for t in (TK, TV, TQ):
        each_peer(lambda d: remote(t, d).start())

    def to_partner(n, src, dst):
        return pltpu.make_async_remote_copy(
            src_ref=src, dst_ref=dst, send_sem=core_send.at[n], recv_sem=core_recv.at[n],
            device_id=partner, device_id_type=MESH,
        )

    def half(ref, base, c):
        return ref.at[:, pl.ds(mult(base + c * HALF, HALF), HALF)]

    group = {OUT: (dsub, 0), VAL: (dqkv, 2 * D), QUE: (dqkv, 0), KEY: (dqkv, D)}

    def swap_half(n):
        ref, base = group[n]
        return to_partner(n, half(ref, base, other), r2.at[theirs, pl.ds(n * HALF, HALF)])

    def own_half(n):
        ref, base = group[n]
        r2[mine, pl.ds(n * HALF, HALF)] = half(ref, base, core)[...]

    swap_li = to_partner(4, li_ref, li2.at[theirs, :])
    swap_att = to_partner(5, att2.at[mine, :], att2.at[theirs, :])
    swap_taps = to_partner(6, taps_c.at[core], taps_c.at[core])
    swap_li.start()

    length = len_ref[0]
    lane = lax.broadcasted_iota(jnp.int32, (BF, HD), 1)
    row = lax.broadcasted_iota(jnp.int32, (BF, HD), 0)

    def extra(d):
        masked = (lane == 0) & (row + origin(d) * BF >= length)
        k_aug[slot(d), pl.ds(HD, HD)] = jnp.where(masked, NEG, 0.0).astype(BF16)
        q_aug[slot(d), pl.ds(HD, HD)] = jnp.where(lane == 0, 1.0, 0.0).astype(BF16)
        v_aug[slot(d), pl.ds(HD, HD)] = jnp.where(lane < 2, 1.0, 0.0).astype(BF16)

    each_slot(extra)
    first = lax.broadcasted_iota(jnp.int32, (16, T), 0) == 0
    v_t[pl.ds(HD, 16), :] = jnp.where(first, 1.0, 0.0).astype(BF16)

    get_g.wait()
    gp[pl.ds(8, BF), :] = g_vm[...].astype(F32)
    to_right.wait_recv()
    to_left.wait_recv()
    low = halo_lo[...].astype(F32)[8:16, :]
    gp[pl.ds(0, 8), :] = jnp.where(me > 0, low, 0.0)
    high = halo_hi[...].astype(F32)[0:8, :]
    gp[pl.ds(8 + BF, 8), :] = jnp.where(me < NC - 1, high, 0.0)

    def conv_grad(n):
        cols = pl.ds(mult(n * HD, HD), HD)
        total = gp[pl.ds(8, BF), cols]
        for t in range(KW):
            total = total + conv_ref[pl.ds(t, 1), cols] * gp[pl.ds(12 - t, BF), cols]
        dsub[:, cols] = total.astype(BF16)

    each_slot(conv_grad)
    swap_half(OUT).start()
    own_half(OUT)
    get_wq.start()

    get_w.wait()

    def datt(d):
        rows = pl.ds(mult(peer(d) * HD, HD), HD)
        dat_s[d] = dot_nt(dsub[...], wout_vm[rows, :]).astype(BF16)

        @pl.when(d > 0)
        def _():
            remote(TD, d).start()

    each_slot(datt)
    local(TD).start()

    def turn_in(src, dst):
        def step(n, carry):
            cols = pl.ds(mult(n * BF, BF), BF)
            dst[cols, :] = src[:, cols].T
            return carry

        lax.fori_loop(0, D // BF, step, 0)

    get_li.wait()
    swap_li.wait_recv()
    turn_in(li2, li_t)

    for t in (TK, TV):
        local(t).wait()
        each_peer(lambda d: remote(t, d).wait_recv())

    def turn(d):
        k_t[:, slot(d)] = k_aug[slot(d), pl.ds(0, HD)].T
        v_t[pl.ds(0, HD), slot(d)] = v_aug[slot(d), pl.ds(0, HD)].T

    each_slot(turn)
    local(TQ).wait()

    def forward(d):
        @pl.when(d > 0)
        def _():
            remote(TQ, d).wait_recv()

        qd = q_aug[slot(d), :]
        top = None
        for b in range(T // KB):
            rows = pl.ds(b * KB, KB)
            s = dot_nt(k_aug[rows, :], qd)
            s_ref[rows, :] = s
            m = jnp.max(s, axis=0, keepdims=True)
            top = m if top is None else jnp.maximum(top, m)
        acc = jnp.zeros((HD + 16, BF), F32)
        for b in range(T // KB):
            rows = pl.ds(b * KB, KB)
            e = jnp.exp2((s_ref[rows, :] - top) * c_exp).astype(BF16)
            e_ref[rows, slot(d)] = e
            acc = acc + dot(v_t[:, rows], e)
        inv = 1.0 / acc[HD : HD + 1, :]
        att_s[d] = (acc[:HD, :] * inv).T.astype(BF16)
        linv_s[d] = jnp.broadcast_to(inv, (HD, BF)).T

        @pl.when(d > 0)
        def _():
            remote(BA, d).start()

    each_slot(forward)
    local(BA).start()

    local(TD).wait()

    def backward_in(d):
        @pl.when(d > 0)
        def _():
            remote(TD, d).wait_recv()

        do = (do_in[slot(d), :].astype(F32) * linv_s[d]).astype(BF16)
        delta = -jnp.sum(do.astype(F32) * att_s[d].astype(F32), axis=1, keepdims=True)
        hi = delta.astype(BF16).astype(F32)
        do_aug[slot(d), pl.ds(0, HD)] = do
        do_aug[slot(d), pl.ds(HD, HD)] = jnp.where(
            lane == 0, hi, jnp.where(lane == 1, delta - hi, 0.0)
        ).astype(BF16)

    each_slot(backward_in)

    def d_value(j):
        dv_s[j] = dot(e_ref[slot(j), :], do_aug[:, pl.ds(0, HD)]).astype(BF16)

        @pl.when(j > 0)
        def _():
            remote(BV, j).start()

    each_slot(d_value)
    local(BV).start()

    def d_query(d):
        dod = do_aug[slot(d), :]
        acc = jnp.zeros((HD, BF), F32)
        for b in range(T // KB):
            rows = pl.ds(b * KB, KB)
            dp = dot_nt(v_aug[rows, :], dod)
            ds = (e_ref[rows, slot(d)].astype(F32) * dp).astype(BF16)
            ds_ref[rows, slot(d)] = ds
            acc = acc + dot(k_t[:, rows], ds)
        dq_s[d] = (acc * inv_root).T.astype(BF16)

        @pl.when(d > 0)
        def _():
            remote(BQ, d).start()

    each_slot(d_query)
    local(BQ).start()

    def product(lhs, start, width):
        def step(b, carry):
            rows = pl.ds(mult(b * HD, HD), HD)
            g = dot(lhs[rows, :], r2[:, pl.ds(start, width)]).astype(BF16)
            grads[lax.div(b, 4), lax.rem(b, 4), :, :, :, pl.ds(start, width)] = g.reshape(
                2, 4, 16, width
            )
            return carry

        lax.fori_loop(0, D // HD, step, 0)

    def region(fixed, start, width):
        zl = zh = slice(None)
        if "z" in fixed:
            zl, zh = lax.rem(fixed["z"], 2), lax.div(fixed["z"], 2)
        return grads.at[
            zl, fixed.get("y", slice(None)), zh, fixed.get("x", slice(None)), :, pl.ds(start, width)
        ]

    class Stage:
        def __init__(self, part, stage):
            self.start, self.width, order = PARTS[part]
            self.axis = order[stage]
            self.fixed = {a: at[a] for a in order[:stage]}
            self.stage = stage

        def piece(self, by, start=0, width=None):
            width = self.width if width is None else width
            fixed = {**self.fixed, self.axis: off(self.axis, by)}
            return region(fixed, self.start + start, width)

        def copy(self, sems, n, src, dst, by):
            return pltpu.make_async_remote_copy(
                src_ref=src, dst_ref=dst, send_sem=sems[0].at[n], recv_sem=sems[1].at[n],
                device_id=device(self.axis, off(self.axis, by)), device_id_type=MESH,
            )

        def keep(self, total):
            if self.stage < 2:
                self.piece(0)[...] = total.astype(BF16)
            else:
                fin[:, pl.ds(self.start, self.width)] = total

        def sent(self):
            for c in self.copies:
                c.wait_send()

    class Ring(Stage):
        def __init__(self, part):
            super().__init__(part, 0)
            self.ra, self.rb, self.low, self.high = bufs[part * 6 : part * 6 + 4]
            h = self.width // 2
            lead = (slice(None),) * (len(self.low.shape) - 1)
            a, b = (*lead, pl.ds(0, h)), (*lead, pl.ds(h, h))
            ends = (
                (self.piece(2, 0, h), self.ra, 1),
                (self.piece(2, h, h), self.rb, 3),
                (self.piece(1, h, h), self.low.at[b], 1),
                (self.piece(3, 0, h), self.high.at[a], 3),
                (self.piece(1, 0, h), self.low.at[a], 1),
                (self.piece(3, h, h), self.high.at[b], 3),
            )
            sems = (ring_send, ring_recv)
            self.copies = [self.copy(sems, part * 6 + n, *e) for n, e in enumerate(ends)]

        def begin(self):
            for c in self.copies[:4]:
                c.start()

        def relay(self):
            h = self.width // 2
            for n, by, buf, start in ((0, 1, self.ra, 0), (1, 3, self.rb, h)):
                self.copies[n].wait_recv()
                here = self.piece(by, start, h)
                here[...] = (here[...].astype(F32) + buf[...].astype(F32)).astype(BF16)
                self.copies[4 + n].start()

        def end(self):
            for n in (2, 3, 4, 5):
                self.copies[n].wait_recv()
            here = self.piece(0)[...].astype(F32)
            self.keep(here + (self.low[...].astype(F32) + self.high[...].astype(F32)))

    class Direct(Stage):
        def __init__(self, part, stage):
            super().__init__(part, stage)
            self.buf = bufs[part * 6 + 3 + stage]
            base = (part * 2 + stage - 1) * 3
            sems = (step_send, step_recv)
            self.copies = [
                self.copy(sems, base + by - 1, self.piece(by), self.buf.at[by - 1], by)
                for by in (1, 2, 3)
            ]

        def begin(self):
            for c in self.copies:
                c.start()

        def end(self):
            for c in self.copies:
                c.wait_recv()
            here = self.piece(0)[...].astype(F32)
            b = [self.buf[n].astype(F32) for n in range(3)]
            self.keep((here + b[0]) + (b[1] + b[2]))

    rings = [(Ring(p), Direct(p, 1), Direct(p, 2)) for p in range(NP)]

    def arrived(t):
        local(t).wait()
        each_peer(lambda d: remote(t, d).wait_recv())

    def on(p, stage):
        rings[p][stage].end()
        rings[p][stage + 1].begin()

    taps_copies = []

    def taps_on(n, axis, value):
        taps_a[n, at[axis]] = value
        for by in (1, 2, 3):
            c = pltpu.make_async_remote_copy(
                src_ref=taps_a.at[n, at[axis]], dst_ref=taps_a.at[n, at[axis]],
                send_sem=taps_send.at[n * 3 + by - 1], recv_sem=taps_recv.at[n * 3 + by - 1],
                device_id=device(axis, off(axis, by)), device_id_type=MESH,
            )
            c.start()
            taps_copies.append(c)

    def taps_sum(n):
        for c in taps_copies[n * 3 :]:
            c.wait_recv()
        return (taps_a[n, 0] + taps_a[n, 1]) + (taps_a[n, 2] + taps_a[n, 3])

    arrived(BA)
    swap_att.start()
    swap_half(OUT).wait_recv()
    swap_att.wait_recv()
    turn_in(att2, att_t)
    product(att_t, OUT * HALF, HALF)
    rings[0][0].begin()

    def d_key(j):
        dk = dot(ds_ref[slot(j), :], q_aug[:, pl.ds(0, HD)])
        dk_s[j] = (dk * inv_root).astype(BF16)

        @pl.when(j > 0)
        def _():
            remote(BK, j).start()

    each_slot(d_key)
    local(BK).start()

    def taps(n):
        cols = pl.ds(mult(n * BF, BF), BF)
        sub = dot(att2[mine, :], wout_vm[:, cols]).astype(BF16).astype(F32)
        for t in range(KW):
            taps_c[core, pl.ds(t, 1), cols] = jnp.sum(
                sub * gp[pl.ds(12 - t, BF), cols], axis=0, keepdims=True
            )

    taps_c[core] = jnp.zeros((16, D), F32)
    lax.fori_loop(0, D // BF, lambda n, c: (taps(n), c)[1], 0)
    swap_taps.start()
    rings[0][0].relay()

    def weight(t, n):
        arrived(t)
        swap_half(n).start()
        own_half(n)
        swap_half(n).wait_recv()
        product(li_t, n * HALF, HALF)

    weight(BV, VAL)
    rings[1][0].begin()
    swap_taps.wait_recv()
    taps_on(0, "x", taps_c[0] + taps_c[1])
    weight(BQ, QUE)
    rings[2][0].begin()
    rings[3][0].begin()
    rings[1][0].relay()
    weight(BK, KEY)
    rings[4][0].begin()
    rings[5][0].begin()
    rings[2][0].relay()
    rings[3][0].relay()

    get_wq.wait()

    def d_input(n, carry):
        cols = pl.ds(mult(n * BF, BF), BF)
        din_vm[:, cols] = dot_nt(dqkv[...], wqkv_vm[cols, :]).astype(BF16)
        return carry

    lax.fori_loop(0, 2, d_input, 0)
    rings[4][0].relay()
    rings[5][0].relay()
    on(0, 0)
    taps_on(1, "y", taps_sum(0))
    lax.fori_loop(2, 4, d_input, 0)
    put_din = pltpu.make_async_copy(din_vm, din_out, local_sem.at[4])
    put_din.start()
    for p in (2, 3, 1, 4, 5):
        on(p, 0)
    on(0, 1)
    taps_on(2, "z", taps_sum(1))
    for p in (2, 3, 1, 4, 5):
        on(p, 1)
    dk_out[...] = taps_sum(2)[:KW]
    for p in range(NP):
        rings[p][2].end()

    last = to_partner(7, fin.at[pl.ds(mult(other * 8, 8), 8), :], fin_x)
    last.start()

    def place(block, who):
        for n, base in ((VAL, 2 * D), (QUE, 0), (KEY, D)):
            dwq_out[:, pl.ds(mult(base + who * HALF, HALF), HALF)] = block[
                :, n * HALF : (n + 1) * HALF
            ]
        dwo_out[:, pl.ds(mult(who * HALF, HALF), HALF)] = block[:, :HALF]

    place(fin[pl.ds(mult(core * 8, 8), 8), :], core)
    last.wait_recv()
    place(fin_x[...], other)

    put_din.wait()
    to_right.wait_send()
    to_left.wait_send()
    for t in range(8):
        each_peer(lambda d: remote(t, d).wait_send())
    for swap in (last, swap_li, swap_att, swap_taps, *(swap_half(n) for n in range(4))):
        swap.wait_send()
    for c in taps_copies:
        c.wait_send()
    for r in rings:
        for stage in r:
            stage.sent()


def collect_kernel(*refs):
    ins, outs, sems = refs[:4], refs[4:8], refs[8]
    copies = [pltpu.make_async_copy(a, b, sems.at[n]) for n, (a, b) in enumerate(zip(ins, outs))]
    for c in copies:
        c.start()
    for c in copies:
        c.wait()


def backward(lengths, li, q, k, v, g, conv, wout, wqkv):
    def vm(shape, dtype=BF16):
        return pltpu.VMEM(shape, dtype)

    buffers = []
    for _, width, order in PARTS:
        leads = []
        for stage in range(3):
            sizes = (("zl", 2), ("y", 4), ("zh", 2), ("x", 4))
            leads.append([n for axis, n in sizes if axis[0] not in order[: stage + 1]])
        for w in (width // 2, width // 2, width, width):
            buffers.append(vm((*leads[0], 16, w)))
        for stage in (1, 2):
            buffers.append(vm((3, *leads[stage], 16, width)))
    dma = pltpu.SemaphoreType.DMA
    outs = (
        jax.ShapeDtypeStruct((BF, D), BF16),
        jax.ShapeDtypeStruct((8, 3 * D), F32),
        jax.ShapeDtypeStruct((8, D), F32),
        jax.ShapeDtypeStruct((KW, D), F32),
    )
    results = pl.pallas_call(
        backward_kernel,
        out_shape=outs,
        in_specs=[pl.BlockSpec(memory_space=pltpu.SMEM), ANY, ANY, ANY, ANY, ANY, VM, ANY, ANY],
        out_specs=(ANY, VM, VM, VM),
        scratch_shapes=[
            vm((T, 2 * HD)), vm((T, 2 * HD)), vm((T, 2 * HD)), vm((T, HD)), vm((T, 2 * HD)),
            vm((HD, T)), vm((HD + 16, T)), vm((T, BF), F32), vm((T, T)), vm((T, T)),
            vm((NC, BF, HD)), vm((NC, BF, HD), F32), vm((NC, BF, HD)), vm((NC, BF, HD)),
            vm((NC, BF, HD)), vm((NC, BF, HD)), vm((BF, 3 * D)), vm((BF, D)),
            vm((BF, D)), vm((BF + 16, D), F32), vm((BF, D)), vm((16, D)), vm((16, D)),
            vm((D, D)), vm((D, 3 * D)),
            vm((2 * BF, D)), vm((2 * BF, D)), vm((2 * BF, CW)), vm((D, 2 * BF)), vm((D, 2 * BF)),
            vm((2, 4, 2, 4, 16, CW)), vm((16, CW), F32), vm((8, CW), F32),
            vm((2, 16, D), F32), vm((3, 4, 16, D), F32), *buffers,
            dma((8, NC)), dma((8, NC)), dma((2,)), dma((2,)), dma((5,)), dma((8,)), dma((8,)),
            dma((NP * 6,)), dma((NP * 6,)), dma((NP * 6,)), dma((NP * 6,)), dma((9,)), dma((9,)),
        ],
        compiler_params=pltpu.CompilerParams(
            collective_id=0, has_side_effects=True, vmem_limit_bytes=60 * 1024 * 1024
        ),
    )(lengths, li, q, k, v, g, conv, wout, wqkv)
    return pl.pallas_call(
        collect_kernel,
        out_shape=outs,
        in_specs=[ANY] * 4,
        out_specs=(ANY,) * 4,
        scratch_shapes=[dma((4,))],
    )(*results)


def shards(layer_in, queries, keys, values, lengths, w_qkv, w_out, conv_kernel, grad_out):
    d_input, d_wqkv, d_wout, d_kernel = backward(
        lengths, layer_in[0], queries[0], keys[0], values[0], grad_out[0], conv_kernel, w_out, w_qkv
    )
    return d_input[None], d_wqkv, d_wout, d_kernel


def solution(mesh):
    frames = P("rec", "ctx", None)
    in_specs = (frames, frames, frames, frames, P("rec"), P(), P(), P(), frames)
    out_specs = (frames, P(("ctx", "rec"), None), P(("ctx", "rec"), None), P())
    return jax.shard_map(
        shards, mesh=mesh, in_specs=in_specs, out_specs=out_specs, check_vma=False
    )
```

```python
import math

import jax
import jax.numpy as jnp
from jax import lax
from jax.experimental import pallas as pl
from jax.experimental.pallas import tpu as pltpu
from jax.sharding import PartitionSpec as P

HD = 128
KW = 9
NC = 8
BF = 256
T = NC * BF
D = 1024
F32 = jnp.float32
BF16 = jnp.bfloat16
MESH = pl.DeviceIdType.MESH
KB = 512
NEG = -1e30
NT = (((1,), (1,)), ((), ()))
ANY = pl.BlockSpec(memory_space=pl.ANY)
VM = pl.BlockSpec(memory_space=pltpu.VMEM)

TQ, TK, TV, TD, BA, BQ, BK, BV = range(8)


def mult(value, of):
    return pl.multiple_of(value, of)


def dot(a, b):
    return jnp.dot(a, b, preferred_element_type=F32)


def dot_nt(a, b):
    return lax.dot_general(a, b, NT, preferred_element_type=F32)


HALF = 512
CW = 4 * HALF
OUT, VAL, QUE, KEY = range(4)
PARTS = (
    (0, 512, ("x", "y", "z")),
    (512, 512, ("x", "z", "y")),
    (1024, 256, ("y", "z", "x")),
    (1280, 256, ("z", "y", "x")),
    (1536, 256, ("x", "y", "z")),
    (1792, 128, ("y", "z", "x")),
    (1920, 128, ("z", "x", "y")),
)
NP = len(PARTS)
NR = 4


def backward_kernel(
    len_ref, li_ref, q_ref, k_ref, v_ref, g_ref, conv_ref, wout_ref, wqkv_ref,
    din_out, dwq_out, dwo_out, dk_out,
    q_aug, k_aug, v_aug, do_in, do_aug, k_t, v_t, s_ref, e_ref, ds_ref,
    att_s, linv_s, dq_s, dk_s, dv_s, dat_s, dqkv, din_vm,
    g_vm, gp, dsub, halo_lo, halo_hi, wout_vm, wqkv_vm,
    li2, att2, r2, li_t, att_t, grads, taps_c, taps_a, *rest,
):
    bufs = rest[: NP * 7]
    (send_sem, recv_sem, halo_send, halo_recv, local_sem, core_send, core_recv,
     ring_send, ring_recv, step_send, step_recv, last_send, last_recv,
     taps_send, taps_recv) = rest[NP * 7 :]
    me = lax.axis_index("ctx")
    rec = lax.axis_index("rec")
    z, y = lax.div(me, 4), lax.rem(me, 4)
    inv_root = 1.0 / math.sqrt(HD)
    c_exp = math.log2(math.e) / math.sqrt(HD)

    def peer(d):
        return lax.rem(z + lax.div(d, 4), 2) * 4 + lax.rem(y + lax.rem(d, 4), 4)

    def origin(d):
        return lax.rem(z + 2 - lax.div(d, 4), 2) * 4 + lax.rem(y + 4 - lax.rem(d, 4), 4)

    def head_cols(h):
        return pl.ds(mult(h * HD, HD), HD)

    def slot(d):
        return pl.ds(mult(d * BF, BF), BF)

    fwd_src = {TQ: q_ref, TK: k_ref, TV: v_ref}
    fwd_dst = {TQ: q_aug, TK: k_aug, TV: v_aug, TD: do_in}
    back_src = {BA: att_s, BQ: dq_s, BK: dk_s, BV: dv_s}
    back_base = {BQ: 0, BK: D, BV: 2 * D}

    def ends(t, d):
        if t <= TD:
            p = peer(d)
            src = dat_s.at[d] if t == TD else fwd_src[t].at[:, head_cols(p)]
            dst = fwd_dst[t].at[slot(d), pl.ds(0, HD)]
        else:
            p = origin(d)
            src = back_src[t].at[d]
            if t == BA:
                dst = att2.at[pl.ds(0, BF), head_cols(me)]
            else:
                dst = dqkv.at[:, pl.ds(mult(back_base[t] + me * HD, HD), HD)]
        return p, src, dst

    def remote(t, d):
        p, src, dst = ends(t, d)
        return pltpu.make_async_remote_copy(
            src_ref=src, dst_ref=dst, send_sem=send_sem.at[t, d], recv_sem=recv_sem.at[t, d],
            device_id=(p, rec), device_id_type=MESH,
        )

    def local(t):
        _, src, dst = ends(t, 0)
        return pltpu.make_async_copy(src, dst, recv_sem.at[t, 0])

    def each_peer(body):
        def step(d, carry):
            body(d)
            return carry

        lax.fori_loop(1, NC, step, 0)

    def each_slot(body):
        def step(d, carry):
            body(d)
            return carry

        lax.fori_loop(0, NC, step, 0)

    get_g = pltpu.make_async_copy(g_ref, g_vm, local_sem.at[0])
    get_w = pltpu.make_async_copy(wout_ref, wout_vm, local_sem.at[1])
    get_g.start()
    get_w.start()
    for t in (TK, TQ, TV):
        local(t).start()
    mine, theirs = pl.ds(0, BF), pl.ds(BF, BF)
    get_li = pltpu.make_async_copy(li_ref, li2.at[mine, :], local_sem.at[2])
    get_li.start()
    get_wq = pltpu.make_async_copy(wqkv_ref, wqkv_vm, local_sem.at[3])

    core = lax.rem(rec, 2)
    other = 1 - core
    at = {"x": lax.rem(lax.div(rec, 2), 4), "y": y, "z": lax.div(rec, 8) * 2 + z}

    def device(moved, to, on_core=core):
        p = {**at, **({moved: to} if moved else {})}
        return (
            lax.rem(p["z"], 2) * 4 + p["y"],
            lax.div(p["z"], 2) * 8 + p["x"] * 2 + on_core,
        )

    def off(axis, by):
        return lax.rem(at[axis] + by, 4)

    partner = device(None, None, other)
    far = lax.rem(lax.div(rec, 8) + 1, 2)
    greet = [partner] + [device("x", off("x", by)) for by in (1, 2, 3)]
    greet += [device("z", far * 2 + zl) for zl in (0, 1)]
    greet += [device(a, off(a, by), other) for a in "xyz" for by in (1, 2, 3)]

    barrier = pltpu.get_barrier_semaphore()
    each_peer(
        lambda d: pl.semaphore_signal(barrier, inc=1, device_id=(peer(d), rec), device_id_type=MESH)
    )
    for who in greet:
        pl.semaphore_signal(barrier, inc=1, device_id=who, device_id_type=MESH)
    pl.semaphore_wait(barrier, NC - 1 + len(greet))

    right, left = lax.rem(me + 1, NC), lax.rem(me + NC - 1, NC)
    to_right = pltpu.make_async_remote_copy(
        src_ref=g_ref.at[pl.ds(BF - 16, 16), :], dst_ref=halo_lo, send_sem=halo_send.at[0],
        recv_sem=halo_recv.at[0], device_id=(right, rec), device_id_type=MESH,
    )
    to_left = pltpu.make_async_remote_copy(
        src_ref=g_ref.at[pl.ds(0, 16), :], dst_ref=halo_hi, send_sem=halo_send.at[1],
        recv_sem=halo_recv.at[1], device_id=(left, rec), device_id_type=MESH,
    )
    to_right.start()
    to_left.start()
    for t in (TK, TQ, TV):
        each_peer(lambda d: remote(t, d).start())

    def to_partner(n, src, dst):
        return pltpu.make_async_remote_copy(
            src_ref=src, dst_ref=dst, send_sem=core_send.at[n], recv_sem=core_recv.at[n],
            device_id=partner, device_id_type=MESH,
        )

    def half(ref, base, c):
        return ref.at[:, pl.ds(mult(base + c * HALF, HALF), HALF)]

    group = {OUT: (dsub, 0), VAL: (dqkv, 2 * D), QUE: (dqkv, 0), KEY: (dqkv, D)}

    def swap_half(n):
        ref, base = group[n]
        return to_partner(n, half(ref, base, other), r2.at[theirs, pl.ds(n * HALF, HALF)])

    def own_half(n):
        ref, base = group[n]
        r2[mine, pl.ds(n * HALF, HALF)] = half(ref, base, core)[...]

    swap_li = to_partner(4, li_ref, li2.at[theirs, :])
    swap_att = to_partner(5, att2.at[mine, :], att2.at[theirs, :])
    swap_taps = to_partner(6, taps_c.at[core], taps_c.at[core])
    swap_li.start()

    length = len_ref[0]
    lane = lax.broadcasted_iota(jnp.int32, (BF, HD), 1)
    row = lax.broadcasted_iota(jnp.int32, (BF, HD), 0)

    def extra(d):
        masked = (lane == 0) & (row + origin(d) * BF >= length)
        k_aug[slot(d), pl.ds(HD, HD)] = jnp.where(masked, NEG, 0.0).astype(BF16)
        q_aug[slot(d), pl.ds(HD, HD)] = jnp.where(lane == 0, 1.0, 0.0).astype(BF16)
        v_aug[slot(d), pl.ds(HD, HD)] = jnp.where(lane < 2, 1.0, 0.0).astype(BF16)

    each_slot(extra)
    first = lax.broadcasted_iota(jnp.int32, (16, T), 0) == 0
    v_t[pl.ds(HD, 16), :] = jnp.where(first, 1.0, 0.0).astype(BF16)

    get_g.wait()
    gp[pl.ds(8, BF), :] = g_vm[...].astype(F32)
    to_right.wait_recv()
    to_left.wait_recv()
    low = halo_lo[...].astype(F32)[8:16, :]
    gp[pl.ds(0, 8), :] = jnp.where(me > 0, low, 0.0)
    high = halo_hi[...].astype(F32)[0:8, :]
    gp[pl.ds(8 + BF, 8), :] = jnp.where(me < NC - 1, high, 0.0)

    def conv_grad(n):
        cols = pl.ds(mult(n * HD, HD), HD)
        total = gp[pl.ds(8, BF), cols]
        for t in range(KW):
            total = total + conv_ref[pl.ds(t, 1), cols] * gp[pl.ds(12 - t, BF), cols]
        dsub[:, cols] = total.astype(BF16)

    each_slot(conv_grad)
    swap_half(OUT).start()
    own_half(OUT)
    get_wq.start()

    get_w.wait()

    def datt(d):
        rows = pl.ds(mult(peer(d) * HD, HD), HD)
        dat_s[d] = dot_nt(dsub[...], wout_vm[rows, :]).astype(BF16)

        @pl.when(d > 0)
        def _():
            remote(TD, d).start()

    each_slot(datt)
    local(TD).start()

    def turn_in(src, dst):
        def step(n, carry):
            cols = pl.ds(mult(n * BF, BF), BF)
            dst[cols, :] = src[:, cols].T
            return carry

        lax.fori_loop(0, D // BF, step, 0)

    get_li.wait()
    swap_li.wait_recv()
    turn_in(li2, li_t)

    def arrived(t):
        local(t).wait()
        each_peer(lambda d: remote(t, d).wait_recv())

    arrived(TK)
    local(TQ).wait()

    def scores(d):
        @pl.when(d > 0)
        def _():
            remote(TQ, d).wait_recv()

        qd = q_aug[slot(d), :]
        top = None
        for b in range(T // KB):
            rows = pl.ds(b * KB, KB)
            s = dot_nt(k_aug[rows, :], qd)
            s_ref[rows, :] = s
            m = jnp.max(s, axis=0, keepdims=True)
            top = m if top is None else jnp.maximum(top, m)
        for b in range(T // KB):
            rows = pl.ds(b * KB, KB)
            e_ref[rows, slot(d)] = jnp.exp2((s_ref[rows, :] - top) * c_exp).astype(BF16)

    each_slot(scores)
    arrived(TV)

    def turn(d):
        k_t[:, slot(d)] = k_aug[slot(d), pl.ds(0, HD)].T
        v_t[pl.ds(0, HD), slot(d)] = v_aug[slot(d), pl.ds(0, HD)].T

    each_slot(turn)

    def attend(d):
        acc = dot(v_t[...], e_ref[:, slot(d)])
        inv = 1.0 / acc[HD : HD + 1, :]
        att_s[d] = (acc[:HD, :] * inv).T.astype(BF16)
        linv_s[d] = jnp.broadcast_to(inv, (HD, BF)).T

        @pl.when(d > 0)
        def _():
            remote(BA, d).start()

    each_slot(attend)
    local(BA).start()

    local(TD).wait()

    def backward_in(d):
        @pl.when(d > 0)
        def _():
            remote(TD, d).wait_recv()

        do = (do_in[slot(d), :].astype(F32) * linv_s[d]).astype(BF16)
        delta = -jnp.sum(do.astype(F32) * att_s[d].astype(F32), axis=1, keepdims=True)
        hi = delta.astype(BF16).astype(F32)
        do_aug[slot(d), pl.ds(0, HD)] = do
        do_aug[slot(d), pl.ds(HD, HD)] = jnp.where(
            lane == 0, hi, jnp.where(lane == 1, delta - hi, 0.0)
        ).astype(BF16)

    each_slot(backward_in)

    def d_value(j):
        two = pl.ds(mult(j * 2 * BF, 2 * BF), 2 * BF)
        dv_s[pl.ds(j * 2, 2)] = dot(e_ref[two, :], do_aug[:, pl.ds(0, HD)]).astype(BF16).reshape(2, BF, HD)

        @pl.when(j > 0)
        def _():
            remote(BV, j * 2).start()

        remote(BV, j * 2 + 1).start()

    lax.fori_loop(0, NC // 2, lambda j, c: (d_value(j), c)[1], 0)
    local(BV).start()

    def d_query(d):
        dod = do_aug[slot(d), :]
        acc = jnp.zeros((HD, BF), F32)
        for b in range(T // KB):
            rows = pl.ds(b * KB, KB)
            dp = dot_nt(v_aug[rows, :], dod)
            ds = (e_ref[rows, slot(d)].astype(F32) * dp).astype(BF16)
            ds_ref[rows, slot(d)] = ds
            acc = acc + dot(k_t[:, rows], ds)
        dq_s[d] = (acc * inv_root).T.astype(BF16)

        @pl.when(d > 0)
        def _():
            remote(BQ, d).start()

    each_slot(d_query)
    local(BQ).start()

    def product(lhs, start, width):
        def step(zl, carry):
            rows = pl.ds(mult(zl * HALF, HALF), HALF)
            g = dot(lhs[rows, :], r2[:, pl.ds(start, width)]).astype(BF16)
            grads[zl, :, :, :, :, pl.ds(start, width)] = g.reshape(4, 2, 4, 16, width)
            return carry

        lax.fori_loop(0, 2, step, 0)

    def region(fixed, start, width):
        zl = zh = slice(None)
        if "z" in fixed:
            zl, zh = lax.rem(fixed["z"], 2), lax.div(fixed["z"], 2)
        return grads.at[
            zl, fixed.get("y", slice(None)), zh, fixed.get("x", slice(None)), :, pl.ds(start, width)
        ]

    class Stage:
        def __init__(self, part, stage):
            self.start, self.width, order = PARTS[part]
            self.part = part
            self.axis = order[stage]
            self.fixed = {a: at[a] for a in order[:stage]}
            self.stage = stage

        def piece(self, by, start=0, width=None):
            width = self.width if width is None else width
            fixed = {**self.fixed, self.axis: off(self.axis, by)}
            return region(fixed, self.start + start, width)

        def copy(self, sems, n, src, dst, by):
            return pltpu.make_async_remote_copy(
                src_ref=src, dst_ref=dst, send_sem=sems[0].at[n], recv_sem=sems[1].at[n],
                device_id=device(self.axis, off(self.axis, by)), device_id_type=MESH,
            )

        def keep(self, total):
            if self.stage == 0:
                self.piece(0)[...] = total.astype(BF16)
            else:
                pair = bufs[self.part * 7 + 5]
                pair[..., 0, :, :] = total[..., :8, :]
                pair[..., 1, :, :] = total[..., 8:, :]

        def sent(self):
            for c in self.copies:
                c.wait_send()

    class Ring(Stage):
        def __init__(self, part):
            super().__init__(part, 0)
            self.ra, self.rb, self.low, self.high = bufs[part * 7 : part * 7 + 4]
            h = self.width // 2
            lead = (slice(None),) * (len(self.low.shape) - 1)
            a, b = (*lead, pl.ds(0, h)), (*lead, pl.ds(h, h))
            ends = (
                (self.piece(2, 0, h), self.ra, 1),
                (self.piece(2, h, h), self.rb, 3),
                (self.piece(1, h, h), self.low.at[b], 1),
                (self.piece(3, 0, h), self.high.at[a], 3),
                (self.piece(1, 0, h), self.low.at[a], 1),
                (self.piece(3, h, h), self.high.at[b], 3),
            )
            sems = (ring_send, ring_recv)
            self.copies = [self.copy(sems, part * 6 + n, *e) for n, e in enumerate(ends)]

        def begin(self):
            for c in self.copies[:4]:
                c.start()

        def relay(self):
            h = self.width // 2
            for n, by, buf, start in ((0, 1, self.ra, 0), (1, 3, self.rb, h)):
                self.copies[n].wait_recv()
                here = self.piece(by, start, h)
                here[...] = (here[...].astype(F32) + buf[...].astype(F32)).astype(BF16)
                self.copies[4 + n].start()

        def end(self):
            for n in (2, 3, 4, 5):
                self.copies[n].wait_recv()
            here = self.piece(0)[...].astype(F32)
            self.keep(here + (self.low[...].astype(F32) + self.high[...].astype(F32)))

    class Direct(Stage):
        def __init__(self, part, stage):
            super().__init__(part, stage)
            self.buf = bufs[part * 7 + 3 + stage] if stage else bufs[part * 7]
            base = (part * 2 + stage) * 3
            sems = (step_send, step_recv)
            self.copies = [
                self.copy(sems, base + by - 1, self.piece(by), self.buf.at[by - 1], by)
                for by in (1, 2, 3)
            ]

        def begin(self):
            for c in self.copies:
                c.start()

        def end(self):
            for c in self.copies:
                c.wait_recv()
            here = self.piece(0)[...].astype(F32)
            b = [self.buf[n].astype(F32) for n in range(3)]
            self.keep((here + b[0]) + (b[1] + b[2]))

    class Last(Stage):
        def __init__(self, part):
            super().__init__(part, 2)
            self.pair, self.buf = bufs[part * 7 + 5 : part * 7 + 7]
            self.copies = []
            for n, (turned, by) in enumerate((t, b) for t in (0, 1) for b in range(4) if t + b):
                to = lax.rem(core + turned, 2)
                who = device(self.axis, off(self.axis, by), to)
                self.copies.append(
                    pltpu.make_async_remote_copy(
                        src_ref=self.rows(by, to), dst_ref=self.buf.at[n],
                        send_sem=last_send.at[part * 7 + n], recv_sem=last_recv.at[part * 7 + n],
                        device_id=who, device_id_type=MESH,
                    )
                )

        def rows(self, by, to):
            chip = off(self.axis, by)
            if self.axis == "z":
                return self.pair.at[lax.rem(chip, 2), lax.div(chip, 2), to]
            return self.pair.at[chip, to]

        def begin(self):
            for c in self.copies:
                c.start()

        def end(self):
            for c in self.copies:
                c.wait_recv()
            b = [self.buf[n] for n in range(7)]
            here = self.rows(0, core)[...]
            n, inside = divmod(self.start, HALF)
            out, base = ((dwo_out, 0), (dwq_out, 2 * D), (dwq_out, 0), (dwq_out, D))[n]
            for who, block in (
                (core, (here + b[0]) + (b[1] + b[2])),
                (other, (b[3] + b[4]) + (b[5] + b[6])),
            ):
                cols = pl.ds(mult(base + who * HALF + inside, HD), self.width)
                out[:, cols] = block

    rings = [(Ring(p) if p < NR else Direct(p, 0), Direct(p, 1), Last(p)) for p in range(NP)]

    def on(p, stage):
        rings[p][stage].end()
        rings[p][stage + 1].begin()

    taps_copies = []

    def taps_on(n, axis, value):
        taps_a[n, at[axis]] = value
        for by in (1, 2, 3):
            c = pltpu.make_async_remote_copy(
                src_ref=taps_a.at[n, at[axis]], dst_ref=taps_a.at[n, at[axis]],
                send_sem=taps_send.at[n * 3 + by - 1], recv_sem=taps_recv.at[n * 3 + by - 1],
                device_id=device(axis, off(axis, by)), device_id_type=MESH,
            )
            c.start()
            taps_copies.append(c)

    def taps_sum(n):
        for c in taps_copies[n * 3 :]:
            c.wait_recv()
        return (taps_a[n, 0] + taps_a[n, 1]) + (taps_a[n, 2] + taps_a[n, 3])

    arrived(BA)
    swap_att.start()

    def d_key(j):
        two = pl.ds(mult(j * 2 * BF, 2 * BF), 2 * BF)
        dk_s[pl.ds(j * 2, 2)] = (dot(ds_ref[two, :], q_aug[:, pl.ds(0, HD)]) * inv_root).astype(BF16).reshape(2, BF, HD)

        @pl.when(j > 0)
        def _():
            remote(BK, j * 2).start()

        remote(BK, j * 2 + 1).start()

    lax.fori_loop(0, NC // 2, lambda j, c: (d_key(j), c)[1], 0)
    local(BK).start()

    swap_half(OUT).wait_recv()
    swap_att.wait_recv()
    turn_in(att2, att_t)
    product(att_t, OUT * HALF, HALF)
    rings[0][0].begin()

    def taps(n):
        cols = pl.ds(mult(n * BF, BF), BF)
        sub = dot(att2[mine, :], wout_vm[:, cols]).astype(BF16).astype(F32)
        for t in range(KW):
            taps_c[core, pl.ds(t, 1), cols] = jnp.sum(
                sub * gp[pl.ds(12 - t, BF), cols], axis=0, keepdims=True
            )

    def back(t, n):
        arrived(t)
        swap_half(n).start()
        own_half(n)

    def weight(n):
        swap_half(n).wait_recv()
        product(li_t, n * HALF, HALF)

    def d_input(n, carry):
        cols = pl.ds(mult(n * BF, BF), BF)
        din_vm[:, cols] = dot_nt(dqkv[...], wqkv_vm[cols, :]).astype(BF16)
        return carry

    taps_c[core] = jnp.zeros((16, D), F32)
    lax.fori_loop(0, D // BF, lambda n, c: (taps(n), c)[1], 0)
    swap_taps.start()
    back(BV, VAL)
    rings[0][0].relay()
    weight(VAL)
    rings[1][0].begin()
    swap_taps.wait_recv()
    taps_on(0, "x", taps_c[0] + taps_c[1])
    back(BQ, QUE)
    get_wq.wait()
    weight(QUE)
    rings[2][0].begin()
    rings[3][0].begin()
    rings[1][0].relay()
    on(0, 0)
    taps_on(1, "y", taps_sum(0))
    back(BK, KEY)
    lax.fori_loop(0, 2, d_input, 0)
    weight(KEY)
    for p in (4, 5, 6):
        rings[p][0].begin()
    rings[2][0].relay()
    rings[3][0].relay()
    lax.fori_loop(2, 4, d_input, 0)
    put_din = pltpu.make_async_copy(din_vm, din_out, local_sem.at[4])
    put_din.start()
    on(1, 0)
    on(0, 1)
    taps_on(2, "z", taps_sum(1))
    for p in (2, 3, 4, 5, 6):
        on(p, 0)
    for p in (1, 2, 3, 4, 5, 6):
        on(p, 1)
    dk_out[...] = taps_sum(2)[:KW]
    for p in range(NP):
        rings[p][2].end()

    put_din.wait()
    to_right.wait_send()
    to_left.wait_send()
    for t in range(8):
        each_peer(lambda d: remote(t, d).wait_send())
    for swap in (swap_li, swap_att, swap_taps, *(swap_half(n) for n in range(4))):
        swap.wait_send()
    for c in taps_copies:
        c.wait_send()
    for r in rings:
        for stage in r:
            stage.sent()


def collect_kernel(*refs):
    for a, b in zip(refs[:4], refs[4:]):
        b[...] = a[...]


def backward(lengths, li, q, k, v, g, conv, wout, wqkv):
    def vm(shape, dtype=BF16):
        return pltpu.VMEM(shape, dtype)

    buffers = []
    for p, (_, width, order) in enumerate(PARTS):
        leads = []
        for stage in range(3):
            sizes = (("zl", 2), ("y", 4), ("zh", 2), ("x", 4))
            leads.append([n for axis, n in sizes if axis[0] not in order[: stage + 1]])
        if p < NR:
            first = [(*leads[0], 16, w) for w in (width // 2, width // 2, width, width)]
        else:
            first = [(3, *leads[0], 16, width)] + [(16, HD)] * 3
        buffers += [vm(shape) for shape in first]
        buffers.append(vm((3, *leads[1], 16, width)))
        buffers.append(vm((*leads[1], 2, 8, width), F32))
        buffers.append(vm((7, 8, width), F32))
    dma = pltpu.SemaphoreType.DMA
    outs = (
        jax.ShapeDtypeStruct((BF, D), BF16),
        jax.ShapeDtypeStruct((8, 3 * D), F32),
        jax.ShapeDtypeStruct((8, D), F32),
        jax.ShapeDtypeStruct((KW, D), F32),
    )
    results = pl.pallas_call(
        backward_kernel,
        out_shape=outs,
        in_specs=[pl.BlockSpec(memory_space=pltpu.SMEM), ANY, ANY, ANY, ANY, ANY, VM, ANY, ANY],
        out_specs=(ANY, VM, VM, VM),
        scratch_shapes=[
            vm((T, 2 * HD)), vm((T, 2 * HD)), vm((T, 2 * HD)), vm((T, HD)), vm((T, 2 * HD)),
            vm((HD, T)), vm((HD + 16, T)), vm((T, BF), F32), vm((T, T)), vm((T, T)),
            vm((NC, BF, HD)), vm((NC, BF, HD), F32), vm((NC, BF, HD)), vm((NC, BF, HD)),
            vm((NC, BF, HD)), vm((NC, BF, HD)), vm((BF, 3 * D)), vm((BF, D)),
            vm((BF, D)), vm((BF + 16, D), F32), vm((BF, D)), vm((16, D)), vm((16, D)),
            vm((D, D)), vm((D, 3 * D)),
            vm((2 * BF, D)), vm((2 * BF, D)), vm((2 * BF, CW)), vm((D, 2 * BF)), vm((D, 2 * BF)),
            vm((2, 4, 2, 4, 16, CW)),
            vm((2, 16, D), F32), vm((3, 4, 16, D), F32), *buffers,
            dma((8, NC)), dma((8, NC)), dma((2,)), dma((2,)), dma((5,)), dma((8,)), dma((8,)),
            dma((NR * 6,)), dma((NR * 6,)), dma((NP * 6,)), dma((NP * 6,)),
            dma((NP * 7,)), dma((NP * 7,)), dma((9,)), dma((9,)),
        ],
        compiler_params=pltpu.CompilerParams(
            collective_id=0, has_side_effects=True, vmem_limit_bytes=60 * 1024 * 1024
        ),
    )(lengths, li, q, k, v, g, conv, wout, wqkv)
    return pl.pallas_call(
        collect_kernel,
        out_shape=outs,
        in_specs=[VM] * 4,
        out_specs=(VM,) * 4,
    )(*results)


def shards(layer_in, queries, keys, values, lengths, w_qkv, w_out, conv_kernel, grad_out):
    d_input, d_wqkv, d_wout, d_kernel = backward(
        lengths, layer_in[0], queries[0], keys[0], values[0], grad_out[0], conv_kernel, w_out, w_qkv
    )
    return d_input[None], d_wqkv, d_wout, d_kernel


def solution(mesh):
    frames = P("rec", "ctx", None)
    in_specs = (frames, frames, frames, frames, P("rec"), P(), P(), P(), frames)
    out_specs = (frames, P(("ctx", "rec"), None), P(("ctx", "rec"), None), P())
    return jax.shard_map(
        shards, mesh=mesh, in_specs=in_specs, out_specs=out_specs, check_vma=False
    )
```

```python
import math

import jax
import jax.numpy as jnp
from jax import lax
from jax.experimental import pallas as pl
from jax.experimental.pallas import tpu as pltpu
from jax.sharding import PartitionSpec as P

HD = 128
KW = 9
NC = 8
BF = 256
T = NC * BF
D = 1024
F32 = jnp.float32
BF16 = jnp.bfloat16
MESH = pl.DeviceIdType.MESH
KB = 512
NEG = -1e30
NT = (((1,), (1,)), ((), ()))
ANY = pl.BlockSpec(memory_space=pl.ANY)
VM = pl.BlockSpec(memory_space=pltpu.VMEM)

TQ, TK, TV, TD, BA, BQ, BK, BV = range(8)


def mult(value, of):
    return pl.multiple_of(value, of)


def dot(a, b):
    return jnp.dot(a, b, preferred_element_type=F32)


def dot_nt(a, b):
    return lax.dot_general(a, b, NT, preferred_element_type=F32)


HALF = 512
CW = 4 * HALF
OUT, VAL, QUE, KEY = range(4)
PARTS = (
    (0, 512, ("x", "y", "z")),
    (512, 512, ("x", "z", "y")),
    (1024, 256, ("y", "x", "z")),
    (1280, 256, ("z", "x", "y")),
    (1536, 256, ("y", "z", "x")),
    (1792, 256, ("z", "y", "x")),
)
NP = len(PARTS)
NR = 6


def backward_kernel(
    len_ref, li_ref, q_ref, k_ref, v_ref, g_ref, conv_ref, wout_ref, wqkv_ref,
    din_hbm, dwq_hbm, dwo_hbm, dk_hbm,
    q_aug, k_aug, v_aug, do_in, do_aug, k_t, v_t, s_ref, e_ref, ds_ref,
    att_s, linv_s, dq_s, dk_s, dv_s, dat_s, dqkv, din_vm,
    g_vm, gp, dsub, halo_lo, halo_hi, wout_vm, wqkv_vm,
    li2, att2, r2, li_t, att_t, grads, taps_c, taps_a, conv_vm, dwq_out, dwo_out, dk_out, *rest,
):
    bufs = rest[: NP * 7]
    (send_sem, recv_sem, halo_send, halo_recv, local_sem, core_send, core_recv,
     ring_send, ring_recv, step_send, step_recv, last_send, last_recv,
     taps_send, taps_recv) = rest[NP * 7 :]
    me = lax.axis_index("ctx")
    rec = lax.axis_index("rec")
    z, y = lax.div(me, 4), lax.rem(me, 4)
    inv_root = 1.0 / math.sqrt(HD)
    c_exp = math.log2(math.e) / math.sqrt(HD)

    def peer(d):
        return lax.rem(z + lax.div(d, 4), 2) * 4 + lax.rem(y + lax.rem(d, 4), 4)

    def origin(d):
        return lax.rem(z + 2 - lax.div(d, 4), 2) * 4 + lax.rem(y + 4 - lax.rem(d, 4), 4)

    def head_cols(h):
        return pl.ds(mult(h * HD, HD), HD)

    def slot(d):
        return pl.ds(mult(d * BF, BF), BF)

    fwd_src = {TQ: q_ref, TK: k_ref, TV: v_ref}
    fwd_dst = {TQ: q_aug, TK: k_aug, TV: v_aug, TD: do_in}
    back_src = {BA: att_s, BQ: dq_s, BK: dk_s, BV: dv_s}
    back_base = {BQ: 0, BK: D, BV: 2 * D}

    def ends(t, d):
        if t <= TD:
            p = peer(d)
            src = dat_s.at[d] if t == TD else fwd_src[t].at[:, head_cols(p)]
            dst = fwd_dst[t].at[slot(d), pl.ds(0, HD)]
        else:
            p = origin(d)
            src = back_src[t].at[d]
            if t == BA:
                dst = att2.at[pl.ds(0, BF), head_cols(me)]
            else:
                dst = dqkv.at[:, pl.ds(mult(back_base[t] + me * HD, HD), HD)]
        return p, src, dst

    def remote(t, d):
        p, src, dst = ends(t, d)
        return pltpu.make_async_remote_copy(
            src_ref=src, dst_ref=dst, send_sem=send_sem.at[t, d], recv_sem=recv_sem.at[t, d],
            device_id=(p, rec), device_id_type=MESH,
        )

    def local(t):
        _, src, dst = ends(t, 0)
        return pltpu.make_async_copy(src, dst, recv_sem.at[t, 0])

    def each_peer(body):
        def step(d, carry):
            body(d)
            return carry

        lax.fori_loop(1, NC, step, 0)

    def each_slot(body):
        def step(d, carry):
            body(d)
            return carry

        lax.fori_loop(0, NC, step, 0)

    get_g = pltpu.make_async_copy(g_ref, g_vm, local_sem.at[0])
    get_w = pltpu.make_async_copy(wout_ref, wout_vm, local_sem.at[1])
    get_g.start()
    get_w.start()
    for t in (TK, TQ, TV):
        local(t).start()
    mine, theirs = pl.ds(0, BF), pl.ds(BF, BF)
    get_li = pltpu.make_async_copy(li_ref, li2.at[mine, :], local_sem.at[2])
    get_li.start()
    get_wq = pltpu.make_async_copy(wqkv_ref, wqkv_vm, local_sem.at[3])
    get_conv = pltpu.make_async_copy(conv_ref, conv_vm, local_sem.at[5])
    get_conv.start()

    core = lax.rem(rec, 2)
    other = 1 - core
    at = {"x": lax.rem(lax.div(rec, 2), 4), "y": y, "z": lax.div(rec, 8) * 2 + z}

    def device(moved, to, on_core=core):
        p = {**at, **({moved: to} if moved else {})}
        return (
            lax.rem(p["z"], 2) * 4 + p["y"],
            lax.div(p["z"], 2) * 8 + p["x"] * 2 + on_core,
        )

    def off(axis, by):
        return lax.rem(at[axis] + by, 4)

    partner = device(None, None, other)
    far = lax.rem(lax.div(rec, 8) + 1, 2)
    greet = [partner] + [device("x", off("x", by)) for by in (1, 2, 3)]
    greet += [device("z", far * 2 + zl) for zl in (0, 1)]
    greet += [device(a, off(a, by), other) for a in "xyz" for by in (1, 2, 3)]

    barrier = pltpu.get_barrier_semaphore()
    each_peer(
        lambda d: pl.semaphore_signal(barrier, inc=1, device_id=(peer(d), rec), device_id_type=MESH)
    )
    for who in greet:
        pl.semaphore_signal(barrier, inc=1, device_id=who, device_id_type=MESH)
    pl.semaphore_wait(barrier, NC - 1 + len(greet))

    right, left = lax.rem(me + 1, NC), lax.rem(me + NC - 1, NC)
    to_right = pltpu.make_async_remote_copy(
        src_ref=g_ref.at[pl.ds(BF - 16, 16), :], dst_ref=halo_lo, send_sem=halo_send.at[0],
        recv_sem=halo_recv.at[0], device_id=(right, rec), device_id_type=MESH,
    )
    to_left = pltpu.make_async_remote_copy(
        src_ref=g_ref.at[pl.ds(0, 16), :], dst_ref=halo_hi, send_sem=halo_send.at[1],
        recv_sem=halo_recv.at[1], device_id=(left, rec), device_id_type=MESH,
    )
    to_right.start()
    to_left.start()
    for t in (TK, TQ, TV):
        each_peer(lambda d: remote(t, d).start())

    def to_partner(n, src, dst):
        return pltpu.make_async_remote_copy(
            src_ref=src, dst_ref=dst, send_sem=core_send.at[n], recv_sem=core_recv.at[n],
            device_id=partner, device_id_type=MESH,
        )

    def half(ref, base, c):
        return ref.at[:, pl.ds(mult(base + c * HALF, HALF), HALF)]

    group = {OUT: (dsub, 0), VAL: (dqkv, 2 * D), QUE: (dqkv, 0), KEY: (dqkv, D)}

    def swap_half(n):
        ref, base = group[n]
        return to_partner(n, half(ref, base, other), r2.at[theirs, pl.ds(n * HALF, HALF)])

    def own_half(n):
        ref, base = group[n]
        r2[mine, pl.ds(n * HALF, HALF)] = half(ref, base, core)[...]

    swap_li = to_partner(4, li_ref, li2.at[theirs, :])
    swap_att = to_partner(5, att2.at[mine, :], att2.at[theirs, :])
    swap_taps = to_partner(6, taps_c.at[core], taps_c.at[core])
    swap_li.start()

    length = len_ref[0]
    lane = lax.broadcasted_iota(jnp.int32, (BF, HD), 1)
    row = lax.broadcasted_iota(jnp.int32, (BF, HD), 0)

    def extra(d):
        masked = (lane == 0) & (row + origin(d) * BF >= length)
        k_aug[slot(d), pl.ds(HD, HD)] = jnp.where(masked, NEG, 0.0).astype(BF16)
        q_aug[slot(d), pl.ds(HD, HD)] = jnp.where(lane == 0, 1.0, 0.0).astype(BF16)
        v_aug[slot(d), pl.ds(HD, HD)] = jnp.where(lane < 2, 1.0, 0.0).astype(BF16)

    each_slot(extra)
    first = lax.broadcasted_iota(jnp.int32, (16, T), 0) == 0
    v_t[pl.ds(HD, 16), :] = jnp.where(first, 1.0, 0.0).astype(BF16)

    get_g.wait()
    get_conv.wait()
    gp[pl.ds(8, BF), :] = g_vm[...].astype(F32)
    to_right.wait_recv()
    to_left.wait_recv()
    low = halo_lo[...].astype(F32)[8:16, :]
    gp[pl.ds(0, 8), :] = jnp.where(me > 0, low, 0.0)
    high = halo_hi[...].astype(F32)[0:8, :]
    gp[pl.ds(8 + BF, 8), :] = jnp.where(me < NC - 1, high, 0.0)

    def conv_grad(n):
        cols = pl.ds(mult(n * HD, HD), HD)
        total = gp[pl.ds(8, BF), cols]
        for t in range(KW):
            total = total + conv_vm[pl.ds(t, 1), cols] * gp[pl.ds(12 - t, BF), cols]
        dsub[:, cols] = total.astype(BF16)

    each_slot(conv_grad)
    swap_half(OUT).start()
    own_half(OUT)
    get_wq.start()

    get_w.wait()

    def datt(d):
        rows = pl.ds(mult(peer(d) * HD, HD), HD)
        dat_s[d] = dot_nt(dsub[...], wout_vm[rows, :]).astype(BF16)

        @pl.when(d > 0)
        def _():
            remote(TD, d).start()

    each_slot(datt)
    local(TD).start()

    def turn_in(src, dst):
        def step(n, carry):
            cols = pl.ds(mult(n * BF, BF), BF)
            dst[cols, :] = src[:, cols].T
            return carry

        lax.fori_loop(0, D // BF, step, 0)

    get_li.wait()
    swap_li.wait_recv()
    turn_in(li2, li_t)

    def arrived(t):
        local(t).wait()
        each_peer(lambda d: remote(t, d).wait_recv())

    arrived(TK)
    local(TQ).wait()

    def scores(d):
        @pl.when(d > 0)
        def _():
            remote(TQ, d).wait_recv()

        qd = q_aug[slot(d), :]
        top = None
        for b in range(T // KB):
            rows = pl.ds(b * KB, KB)
            s = dot_nt(k_aug[rows, :], qd)
            s_ref[rows, :] = s
            m = jnp.max(s, axis=0, keepdims=True)
            top = m if top is None else jnp.maximum(top, m)
        for b in range(T // KB):
            rows = pl.ds(b * KB, KB)
            e_ref[rows, slot(d)] = jnp.exp2((s_ref[rows, :] - top) * c_exp).astype(BF16)

    each_slot(scores)
    arrived(TV)

    def turn(d):
        k_t[:, slot(d)] = k_aug[slot(d), pl.ds(0, HD)].T
        v_t[pl.ds(0, HD), slot(d)] = v_aug[slot(d), pl.ds(0, HD)].T

    each_slot(turn)

    def attend(d):
        acc = dot(v_t[...], e_ref[:, slot(d)])
        inv = 1.0 / acc[HD : HD + 1, :]
        att_s[d] = (acc[:HD, :] * inv).T.astype(BF16)
        linv_s[d] = jnp.broadcast_to(inv, (HD, BF)).T

        @pl.when(d > 0)
        def _():
            remote(BA, d).start()

    each_slot(attend)
    local(BA).start()

    local(TD).wait()

    def backward_in(d):
        @pl.when(d > 0)
        def _():
            remote(TD, d).wait_recv()

        do = (do_in[slot(d), :].astype(F32) * linv_s[d]).astype(BF16)
        delta = -jnp.sum(do.astype(F32) * att_s[d].astype(F32), axis=1, keepdims=True)
        hi = delta.astype(BF16).astype(F32)
        do_aug[slot(d), pl.ds(0, HD)] = do
        do_aug[slot(d), pl.ds(HD, HD)] = jnp.where(
            lane == 0, hi, jnp.where(lane == 1, delta - hi, 0.0)
        ).astype(BF16)

    each_slot(backward_in)

    def d_value(j):
        two = pl.ds(mult(j * 2 * BF, 2 * BF), 2 * BF)
        dv_s[pl.ds(j * 2, 2)] = dot(e_ref[two, :], do_aug[:, pl.ds(0, HD)]).astype(BF16).reshape(2, BF, HD)

        @pl.when(j > 0)
        def _():
            remote(BV, j * 2).start()

        remote(BV, j * 2 + 1).start()

    lax.fori_loop(0, NC // 2, lambda j, c: (d_value(j), c)[1], 0)
    local(BV).start()

    def d_query(d):
        dod = do_aug[slot(d), :]
        acc = jnp.zeros((HD, BF), F32)
        for b in range(T // KB):
            rows = pl.ds(b * KB, KB)
            dp = dot_nt(v_aug[rows, :], dod)
            ds = (e_ref[rows, slot(d)].astype(F32) * dp).astype(BF16)
            ds_ref[rows, slot(d)] = ds
            acc = acc + dot(k_t[:, rows], ds)
        dq_s[d] = (acc * inv_root).T.astype(BF16)

        @pl.when(d > 0)
        def _():
            remote(BQ, d).start()

    lax.fori_loop(0, 5, lambda d, c: (d_query(d), c)[1], 0)
    arrived(BA)
    swap_att.start()
    lax.fori_loop(5, NC, lambda d, c: (d_query(d), c)[1], 0)
    local(BQ).start()

    def product(lhs, start, width):
        def step(zl, carry):
            rows = pl.ds(mult(zl * HALF, HALF), HALF)
            g = dot(lhs[rows, :], r2[:, pl.ds(start, width)]).astype(BF16)
            grads[zl, :, :, :, :, pl.ds(start, width)] = g.reshape(4, 2, 4, 16, width)
            return carry

        lax.fori_loop(0, 2, step, 0)

    def region(fixed, start, width):
        zl = zh = slice(None)
        if "z" in fixed:
            zl, zh = lax.rem(fixed["z"], 2), lax.div(fixed["z"], 2)
        return grads.at[
            zl, fixed.get("y", slice(None)), zh, fixed.get("x", slice(None)), :, pl.ds(start, width)
        ]

    class Stage:
        def __init__(self, part, stage):
            self.start, self.width, order = PARTS[part]
            self.part = part
            self.axis = order[stage]
            self.fixed = {a: at[a] for a in order[:stage]}
            self.stage = stage

        def piece(self, by, start=0, width=None):
            width = self.width if width is None else width
            fixed = {**self.fixed, self.axis: off(self.axis, by)}
            return region(fixed, self.start + start, width)

        def copy(self, sems, n, src, dst, by):
            return pltpu.make_async_remote_copy(
                src_ref=src, dst_ref=dst, send_sem=sems[0].at[n], recv_sem=sems[1].at[n],
                device_id=device(self.axis, off(self.axis, by)), device_id_type=MESH,
            )

        def keep(self, total):
            if self.stage == 0:
                self.piece(0)[...] = total.astype(BF16)
            else:
                pair = bufs[self.part * 7 + 5]
                pair[..., 0, :, :] = total[..., :8, :]
                pair[..., 1, :, :] = total[..., 8:, :]

        def sent(self):
            for c in self.copies:
                c.wait_send()

    class Ring(Stage):
        def __init__(self, part):
            super().__init__(part, 0)
            self.ra, self.rb, self.low, self.high = bufs[part * 7 : part * 7 + 4]
            h = self.width // 2
            lead = (slice(None),) * (len(self.low.shape) - 1)
            a, b = (*lead, pl.ds(0, h)), (*lead, pl.ds(h, h))
            ends = (
                (self.piece(2, 0, h), self.ra, 1),
                (self.piece(2, h, h), self.rb, 3),
                (self.piece(1, h, h), self.low.at[b], 1),
                (self.piece(3, 0, h), self.high.at[a], 3),
                (self.piece(1, 0, h), self.low.at[a], 1),
                (self.piece(3, h, h), self.high.at[b], 3),
            )
            sems = (ring_send, ring_recv)
            self.copies = [self.copy(sems, part * 6 + n, *e) for n, e in enumerate(ends)]

        def begin(self):
            for c in self.copies[:4]:
                c.start()

        def relay(self):
            h = self.width // 2
            for n, by, buf, start in ((0, 1, self.ra, 0), (1, 3, self.rb, h)):
                self.copies[n].wait_recv()
                here = self.piece(by, start, h)
                here[...] = (here[...].astype(F32) + buf[...].astype(F32)).astype(BF16)
                self.copies[4 + n].start()

        def end(self):
            for n in (2, 3, 4, 5):
                self.copies[n].wait_recv()
            here = self.piece(0)[...].astype(F32)
            self.keep(here + (self.low[...].astype(F32) + self.high[...].astype(F32)))

    class Direct(Stage):
        def __init__(self, part, stage):
            super().__init__(part, stage)
            self.buf = bufs[part * 7 + 3 + stage] if stage else bufs[part * 7]
            base = (part * 2 + stage) * 3
            sems = (step_send, step_recv)
            self.copies = [
                self.copy(sems, base + by - 1, self.piece(by), self.buf.at[by - 1], by)
                for by in (1, 2, 3)
            ]

        def begin(self):
            for c in self.copies:
                c.start()

        def end(self):
            for c in self.copies:
                c.wait_recv()
            here = self.piece(0)[...].astype(F32)
            b = [self.buf[n].astype(F32) for n in range(3)]
            self.keep((here + b[0]) + (b[1] + b[2]))

    class Last(Stage):
        def __init__(self, part):
            super().__init__(part, 2)
            self.pair, self.buf = bufs[part * 7 + 5 : part * 7 + 7]
            self.copies = []
            for n, (turned, by) in enumerate((t, b) for t in (0, 1) for b in range(4) if t + b):
                to = lax.rem(core + turned, 2)
                who = device(self.axis, off(self.axis, by), to)
                self.copies.append(
                    pltpu.make_async_remote_copy(
                        src_ref=self.rows(by, to), dst_ref=self.buf.at[n],
                        send_sem=last_send.at[part * 7 + n], recv_sem=last_recv.at[part * 7 + n],
                        device_id=who, device_id_type=MESH,
                    )
                )

        def rows(self, by, to):
            chip = off(self.axis, by)
            if self.axis == "z":
                return self.pair.at[lax.rem(chip, 2), lax.div(chip, 2), to]
            return self.pair.at[chip, to]

        def begin(self):
            for c in self.copies:
                c.start()

        def end(self):
            for c in self.copies:
                c.wait_recv()
            b = [self.buf[n] for n in range(7)]
            here = self.rows(0, core)[...]
            n, inside = divmod(self.start, HALF)
            out, base = ((dwo_out, 0), (dwq_out, 2 * D), (dwq_out, 0), (dwq_out, D))[n]
            for who, block in (
                (core, (here + b[0]) + (b[1] + b[2])),
                (other, (b[3] + b[4]) + (b[5] + b[6])),
            ):
                cols = pl.ds(mult(base + who * HALF + inside, HD), self.width)
                out[:, cols] = block

    rings = [(Ring(p) if p < NR else Direct(p, 0), Direct(p, 1), Last(p)) for p in range(NP)]

    def on(p, stage):
        rings[p][stage].end()
        rings[p][stage + 1].begin()

    taps_copies = []

    def taps_on(n, axis, value):
        taps_a[n, at[axis]] = value
        for by in (1, 2, 3):
            c = pltpu.make_async_remote_copy(
                src_ref=taps_a.at[n, at[axis]], dst_ref=taps_a.at[n, at[axis]],
                send_sem=taps_send.at[n * 3 + by - 1], recv_sem=taps_recv.at[n * 3 + by - 1],
                device_id=device(axis, off(axis, by)), device_id_type=MESH,
            )
            c.start()
            taps_copies.append(c)

    def taps_sum(n):
        for c in taps_copies[n * 3 :]:
            c.wait_recv()
        return (taps_a[n, 0] + taps_a[n, 1]) + (taps_a[n, 2] + taps_a[n, 3])

    swap_half(OUT).wait_recv()
    swap_att.wait_recv()
    turn_in(att2, att_t)
    product(att_t, OUT * HALF, HALF)
    rings[0][0].begin()

    def d_key(j):
        two = pl.ds(mult(j * 2 * BF, 2 * BF), 2 * BF)
        dk_s[pl.ds(j * 2, 2)] = (dot(ds_ref[two, :], q_aug[:, pl.ds(0, HD)]) * inv_root).astype(BF16).reshape(2, BF, HD)

        @pl.when(j > 0)
        def _():
            remote(BK, j * 2).start()

        remote(BK, j * 2 + 1).start()

    lax.fori_loop(0, NC // 2, lambda j, c: (d_key(j), c)[1], 0)
    local(BK).start()

    def taps(n):
        cols = pl.ds(mult(n * BF, BF), BF)
        sub = dot(att2[mine, :], wout_vm[:, cols]).astype(BF16).astype(F32)
        for t in range(KW):
            taps_c[core, pl.ds(t, 1), cols] = jnp.sum(
                sub * gp[pl.ds(12 - t, BF), cols], axis=0, keepdims=True
            )

    def back(t, n):
        arrived(t)
        swap_half(n).start()
        own_half(n)

    def weight(n):
        swap_half(n).wait_recv()
        product(li_t, n * HALF, HALF)

    def d_input(n, carry):
        cols = pl.ds(mult(n * BF, BF), BF)
        din_vm[:, cols] = dot_nt(dqkv[...], wqkv_vm[cols, :]).astype(BF16)
        return carry

    back(BV, VAL)
    rings[0][0].relay()
    taps_c[core] = jnp.zeros((16, D), F32)
    lax.fori_loop(0, D // BF, lambda n, c: (taps(n), c)[1], 0)
    swap_taps.start()
    weight(VAL)
    rings[1][0].begin()
    back(BQ, QUE)
    get_wq.wait()
    swap_taps.wait_recv()
    taps_on(0, "x", taps_c[0] + taps_c[1])
    weight(QUE)
    rings[2][0].begin()
    rings[3][0].begin()
    back(BK, KEY)
    lax.fori_loop(0, 2, d_input, 0)
    weight(KEY)
    rings[4][0].begin()
    rings[5][0].begin()
    rings[1][0].relay()
    rings[2][0].relay()
    rings[3][0].relay()
    on(0, 0)
    rings[4][0].relay()
    rings[5][0].relay()
    lax.fori_loop(2, 4, d_input, 0)
    put_din = pltpu.make_async_copy(din_vm, din_hbm, local_sem.at[4])
    put_din.start()
    taps_on(1, "y", taps_sum(0))
    on(2, 0)
    on(3, 0)
    on(0, 1)
    on(1, 0)
    on(4, 0)
    on(5, 0)
    taps_on(2, "z", taps_sum(1))
    for p in (2, 3, 1, 4, 5):
        on(p, 1)
    dk_out[...] = taps_sum(2)[:KW]
    puts = [
        pltpu.make_async_copy(a, b, local_sem.at[n])
        for a, b, n in ((dk_out, dk_hbm, 6), (dwo_out, dwo_hbm, 7), (dwq_out, dwq_hbm, 8))
    ]
    puts[0].start()
    to_right.wait_send()
    to_left.wait_send()
    for t in range(8):
        each_peer(lambda d: remote(t, d).wait_send())
    for swap in (swap_li, swap_att, swap_taps, *(swap_half(n) for n in range(4))):
        swap.wait_send()
    for c in taps_copies:
        c.wait_send()
    for r in rings:
        r[0].sent()
        r[1].sent()
    rings[0][2].end()
    puts[1].start()
    for p in range(1, NP):
        rings[p][2].end()
    puts[2].start()
    for r in rings:
        r[2].sent()
    put_din.wait()
    for put in puts:
        put.wait()


def collect_kernel(*refs):
    for a, b in zip(refs[:4], refs[4:]):
        b[...] = a[...]


def backward(lengths, li, q, k, v, g, conv, wout, wqkv):
    def vm(shape, dtype=BF16):
        return pltpu.VMEM(shape, dtype)

    buffers = []
    for p, (_, width, order) in enumerate(PARTS):
        leads = []
        for stage in range(3):
            sizes = (("zl", 2), ("y", 4), ("zh", 2), ("x", 4))
            leads.append([n for axis, n in sizes if axis[0] not in order[: stage + 1]])
        if p < NR:
            first = [(*leads[0], 16, w) for w in (width // 2, width // 2, width, width)]
        else:
            first = [(3, *leads[0], 16, width)] + [(16, HD)] * 3
        buffers += [vm(shape) for shape in first]
        buffers.append(vm((3, *leads[1], 16, width)))
        buffers.append(vm((*leads[1], 2, 8, width), F32))
        buffers.append(vm((7, 8, width), F32))
    dma = pltpu.SemaphoreType.DMA
    outs = (
        jax.ShapeDtypeStruct((BF, D), BF16),
        jax.ShapeDtypeStruct((8, 3 * D), F32),
        jax.ShapeDtypeStruct((8, D), F32),
        jax.ShapeDtypeStruct((KW, D), F32),
    )
    results = pl.pallas_call(
        backward_kernel,
        out_shape=outs,
        in_specs=[pl.BlockSpec(memory_space=pltpu.SMEM)] + [ANY] * 8,
        out_specs=(ANY,) * 4,
        scratch_shapes=[
            vm((T, 2 * HD)), vm((T, 2 * HD)), vm((T, 2 * HD)), vm((T, HD)), vm((T, 2 * HD)),
            vm((HD, T)), vm((HD + 16, T)), vm((T, BF), F32), vm((T, T)), vm((T, T)),
            vm((NC, BF, HD)), vm((NC, BF, HD), F32), vm((NC, BF, HD)), vm((NC, BF, HD)),
            vm((NC, BF, HD)), vm((NC, BF, HD)), vm((BF, 3 * D)), vm((BF, D)),
            vm((BF, D)), vm((BF + 16, D), F32), vm((BF, D)), vm((16, D)), vm((16, D)),
            vm((D, D)), vm((D, 3 * D)),
            vm((2 * BF, D)), vm((2 * BF, D)), vm((2 * BF, CW)), vm((D, 2 * BF)), vm((D, 2 * BF)),
            vm((2, 4, 2, 4, 16, CW)),
            vm((2, 16, D), F32), vm((3, 4, 16, D), F32),
            vm((KW, D), F32), vm((8, 3 * D), F32), vm((8, D), F32), vm((KW, D), F32), *buffers,
            dma((8, NC)), dma((8, NC)), dma((2,)), dma((2,)), dma((9,)), dma((8,)), dma((8,)),
            dma((NR * 6,)), dma((NR * 6,)), dma((NP * 6,)), dma((NP * 6,)),
            dma((NP * 7,)), dma((NP * 7,)), dma((9,)), dma((9,)),
        ],
        compiler_params=pltpu.CompilerParams(
            collective_id=0, has_side_effects=True, vmem_limit_bytes=60 * 1024 * 1024
        ),
    )(lengths, li, q, k, v, g, conv, wout, wqkv)
    return pl.pallas_call(
        collect_kernel,
        out_shape=outs,
        in_specs=[VM] * 4,
        out_specs=(VM,) * 4,
    )(*results)


def shards(layer_in, queries, keys, values, lengths, w_qkv, w_out, conv_kernel, grad_out):
    d_input, d_wqkv, d_wout, d_kernel = backward(
        lengths, layer_in[0], queries[0], keys[0], values[0], grad_out[0], conv_kernel, w_out, w_qkv
    )
    return d_input[None], d_wqkv, d_wout, d_kernel


def solution(mesh):
    frames = P("rec", "ctx", None)
    in_specs = (frames, frames, frames, frames, P("rec"), P(), P(), P(), frames)
    out_specs = (frames, P(("ctx", "rec"), None), P(("ctx", "rec"), None), P())
    return jax.shard_map(
        shards, mesh=mesh, in_specs=in_specs, out_specs=out_specs, check_vma=False
    )
```

```python
import math

import jax
import jax.numpy as jnp
from jax import lax
from jax.experimental import pallas as pl
from jax.experimental.pallas import tpu as pltpu
from jax.sharding import PartitionSpec as P

HD = 128
KW = 9
NC = 8
BF = 256
T = NC * BF
D = 1024
F32 = jnp.float32
BF16 = jnp.bfloat16
MESH = pl.DeviceIdType.MESH
KB = 512
NEG = -1e30
NT = (((1,), (1,)), ((), ()))
ANY = pl.BlockSpec(memory_space=pl.ANY)
VM = pl.BlockSpec(memory_space=pltpu.VMEM)

TQ, TK, TV, TD, BA, BQ, BK, BV = range(8)


def mult(value, of):
    return pl.multiple_of(value, of)


def dot(a, b):
    return jnp.dot(a, b, preferred_element_type=F32)


def dot_nt(a, b):
    return lax.dot_general(a, b, NT, preferred_element_type=F32)


HALF = 512
CW = 4 * HALF
OUT, VAL, QUE, KEY = range(4)
PARTS = (
    (0, 512, ("x", "y", "z")),
    (512, 512, ("x", "z", "y")),
    (1024, 256, ("y", "x", "z")),
    (1280, 256, ("z", "x", "y")),
    (1536, 256, ("y", "z", "x")),
    (1792, 256, ("z", "y", "x")),
)
NP = len(PARTS)


def backward_kernel(
    len_ref, li_ref, q_ref, k_ref, v_ref, g_ref, conv_ref, wout_ref, wqkv_ref,
    din_hbm, dwq_hbm, dwo_hbm, dk_hbm,
    q_aug, k_aug, v_aug, do_in, do_aug, k_t, v_t, s_ref, e_ref, ds_ref,
    att_s, linv_s, dq_s, dk_s, dv_s, dat_s, dqkv, din_vm,
    g_vm, gp, dsub, halo_lo, halo_hi, wout_vm, wqkv_vm,
    li2, att2, r2, li_t, att_t, grads, taps_c, taps_p, taps_a, taps_z, conv_vm, dwq_out, dwo_out, dk_out, *rest,
):
    bufs = rest[: NP * 6]
    (send_sem, recv_sem, q_recv, halo_send, halo_recv, local_sem, core_send, core_recv,
     ring_send, ring_recv, step_send, step_recv, last_send, last_recv,
     taps_send, taps_recv) = rest[NP * 6 :]
    me = lax.axis_index("ctx")
    rec = lax.axis_index("rec")
    z, y = lax.div(me, 4), lax.rem(me, 4)
    inv_root = 1.0 / math.sqrt(HD)
    c_exp = math.log2(math.e) / math.sqrt(HD)

    def peer(d):
        return lax.rem(z + lax.div(d, 4), 2) * 4 + lax.rem(y + lax.rem(d, 4), 4)

    def origin(d):
        return lax.rem(z + 2 - lax.div(d, 4), 2) * 4 + lax.rem(y + 4 - lax.rem(d, 4), 4)

    def head_cols(h):
        return pl.ds(mult(h * HD, HD), HD)

    def slot(d):
        return pl.ds(mult(d * BF, BF), BF)

    fwd_src = {TQ: q_ref, TK: k_ref, TV: v_ref}
    fwd_dst = {TQ: q_aug, TK: k_aug, TV: v_aug, TD: do_in}
    back_src = {BA: att_s, BQ: dq_s, BK: dk_s, BV: dv_s}
    back_base = {BQ: 0, BK: D, BV: 2 * D}

    def ends(t, d):
        if t <= TD:
            p = peer(d)
            src = dat_s.at[d] if t == TD else fwd_src[t].at[:, head_cols(p)]
            dst = fwd_dst[t].at[slot(d), pl.ds(0, HD)]
        else:
            p = origin(d)
            src = back_src[t].at[d]
            if t == BA:
                dst = att2.at[pl.ds(0, BF), head_cols(me)]
            else:
                dst = dqkv.at[:, pl.ds(mult(back_base[t] + me * HD, HD), HD)]
        return p, src, dst

    def remote(t, d):
        p, src, dst = ends(t, d)
        return pltpu.make_async_remote_copy(
            src_ref=src, dst_ref=dst, send_sem=send_sem.at[t],
            recv_sem=q_recv.at[d] if t == TQ else recv_sem.at[t],
            device_id=(p, rec), device_id_type=MESH,
        )

    def local(t):
        _, src, dst = ends(t, 0)
        return pltpu.make_async_copy(src, dst, q_recv.at[0] if t == TQ else recv_sem.at[t])

    def whole(ref, sem):
        pltpu.make_async_copy(ref, ref, sem).wait()

    def drain(sem, count):
        whole(s_ref.at[pl.ds(0, count // (4 * BF)), :], sem)

    def arrived(t):
        if t <= TD:
            whole(fwd_dst[t].at[:, pl.ds(0, HD)], recv_sem.at[t])
        elif t == BA:
            whole(att2.at[pl.ds(0, BF), :], recv_sem.at[t])
        else:
            whole(dqkv.at[:, pl.ds(back_base[t], D)], recv_sem.at[t])

    def each_peer(body):
        def step(d, carry):
            body(d)
            return carry

        lax.fori_loop(1, NC, step, 0)

    def each_slot(body):
        def step(d, carry):
            body(d)
            return carry

        lax.fori_loop(0, NC, step, 0)

    get_g = pltpu.make_async_copy(g_ref, g_vm, local_sem.at[0])
    get_w = pltpu.make_async_copy(wout_ref, wout_vm, local_sem.at[1])
    get_g.start()
    get_w.start()
    for t in (TK, TQ, TV):
        local(t).start()
    mine, theirs = pl.ds(0, BF), pl.ds(BF, BF)
    get_li = pltpu.make_async_copy(li_ref, li2.at[mine, :], local_sem.at[2])
    get_li.start()
    get_wq = pltpu.make_async_copy(wqkv_ref, wqkv_vm, local_sem.at[3])
    get_conv = pltpu.make_async_copy(conv_ref, conv_vm, local_sem.at[5])
    get_conv.start()

    core = lax.rem(rec, 2)
    other = 1 - core
    at = {"x": lax.rem(lax.div(rec, 2), 4), "y": y, "z": lax.div(rec, 8) * 2 + z}

    def device(moved, to, on_core=core):
        p = {**at, **({moved: to} if moved else {})}
        return (
            lax.rem(p["z"], 2) * 4 + p["y"],
            lax.div(p["z"], 2) * 8 + p["x"] * 2 + on_core,
        )

    def off(axis, by):
        return lax.rem(at[axis] + by, 4)

    partner = device(None, None, other)
    far = lax.rem(lax.div(rec, 8) + 1, 2)
    greet = [partner] + [device("x", off("x", by)) for by in (1, 2, 3)]
    greet += [device("z", far * 2 + zl) for zl in (0, 1)]
    greet += [device(a, off(a, by), other) for a in "xyz" for by in (1, 2, 3)]

    barrier = pltpu.get_barrier_semaphore()
    each_peer(
        lambda d: pl.semaphore_signal(barrier, inc=1, device_id=(peer(d), rec), device_id_type=MESH)
    )
    for who in greet:
        pl.semaphore_signal(barrier, inc=1, device_id=who, device_id_type=MESH)
    pl.semaphore_wait(barrier, NC - 1 + len(greet))

    right, left = lax.rem(me + 1, NC), lax.rem(me + NC - 1, NC)
    to_right = pltpu.make_async_remote_copy(
        src_ref=g_ref.at[pl.ds(BF - 16, 16), :], dst_ref=halo_lo, send_sem=halo_send,
        recv_sem=halo_recv.at[0], device_id=(right, rec), device_id_type=MESH,
    )
    to_left = pltpu.make_async_remote_copy(
        src_ref=g_ref.at[pl.ds(0, 16), :], dst_ref=halo_hi, send_sem=halo_send,
        recv_sem=halo_recv.at[1], device_id=(left, rec), device_id_type=MESH,
    )
    to_right.start()
    to_left.start()
    for t in (TK, TQ, TV):
        each_peer(lambda d: remote(t, d).start())

    def to_partner(n, src, dst):
        return pltpu.make_async_remote_copy(
            src_ref=src, dst_ref=dst, send_sem=core_send.at[n], recv_sem=core_recv.at[n],
            device_id=partner, device_id_type=MESH,
        )

    def half(ref, base, c):
        return ref.at[:, pl.ds(mult(base + c * HALF, HALF), HALF)]

    group = {OUT: (dsub, 0), VAL: (dqkv, 2 * D), QUE: (dqkv, 0), KEY: (dqkv, D)}

    def swap_half(n):
        ref, base = group[n]
        return to_partner(n, half(ref, base, other), r2.at[theirs, pl.ds(n * HALF, HALF)])

    def own_half(n):
        ref, base = group[n]
        r2[mine, pl.ds(n * HALF, HALF)] = half(ref, base, core)[...]

    swap_li = to_partner(4, li_ref, li2.at[theirs, :])
    swap_att = to_partner(5, att2.at[mine, :], att2.at[theirs, :])
    swap_taps = to_partner(6, taps_c.at[pl.ds(other * 4, 5)], taps_p)
    swap_li.start()

    length = len_ref[0]
    lane = lax.broadcasted_iota(jnp.int32, (BF, HD), 1)
    row = lax.broadcasted_iota(jnp.int32, (BF, HD), 0)

    def extra(d):
        masked = (lane == 0) & (row + origin(d) * BF >= length)
        k_aug[slot(d), pl.ds(HD, HD)] = jnp.where(masked, NEG, 0.0).astype(BF16)
        q_aug[slot(d), pl.ds(HD, HD)] = jnp.where(lane == 0, 1.0, 0.0).astype(BF16)
        v_aug[slot(d), pl.ds(HD, HD)] = jnp.where(lane < 2, 1.0, 0.0).astype(BF16)

    each_slot(extra)
    first = lax.broadcasted_iota(jnp.int32, (16, T), 0) == 0
    v_t[pl.ds(HD, 16), :] = jnp.where(first, 1.0, 0.0).astype(BF16)

    get_g.wait()
    get_conv.wait()
    gp[pl.ds(8, BF), :] = g_vm[...].astype(F32)
    to_right.wait_recv()
    to_left.wait_recv()
    low = halo_lo[...].astype(F32)[8:16, :]
    gp[pl.ds(0, 8), :] = jnp.where(me > 0, low, 0.0)
    high = halo_hi[...].astype(F32)[0:8, :]
    gp[pl.ds(8 + BF, 8), :] = jnp.where(me < NC - 1, high, 0.0)

    def conv_grad(n):
        cols = pl.ds(mult(n * HD, HD), HD)
        total = gp[pl.ds(8, BF), cols]
        for t in range(KW):
            total = total + conv_vm[pl.ds(t, 1), cols] * gp[pl.ds(12 - t, BF), cols]
        dsub[:, cols] = total.astype(BF16)

    each_slot(conv_grad)
    swap_half(OUT).start()
    own_half(OUT)
    get_wq.start()

    get_w.wait()

    def datt(d):
        rows = pl.ds(mult(peer(d) * HD, HD), HD)
        dat_s[d] = dot_nt(dsub[...], wout_vm[rows, :]).astype(BF16)

        @pl.when(d > 0)
        def _():
            remote(TD, d).start()

    each_slot(datt)
    local(TD).start()

    def turn_in(src, dst):
        def step(n, carry):
            cols = pl.ds(mult(n * BF, BF), BF)
            dst[cols, :] = src[:, cols].T
            return carry

        lax.fori_loop(0, D // BF, step, 0)

    get_li.wait()
    swap_li.wait_recv()
    turn_in(li2, li_t)

    arrived(TK)
    local(TQ).wait()

    def scores(d):
        @pl.when(d > 0)
        def _():
            remote(TQ, d).wait_recv()

        qd = q_aug[slot(d), :]
        top = None
        for b in range(T // KB):
            rows = pl.ds(b * KB, KB)
            s = dot_nt(k_aug[rows, :], qd)
            s_ref[rows, :] = s
            m = jnp.max(s, axis=0, keepdims=True)
            top = m if top is None else jnp.maximum(top, m)
        for b in range(T // KB):
            rows = pl.ds(b * KB, KB)
            e_ref[rows, slot(d)] = jnp.exp2((s_ref[rows, :] - top) * c_exp).astype(BF16)

    each_slot(scores)
    arrived(TV)

    def turn(d):
        k_t[:, slot(d)] = k_aug[slot(d), pl.ds(0, HD)].T
        v_t[pl.ds(0, HD), slot(d)] = v_aug[slot(d), pl.ds(0, HD)].T

    each_slot(turn)

    def attend(d):
        acc = dot(v_t[...], e_ref[:, slot(d)])
        inv = 1.0 / acc[HD : HD + 1, :]
        att_s[d] = (acc[:HD, :] * inv).T.astype(BF16)
        linv_s[d] = jnp.broadcast_to(inv, (HD, BF)).T

        @pl.when(d > 0)
        def _():
            remote(BA, d).start()

    each_slot(attend)
    local(BA).start()

    arrived(TD)

    def backward_in(d):
        do = (do_in[slot(d), :].astype(F32) * linv_s[d]).astype(BF16)
        delta = -jnp.sum(do.astype(F32) * att_s[d].astype(F32), axis=1, keepdims=True)
        hi = delta.astype(BF16).astype(F32)
        do_aug[slot(d), pl.ds(0, HD)] = do
        do_aug[slot(d), pl.ds(HD, HD)] = jnp.where(
            lane == 0, hi, jnp.where(lane == 1, delta - hi, 0.0)
        ).astype(BF16)

    each_slot(backward_in)

    def d_value(j):
        two = pl.ds(mult(j * 2 * BF, 2 * BF), 2 * BF)
        dv_s[pl.ds(j * 2, 2)] = dot(e_ref[two, :], do_aug[:, pl.ds(0, HD)]).astype(BF16).reshape(2, BF, HD)

        @pl.when(j > 0)
        def _():
            remote(BV, j * 2).start()

        remote(BV, j * 2 + 1).start()

    lax.fori_loop(0, NC // 2, lambda j, c: (d_value(j), c)[1], 0)
    local(BV).start()

    def d_query(d):
        dod = do_aug[slot(d), :]
        acc = jnp.zeros((HD, BF), F32)
        for b in range(T // KB):
            rows = pl.ds(b * KB, KB)
            dp = dot_nt(v_aug[rows, :], dod)
            ds = (e_ref[rows, slot(d)].astype(F32) * dp).astype(BF16)
            ds_ref[rows, slot(d)] = ds
            acc = acc + dot(k_t[:, rows], ds)
        dq_s[d] = (acc * inv_root).T.astype(BF16)

        @pl.when(d > 0)
        def _():
            remote(BQ, d).start()

    lax.fori_loop(0, 5, lambda d, c: (d_query(d), c)[1], 0)
    arrived(BA)
    swap_att.start()
    lax.fori_loop(5, NC, lambda d, c: (d_query(d), c)[1], 0)
    local(BQ).start()

    def product(lhs, start, width):
        def step(zl, carry):
            rows = pl.ds(mult(zl * HALF, HALF), HALF)
            g = dot(lhs[rows, :], r2[:, pl.ds(start, width)]).astype(BF16)
            grads[zl, :, :, :, :, pl.ds(start, width)] = g.reshape(4, 2, 4, 16, width)
            return carry

        lax.fori_loop(0, 2, step, 0)

    def region(fixed, start, width):
        zl = zh = slice(None)
        if "z" in fixed:
            zl, zh = lax.rem(fixed["z"], 2), lax.div(fixed["z"], 2)
        return grads.at[
            zl, fixed.get("y", slice(None)), zh, fixed.get("x", slice(None)), :, pl.ds(start, width)
        ]

    class Stage:
        def __init__(self, part, stage):
            self.start, self.width, order = PARTS[part]
            self.part = part
            self.axis = order[stage]
            self.fixed = {a: at[a] for a in order[:stage]}
            self.stage = stage

        def piece(self, by, start=0, width=None):
            width = self.width if width is None else width
            fixed = {**self.fixed, self.axis: off(self.axis, by)}
            return region(fixed, self.start + start, width)

        def copy(self, src, dst, by, recv):
            return pltpu.make_async_remote_copy(
                src_ref=src, dst_ref=dst, send_sem=self.send, recv_sem=recv,
                device_id=device(self.axis, off(self.axis, by)), device_id_type=MESH,
            )

        def keep(self, total):
            if self.stage == 0:
                self.piece(0)[...] = total.astype(BF16)
            else:
                pair = bufs[self.part * 6 + 4]
                pair[..., 0, :, :] = total[..., :8, :]
                pair[..., 1, :, :] = total[..., 8:, :]

        def sent(self):
            drain(self.send, self.sent_bytes)

    class Ring(Stage):
        def __init__(self, part):
            super().__init__(part, 0)
            self.ra, self.rb, self.ends = bufs[part * 6 : part * 6 + 3]
            h = self.width // 2
            lead = (slice(None),) * (len(self.ra.shape) - 1)
            low_a, low_b = (0, *lead, pl.ds(0, h)), (0, *lead, pl.ds(h, h))
            high_a, high_b = (1, *lead, pl.ds(0, h)), (1, *lead, pl.ds(h, h))
            self.send = ring_send.at[part]
            self.sent_bytes = 3 * 4 * HALF * self.width // 4 * 2 // 2
            recv = [ring_recv.at[part * 3 + n] for n in range(3)]
            self.copies = [
                self.copy(self.piece(2, 0, h), self.ra, 1, recv[0]),
                self.copy(self.piece(2, h, h), self.rb, 3, recv[1]),
                self.copy(self.piece(1, h, h), self.ends.at[low_b], 1, recv[2]),
                self.copy(self.piece(3, 0, h), self.ends.at[high_a], 3, recv[2]),
                self.copy(self.piece(1, 0, h), self.ends.at[low_a], 1, recv[2]),
                self.copy(self.piece(3, h, h), self.ends.at[high_b], 3, recv[2]),
            ]
            self.recv = recv[2]

        def begin(self):
            for c in self.copies[:4]:
                c.start()

        def relay(self):
            h = self.width // 2
            for n, by, buf, start in ((0, 1, self.ra, 0), (1, 3, self.rb, h)):
                self.copies[n].wait_recv()
                here = self.piece(by, start, h)
                here[...] = (here[...].astype(F32) + buf[...].astype(F32)).astype(BF16)
                self.copies[4 + n].start()

        def end(self):
            whole(self.ends, self.recv)
            here = self.piece(0)[...].astype(F32)
            self.keep(here + (self.ends[0].astype(F32) + self.ends[1].astype(F32)))

    class Direct(Stage):
        def __init__(self, part, stage):
            super().__init__(part, stage)
            self.buf = bufs[part * 6 + 3]
            self.send, self.recv = step_send.at[part], step_recv.at[part]
            self.sent_bytes = 3 * HD // 2 * self.width * 2
            self.copies = [
                self.copy(self.piece(by), self.buf.at[by - 1], by, self.recv) for by in (1, 2, 3)
            ]

        def begin(self):
            for c in self.copies:
                c.start()

        def end(self):
            whole(self.buf, self.recv)
            here = self.piece(0)[...].astype(F32)
            b = [self.buf[n].astype(F32) for n in range(3)]
            self.keep((here + b[0]) + (b[1] + b[2]))

    class Last(Stage):
        def __init__(self, part):
            super().__init__(part, 2)
            self.pair, self.buf = bufs[part * 6 + 4 : part * 6 + 6]
            self.send, self.recv = last_send.at[part], last_recv.at[part]
            self.sent_bytes = 7 * 8 * self.width * 4
            self.copies = []
            for n, (turned, by) in enumerate((t, b) for t in (0, 1) for b in range(4) if t + b):
                to = lax.rem(core + turned, 2)
                who = device(self.axis, off(self.axis, by), to)
                self.copies.append(
                    pltpu.make_async_remote_copy(
                        src_ref=self.rows(by, to), dst_ref=self.buf.at[n],
                        send_sem=self.send, recv_sem=self.recv,
                        device_id=who, device_id_type=MESH,
                    )
                )

        def rows(self, by, to):
            chip = off(self.axis, by)
            if self.axis == "z":
                return self.pair.at[lax.rem(chip, 2), lax.div(chip, 2), to]
            return self.pair.at[chip, to]

        def begin(self):
            for c in self.copies:
                c.start()

        def end(self):
            whole(self.buf, self.recv)
            b = [self.buf[n] for n in range(7)]
            here = self.rows(0, core)[...]
            n, inside = divmod(self.start, HALF)
            out, base = ((dwo_out, 0), (dwq_out, 2 * D), (dwq_out, 0), (dwq_out, D))[n]
            for who, block in (
                (core, (here + b[0]) + (b[1] + b[2])),
                (other, (b[3] + b[4]) + (b[5] + b[6])),
            ):
                cols = pl.ds(mult(base + who * HALF + inside, HD), self.width)
                out[:, cols] = block

    rings = [(Ring(p), Direct(p, 1), Last(p)) for p in range(NP)]

    def on(p, stage):
        rings[p][stage].end()
        rings[p][stage + 1].begin()

    def taps_copy(n, src, dst, who):
        pltpu.make_async_remote_copy(
            src_ref=src, dst_ref=dst, send_sem=taps_send.at[n], recv_sem=taps_recv.at[n],
            device_id=who, device_id_type=MESH,
        ).start()

    def taps_on(n, axis, value):
        here = taps_a.at[n, at[axis]]
        here[...] = value
        for by in (1, 2, 3):
            taps_copy(n, here, here, device(axis, off(axis, by)))

    def taps_last(axis, value):
        here = taps_z.at[core * 4 + at[axis]]
        here[...] = value
        for by in (0, 1, 2, 3):
            if by:
                taps_copy(2, here, here, device(axis, off(axis, by)))
            taps_copy(2, here, here, device(axis, off(axis, by), other))

    def sum_4(ref, n):
        return (ref[n] + ref[n + 1]) + (ref[n + 2] + ref[n + 3])

    def taps_sum(n):
        whole(taps_a.at[n, pl.ds(0, 3)], taps_recv.at[n])
        return sum_4(taps_a.at[n], 0)

    def taps_end():
        whole(taps_z.at[pl.ds(0, 7)], taps_recv.at[2])
        halves = sum_4(taps_z, 0), sum_4(taps_z, 4)
        for t in range(KW):
            block = halves[0][t] if t < 5 else halves[1][t - 4]
            for n in range(D // HD):
                dk_out[t : t + 1, n * HD : (n + 1) * HD] = block[n : n + 1, :]

    swap_half(OUT).wait_recv()
    swap_att.wait_recv()
    turn_in(att2, att_t)
    product(att_t, OUT * HALF, HALF)
    rings[0][0].begin()

    def d_key(j):
        two = pl.ds(mult(j * 2 * BF, 2 * BF), 2 * BF)
        dk_s[pl.ds(j * 2, 2)] = (dot(ds_ref[two, :], q_aug[:, pl.ds(0, HD)]) * inv_root).astype(BF16).reshape(2, BF, HD)

        @pl.when(j > 0)
        def _():
            remote(BK, j * 2).start()

        remote(BK, j * 2 + 1).start()

    lax.fori_loop(0, NC // 2, lambda j, c: (d_key(j), c)[1], 0)
    local(BK).start()

    def taps(n):
        cols = pl.ds(mult(n * BF, BF), BF)
        sub = dot(att2[mine, :], wout_vm[:, cols]).astype(BF16).astype(F32)
        for t in range(KW):
            total = jnp.sum(sub * gp[pl.ds(12 - t, BF), cols], axis=0, keepdims=True)
            taps_c[t, pl.ds(2 * n, 1), :] = total[:, :HD]
            taps_c[t, pl.ds(2 * n + 1, 1), :] = total[:, HD:]

    def back(t, n):
        arrived(t)
        swap_half(n).start()
        own_half(n)

    def weight(n):
        swap_half(n).wait_recv()
        product(li_t, n * HALF, HALF)

    def d_input(n, carry):
        cols = pl.ds(mult(n * BF, BF), BF)
        din_vm[:, cols] = dot_nt(dqkv[...], wqkv_vm[cols, :]).astype(BF16)
        return carry

    back(BV, VAL)
    rings[0][0].relay()
    lax.fori_loop(0, D // BF, lambda n, c: (taps(n), c)[1], 0)
    swap_taps.start()
    weight(VAL)
    swap_taps.wait_recv()
    taps_on(0, "x", taps_c[pl.ds(core * 4, 5)] + taps_p[...])
    rings[1][0].begin()
    back(BQ, QUE)
    get_wq.wait()
    weight(QUE)
    rings[2][0].begin()
    rings[3][0].begin()
    back(BK, KEY)
    taps_on(1, "y", taps_sum(0))
    lax.fori_loop(0, 2, d_input, 0)
    weight(KEY)
    rings[4][0].begin()
    rings[5][0].begin()
    rings[2][0].relay()
    rings[3][0].relay()
    rings[1][0].relay()
    taps_last("z", taps_sum(1))
    rings[4][0].relay()
    rings[5][0].relay()
    on(0, 0)
    lax.fori_loop(2, 4, d_input, 0)
    put_din = pltpu.make_async_copy(din_vm, din_hbm, local_sem.at[4])
    put_din.start()
    on(2, 0)
    on(3, 0)
    on(1, 0)
    on(4, 0)
    on(5, 0)
    on(0, 1)
    taps_end()
    puts = [
        pltpu.make_async_copy(a, b, local_sem.at[n])
        for a, b, n in ((dk_out, dk_hbm, 6), (dwo_out, dwo_hbm, 7), (dwq_out, dwq_hbm, 8))
    ]
    puts[0].start()
    for p in (2, 3, 1, 4, 5):
        on(p, 1)
    whole(att2.at[pl.ds(0, 32), :], halo_send)
    for t in range(8):
        drain(send_sem.at[t], (NC - 1) * BF * HD * 2)
    for swap in (swap_li, swap_att, swap_taps, *(swap_half(n) for n in range(4))):
        swap.wait_send()
    for n in (0, 1):
        whole(taps_a.at[n, pl.ds(0, 3)], taps_send.at[n])
    whole(taps_z.at[pl.ds(0, 7)], taps_send.at[2])
    for r in rings:
        r[0].sent()
        r[1].sent()
    rings[0][2].end()
    puts[1].start()
    for p in range(1, NP):
        rings[p][2].end()
    puts[2].start()
    for r in rings:
        r[2].sent()
    put_din.wait()
    for put in puts:
        put.wait()


def collect_kernel(*refs):
    for a, b in zip(refs[:4], refs[4:]):
        b[...] = a[...]


def backward(lengths, li, q, k, v, g, conv, wout, wqkv):
    def vm(shape, dtype=BF16):
        return pltpu.VMEM(shape, dtype)

    buffers = []
    for _, width, order in PARTS:
        leads = []
        for stage in range(3):
            sizes = (("zl", 2), ("y", 4), ("zh", 2), ("x", 4))
            leads.append([n for axis, n in sizes if axis[0] not in order[: stage + 1]])
        halves = [(*leads[0], 16, width // 2)] * 2
        buffers += [vm(shape) for shape in (*halves, (2, *leads[0], 16, width))]
        buffers.append(vm((3, *leads[1], 16, width)))
        buffers.append(vm((*leads[1], 2, 8, width), F32))
        buffers.append(vm((7, 8, width), F32))
    dma = pltpu.SemaphoreType.DMA
    outs = (
        jax.ShapeDtypeStruct((BF, D), BF16),
        jax.ShapeDtypeStruct((8, 3 * D), F32),
        jax.ShapeDtypeStruct((8, D), F32),
        jax.ShapeDtypeStruct((KW, D), F32),
    )
    results = pl.pallas_call(
        backward_kernel,
        out_shape=outs,
        in_specs=[pl.BlockSpec(memory_space=pltpu.SMEM)] + [ANY] * 8,
        out_specs=(ANY,) * 4,
        scratch_shapes=[
            vm((T, 2 * HD)), vm((T, 2 * HD)), vm((T, 2 * HD)), vm((T, HD)), vm((T, 2 * HD)),
            vm((HD, T)), vm((HD + 16, T)), vm((T, BF), F32), vm((T, T)), vm((T, T)),
            vm((NC, BF, HD)), vm((NC, BF, HD), F32), vm((NC, BF, HD)), vm((NC, BF, HD)),
            vm((NC, BF, HD)), vm((NC, BF, HD)), vm((BF, 3 * D)), vm((BF, D)),
            vm((BF, D)), vm((BF + 16, D), F32), vm((BF, D)), vm((16, D)), vm((16, D)),
            vm((D, D)), vm((D, 3 * D)),
            vm((2 * BF, D)), vm((2 * BF, D)), vm((2 * BF, CW)), vm((D, 2 * BF)), vm((D, 2 * BF)),
            vm((2, 4, 2, 4, 16, CW)),
            vm((KW, 8, HD), F32), vm((5, 8, HD), F32), vm((2, 4, 5, 8, HD), F32), vm((8, 5, 8, HD), F32),
            vm((KW, D), F32), vm((8, 3 * D), F32), vm((8, D), F32), vm((KW, D), F32), *buffers,
            dma((8,)), dma((8,)), dma((NC,)), dma(()), dma((2,)), dma((9,)), dma((7,)), dma((7,)),
            dma((NP,)), dma((NP * 3,)), dma((NP,)), dma((NP,)), dma((NP,)), dma((NP,)),
            dma((3,)), dma((3,)),
        ],
        compiler_params=pltpu.CompilerParams(
            collective_id=0, has_side_effects=True, vmem_limit_bytes=60 * 1024 * 1024
        ),
    )(lengths, li, q, k, v, g, conv, wout, wqkv)
    return pl.pallas_call(
        collect_kernel,
        out_shape=outs,
        in_specs=[VM] * 4,
        out_specs=(VM,) * 4,
    )(*results)


def shards(layer_in, queries, keys, values, lengths, w_qkv, w_out, conv_kernel, grad_out):
    d_input, d_wqkv, d_wout, d_kernel = backward(
        lengths, layer_in[0], queries[0], keys[0], values[0], grad_out[0], conv_kernel, w_out, w_qkv
    )
    return d_input[None], d_wqkv, d_wout, d_kernel


def solution(mesh):
    frames = P("rec", "ctx", None)
    in_specs = (frames, frames, frames, frames, P("rec"), P(), P(), P(), frames)
    out_specs = (frames, P(("ctx", "rec"), None), P(("ctx", "rec"), None), P())
    return jax.shard_map(
        shards, mesh=mesh, in_specs=in_specs, out_specs=out_specs, check_vma=False
    )
```

```python
import math

import jax
import jax.numpy as jnp
from jax import lax
from jax.experimental import pallas as pl
from jax.experimental.pallas import tpu as pltpu
from jax.sharding import PartitionSpec as P

HD = 128
KW = 9
NC = 8
BF = 256
T = NC * BF
D = 1024
F32 = jnp.float32
BF16 = jnp.bfloat16
MESH = pl.DeviceIdType.MESH
KB = 512
NEG = -1e30
NT = (((1,), (1,)), ((), ()))
ANY = pl.BlockSpec(memory_space=pl.ANY)
VM = pl.BlockSpec(memory_space=pltpu.VMEM)

TQ, TK, TV, TD, BA, BQ, BK, BV = range(8)


def mult(value, of):
    return pl.multiple_of(value, of)


def dot(a, b):
    return jnp.dot(a, b, preferred_element_type=F32)


def dot_nt(a, b):
    return lax.dot_general(a, b, NT, preferred_element_type=F32)


HALF = 512
CW = 4 * HALF
OUT, VAL, QUE, KEY = range(4)
PARTS = (
    (0, 512, ("x", "y", "z")),
    (512, 512, ("x", "z", "y")),
    (1024, 256, ("y", "x", "z")),
    (1280, 256, ("z", "x", "y")),
    (1536, 256, ("x", "y", "z")),
    (1792, 128, ("y", "z", "x")),
    (1920, 128, ("z", "y", "x")),
)
RINGS = (0, 1, 2, 3)
NP = len(PARTS)


def backward_kernel(
    len_ref, li_ref, q_ref, k_ref, v_ref, g_ref, conv_ref, wout_ref, wqkv_ref,
    din_vm, dwq_out, dwo_out, dk_out,
    q_aug, k_aug, v_aug, do_in, do_aug, k_t, v_t, s_ref, e_ref, ds_ref,
    att_s, linv_s, dq_s, dk_s, dv_s, dat_s, dqkv,
    g_vm, gp, dsub, halo_lo, halo_hi, wout_vm, wqkv_vm,
    li2, att2, r2, li_t, att_t, grads, taps_c, taps_p, taps_a, taps_z, conv_vm, *rest,
):
    bufs = rest[: NP * 6]
    (send_sem, recv_sem, q_recv, halo_send, halo_recv, local_sem, core_send, core_recv,
     ring_send, ring_recv, step_send, step_recv, last_send, last_recv,
     taps_send, taps_recv) = rest[NP * 6 :]
    me = lax.axis_index("ctx")
    rec = lax.axis_index("rec")
    z, y = lax.div(me, 4), lax.rem(me, 4)
    inv_root = 1.0 / math.sqrt(HD)
    c_exp = math.log2(math.e) / math.sqrt(HD)

    def peer(d):
        return lax.rem(z + lax.div(d, 4), 2) * 4 + lax.rem(y + lax.rem(d, 4), 4)

    def origin(d):
        return lax.rem(z + 2 - lax.div(d, 4), 2) * 4 + lax.rem(y + 4 - lax.rem(d, 4), 4)

    def head_cols(h):
        return pl.ds(mult(h * HD, HD), HD)

    def slot(d):
        return pl.ds(mult(d * BF, BF), BF)

    fwd_src = {TQ: q_ref, TK: k_ref, TV: v_ref}
    fwd_dst = {TQ: q_aug, TK: k_aug, TV: v_aug, TD: do_in}
    back_src = {BA: att_s, BQ: dq_s, BK: dk_s, BV: dv_s}
    back_base = {BQ: 0, BK: D, BV: 2 * D}

    def ends(t, d):
        if t <= TD:
            p = peer(d)
            src = dat_s.at[d] if t == TD else fwd_src[t].at[:, head_cols(p)]
            dst = fwd_dst[t].at[slot(d), pl.ds(0, HD)]
        else:
            p = origin(d)
            src = back_src[t].at[d]
            if t == BA:
                dst = att2.at[pl.ds(0, BF), head_cols(me)]
            else:
                dst = dqkv.at[:, pl.ds(mult(back_base[t] + me * HD, HD), HD)]
        return p, src, dst

    def remote(t, d):
        p, src, dst = ends(t, d)
        return pltpu.make_async_remote_copy(
            src_ref=src, dst_ref=dst, send_sem=send_sem.at[t],
            recv_sem=q_recv.at[d] if t == TQ else recv_sem.at[t],
            device_id=(p, rec), device_id_type=MESH,
        )

    def local(t):
        _, src, dst = ends(t, 0)
        return pltpu.make_async_copy(src, dst, q_recv.at[0] if t == TQ else recv_sem.at[t])

    def whole(ref, sem):
        pltpu.make_async_copy(ref, ref, sem).wait()

    def drain(sem, count):
        whole(s_ref.at[pl.ds(0, count // (4 * BF)), :], sem)

    def arrived(t):
        if t <= TD:
            whole(fwd_dst[t].at[:, pl.ds(0, HD)], recv_sem.at[t])
        elif t == BA:
            whole(att2.at[pl.ds(0, BF), :], recv_sem.at[t])
        else:
            whole(dqkv.at[:, pl.ds(back_base[t], D)], recv_sem.at[t])

    def each_peer(body):
        def step(d, carry):
            body(d)
            return carry

        lax.fori_loop(1, NC, step, 0)

    def each_slot(body):
        def step(d, carry):
            body(d)
            return carry

        lax.fori_loop(0, NC, step, 0)

    get_g = pltpu.make_async_copy(g_ref, g_vm, local_sem.at[0])
    get_w = pltpu.make_async_copy(wout_ref, wout_vm, local_sem.at[1])
    get_g.start()
    get_w.start()
    for t in (TK, TQ, TV):
        local(t).start()
    mine, theirs = pl.ds(0, BF), pl.ds(BF, BF)
    get_li = pltpu.make_async_copy(li_ref, li2.at[mine, :], local_sem.at[2])
    get_li.start()
    get_wq = pltpu.make_async_copy(wqkv_ref, wqkv_vm, local_sem.at[3])
    get_conv = pltpu.make_async_copy(conv_ref, conv_vm, local_sem.at[5])
    get_conv.start()

    core = lax.rem(rec, 2)
    other = 1 - core
    at = {"x": lax.rem(lax.div(rec, 2), 4), "y": y, "z": lax.div(rec, 8) * 2 + z}

    def device(moved, to, on_core=core):
        p = {**at, **({moved: to} if moved else {})}
        return (
            lax.rem(p["z"], 2) * 4 + p["y"],
            lax.div(p["z"], 2) * 8 + p["x"] * 2 + on_core,
        )

    def off(axis, by):
        return lax.rem(at[axis] + by, 4)

    partner = device(None, None, other)
    far = lax.rem(lax.div(rec, 8) + 1, 2)
    greet = [partner] + [device("x", off("x", by)) for by in (1, 2, 3)]
    greet += [device("z", far * 2 + zl) for zl in (0, 1)]
    greet += [device(a, off(a, by), other) for a in "xyz" for by in (1, 2, 3)]

    barrier = pltpu.get_barrier_semaphore()
    each_peer(
        lambda d: pl.semaphore_signal(barrier, inc=1, device_id=(peer(d), rec), device_id_type=MESH)
    )
    for who in greet:
        pl.semaphore_signal(barrier, inc=1, device_id=who, device_id_type=MESH)
    pl.semaphore_wait(barrier, NC - 1 + len(greet))

    right, left = lax.rem(me + 1, NC), lax.rem(me + NC - 1, NC)
    to_right = pltpu.make_async_remote_copy(
        src_ref=g_ref.at[pl.ds(BF - 16, 16), :], dst_ref=halo_lo, send_sem=halo_send,
        recv_sem=halo_recv.at[0], device_id=(right, rec), device_id_type=MESH,
    )
    to_left = pltpu.make_async_remote_copy(
        src_ref=g_ref.at[pl.ds(0, 16), :], dst_ref=halo_hi, send_sem=halo_send,
        recv_sem=halo_recv.at[1], device_id=(left, rec), device_id_type=MESH,
    )
    to_right.start()
    to_left.start()
    for t in (TK, TQ, TV):
        each_peer(lambda d: remote(t, d).start())

    def to_partner(n, src, dst):
        return pltpu.make_async_remote_copy(
            src_ref=src, dst_ref=dst, send_sem=core_send.at[n], recv_sem=core_recv.at[n],
            device_id=partner, device_id_type=MESH,
        )

    def half(ref, base, c):
        return ref.at[:, pl.ds(mult(base + c * HALF, HALF), HALF)]

    group = {OUT: (dsub, 0), VAL: (dqkv, 2 * D), QUE: (dqkv, 0), KEY: (dqkv, D)}

    def swap_half(n):
        ref, base = group[n]
        return to_partner(n, half(ref, base, other), r2.at[theirs, pl.ds(n * HALF, HALF)])

    def own_half(n):
        ref, base = group[n]
        r2[mine, pl.ds(n * HALF, HALF)] = half(ref, base, core)[...]

    swap_li = to_partner(4, li_ref, li2.at[theirs, :])
    swap_att = to_partner(5, att2.at[mine, :], att2.at[theirs, :])
    swap_taps = to_partner(6, taps_c.at[pl.ds(other * 4, 5)], taps_p)
    swap_li.start()

    length = len_ref[0]
    lane = lax.broadcasted_iota(jnp.int32, (BF, HD), 1)
    row = lax.broadcasted_iota(jnp.int32, (BF, HD), 0)

    def extra(d):
        masked = (lane == 0) & (row + origin(d) * BF >= length)
        k_aug[slot(d), pl.ds(HD, HD)] = jnp.where(masked, NEG, 0.0).astype(BF16)
        q_aug[slot(d), pl.ds(HD, HD)] = jnp.where(lane == 0, 1.0, 0.0).astype(BF16)
        v_aug[slot(d), pl.ds(HD, HD)] = jnp.where(lane < 2, 1.0, 0.0).astype(BF16)

    each_slot(extra)
    first = lax.broadcasted_iota(jnp.int32, (16, T), 0) == 0
    v_t[pl.ds(HD, 16), :] = jnp.where(first, 1.0, 0.0).astype(BF16)

    get_g.wait()
    get_conv.wait()
    gp[pl.ds(8, BF), :] = g_vm[...].astype(F32)
    to_right.wait_recv()
    to_left.wait_recv()
    low = halo_lo[...].astype(F32)[8:16, :]
    gp[pl.ds(0, 8), :] = jnp.where(me > 0, low, 0.0)
    high = halo_hi[...].astype(F32)[0:8, :]
    gp[pl.ds(8 + BF, 8), :] = jnp.where(me < NC - 1, high, 0.0)

    def conv_grad(n):
        cols = pl.ds(mult(n * HD, HD), HD)
        total = gp[pl.ds(8, BF), cols]
        for t in range(KW):
            total = total + conv_vm[pl.ds(t, 1), cols] * gp[pl.ds(12 - t, BF), cols]
        dsub[:, cols] = total.astype(BF16)

    each_slot(conv_grad)
    swap_half(OUT).start()
    own_half(OUT)
    get_wq.start()

    get_w.wait()

    def datt(d):
        rows = pl.ds(mult(peer(d) * HD, HD), HD)
        dat_s[d] = dot_nt(dsub[...], wout_vm[rows, :]).astype(BF16)

        @pl.when(d > 0)
        def _():
            remote(TD, d).start()

    each_slot(datt)
    local(TD).start()

    def turn_in(src, dst):
        def step(n, carry):
            cols = pl.ds(mult(n * BF, BF), BF)
            dst[cols, :] = src[:, cols].T
            return carry

        lax.fori_loop(0, D // BF, step, 0)

    get_li.wait()
    swap_li.wait_recv()
    turn_in(li2, li_t)

    arrived(TK)
    local(TQ).wait()

    def scores(d):
        @pl.when(d > 0)
        def _():
            remote(TQ, d).wait_recv()

        qd = q_aug[slot(d), :]
        top = None
        for b in range(T // KB):
            rows = pl.ds(b * KB, KB)
            s = dot_nt(k_aug[rows, :], qd)
            s_ref[rows, :] = s
            m = jnp.max(s, axis=0, keepdims=True)
            top = m if top is None else jnp.maximum(top, m)
        for b in range(T // KB):
            rows = pl.ds(b * KB, KB)
            e_ref[rows, slot(d)] = jnp.exp2((s_ref[rows, :] - top) * c_exp).astype(BF16)

    each_slot(scores)
    arrived(TV)

    def turn(d):
        k_t[:, slot(d)] = k_aug[slot(d), pl.ds(0, HD)].T
        v_t[pl.ds(0, HD), slot(d)] = v_aug[slot(d), pl.ds(0, HD)].T

    each_slot(turn)

    def attend(d):
        acc = dot(v_t[...], e_ref[:, slot(d)])
        inv = 1.0 / acc[HD : HD + 1, :]
        att_s[d] = (acc[:HD, :] * inv).T.astype(BF16)
        linv_s[d] = jnp.broadcast_to(inv, (HD, BF)).T

        @pl.when(d > 0)
        def _():
            remote(BA, d).start()

    each_slot(attend)
    local(BA).start()

    arrived(TD)

    def backward_in(d):
        do = (do_in[slot(d), :].astype(F32) * linv_s[d]).astype(BF16)
        delta = -jnp.sum(do.astype(F32) * att_s[d].astype(F32), axis=1, keepdims=True)
        hi = delta.astype(BF16).astype(F32)
        do_aug[slot(d), pl.ds(0, HD)] = do
        do_aug[slot(d), pl.ds(HD, HD)] = jnp.where(
            lane == 0, hi, jnp.where(lane == 1, delta - hi, 0.0)
        ).astype(BF16)

    each_slot(backward_in)

    def d_value(j):
        two = pl.ds(mult(j * 2 * BF, 2 * BF), 2 * BF)
        dv_s[pl.ds(j * 2, 2)] = dot(e_ref[two, :], do_aug[:, pl.ds(0, HD)]).astype(BF16).reshape(2, BF, HD)

        @pl.when(j > 0)
        def _():
            remote(BV, j * 2).start()

        remote(BV, j * 2 + 1).start()

    lax.fori_loop(0, NC // 2, lambda j, c: (d_value(j), c)[1], 0)
    local(BV).start()

    def d_query(d):
        dod = do_aug[slot(d), :]
        acc = jnp.zeros((HD, BF), F32)
        for b in range(T // KB):
            rows = pl.ds(b * KB, KB)
            dp = dot_nt(v_aug[rows, :], dod)
            ds = (e_ref[rows, slot(d)].astype(F32) * dp).astype(BF16)
            ds_ref[rows, slot(d)] = ds
            acc = acc + dot(k_t[:, rows], ds)
        dq_s[d] = (acc * inv_root).T.astype(BF16)

        @pl.when(d > 0)
        def _():
            remote(BQ, d).start()

    def product(lhs, start, width):
        def step(zl, carry):
            rows = pl.ds(mult(zl * HALF, HALF), HALF)
            g = dot(lhs[rows, :], r2[:, pl.ds(start, width)]).astype(BF16)
            grads[zl, :, :, :, :, pl.ds(start, width)] = g.reshape(4, 2, 4, 16, width)
            return carry

        lax.fori_loop(0, 2, step, 0)

    def region(fixed, start, width):
        zl = zh = slice(None)
        if "z" in fixed:
            zl, zh = lax.rem(fixed["z"], 2), lax.div(fixed["z"], 2)
        return grads.at[
            zl, fixed.get("y", slice(None)), zh, fixed.get("x", slice(None)), :, pl.ds(start, width)
        ]

    class Stage:
        def __init__(self, part, stage):
            self.start, self.width, order = PARTS[part]
            self.part = part
            self.axis = order[stage]
            self.fixed = {a: at[a] for a in order[:stage]}
            self.stage = stage

        def piece(self, by, start=0, width=None):
            width = self.width if width is None else width
            fixed = {**self.fixed, self.axis: off(self.axis, by)}
            return region(fixed, self.start + start, width)

        def copy(self, src, dst, by, recv):
            return pltpu.make_async_remote_copy(
                src_ref=src, dst_ref=dst, send_sem=self.send, recv_sem=recv,
                device_id=device(self.axis, off(self.axis, by)), device_id_type=MESH,
            )

        def keep(self, total):
            if self.stage == 0:
                self.piece(0)[...] = total.astype(BF16)
            else:
                pair = bufs[self.part * 6 + 4]
                for c in (0, 1):
                    rows = total[..., c * 8 : c * 8 + 8, :]
                    if self.width > HD:
                        h = self.width // 2
                        rows = jnp.concatenate([rows[..., :h], rows[..., h:]], axis=-2)
                    pair[..., c, :, :] = rows.astype(pair.dtype)

        def sent(self):
            whole(self.buf, self.send)

    class Ring(Stage):
        def __init__(self, part):
            super().__init__(part, 0)
            self.ra, self.rb, self.ends = bufs[part * 6 : part * 6 + 3]
            h = self.width // 2
            lead = (slice(None),) * (len(self.ra.shape) - 1)
            low_a, low_b = (0, *lead, pl.ds(0, h)), (0, *lead, pl.ds(h, h))
            high_a, high_b = (1, *lead, pl.ds(0, h)), (1, *lead, pl.ds(h, h))
            self.send = ring_send.at[part]
            recv = [ring_recv.at[part * 3 + n] for n in range(3)]
            self.copies = [
                self.copy(self.piece(2, 0, h), self.ra, 1, recv[0]),
                self.copy(self.piece(2, h, h), self.rb, 3, recv[1]),
                self.copy(self.piece(1, h, h), self.ends.at[low_b], 1, recv[2]),
                self.copy(self.piece(3, 0, h), self.ends.at[high_a], 3, recv[2]),
                self.copy(self.piece(1, 0, h), self.ends.at[low_a], 1, recv[2]),
                self.copy(self.piece(3, h, h), self.ends.at[high_b], 3, recv[2]),
            ]
            self.recv = recv[2]

        def begin(self):
            for c in self.copies[:4]:
                c.start()

        def sent(self):
            drain(self.send, 3 * BF * self.width * 2)

        def relay(self):
            h = self.width // 2
            for n, by, buf, start in ((0, 1, self.ra, 0), (1, 3, self.rb, h)):
                self.copies[n].wait_recv()
                here = self.piece(by, start, h)
                here[...] = (here[...].astype(F32) + buf[...].astype(F32)).astype(BF16)
                self.copies[4 + n].start()

        def end(self):
            whole(self.ends, self.recv)
            here = self.piece(0)[...].astype(F32)
            self.keep(here + (self.ends[0].astype(F32) + self.ends[1].astype(F32)))

    class Direct(Stage):
        def __init__(self, part, stage):
            super().__init__(part, stage)
            self.buf = bufs[part * 6 + (3 if stage else 2)]
            n = part if stage else NP + part
            self.send, self.recv = step_send.at[n], step_recv.at[n]
            self.copies = [
                self.copy(self.piece(by), self.buf.at[by - 1], by, self.recv) for by in (1, 2, 3)
            ]

        def begin(self):
            for c in self.copies:
                c.start()

        def end(self):
            whole(self.buf, self.recv)
            here = self.piece(0)[...].astype(F32)
            b = [self.buf[n].astype(F32) for n in range(3)]
            self.keep((here + b[0]) + (b[1] + b[2]))

    class Last(Stage):
        def __init__(self, part):
            super().__init__(part, 2)
            self.pair, self.buf = bufs[part * 6 + 4 : part * 6 + 6]
            self.send, self.recv = last_send.at[part], last_recv.at[part]
            self.copies = []
            for n, (turned, by) in enumerate((t, b) for t in (0, 1) for b in range(4) if t + b):
                to = lax.rem(core + turned, 2)
                who = device(self.axis, off(self.axis, by), to)
                self.copies.append(
                    pltpu.make_async_remote_copy(
                        src_ref=self.rows(by, to), dst_ref=self.buf.at[n],
                        send_sem=self.send, recv_sem=self.recv,
                        device_id=who, device_id_type=MESH,
                    )
                )

        def rows(self, by, to):
            chip = off(self.axis, by)
            if self.axis == "z":
                return self.pair.at[lax.rem(chip, 2), lax.div(chip, 2), to]
            return self.pair.at[chip, to]

        def begin(self):
            for c in self.copies:
                c.start()

        def end(self):
            whole(self.buf, self.recv)
            b = [self.buf[n].astype(F32) for n in range(7)]
            here = self.rows(0, core)[...].astype(F32)
            n, inside = divmod(self.start, HALF)
            out, base = ((dwo_out, 0), (dwq_out, 2 * D), (dwq_out, 0), (dwq_out, D))[n]
            for who, block in (
                (core, (here + b[0]) + (b[1] + b[2])),
                (other, (b[3] + b[4]) + (b[5] + b[6])),
            ):
                first = base + who * HALF + inside
                if self.width > HD:
                    h = self.width // 2
                    out[:, pl.ds(mult(first, HD), h)] = block[:8]
                    out[:, pl.ds(mult(first + h, HD), h)] = block[8:]
                else:
                    out[:, pl.ds(mult(first, HD), HD)] = block

    rings = [
        (Ring(p) if p in RINGS else Direct(p, 0), Direct(p, 1), Last(p)) for p in range(NP)
    ]

    def on(p, stage):
        rings[p][stage].end()
        rings[p][stage + 1].begin()

    def taps_copy(n, src, dst, who):
        pltpu.make_async_remote_copy(
            src_ref=src, dst_ref=dst, send_sem=taps_send.at[n], recv_sem=taps_recv.at[n],
            device_id=who, device_id_type=MESH,
        ).start()

    def taps_on(n, axis, value):
        here = taps_a.at[n, at[axis]]
        here[...] = value
        for by in (1, 2, 3):
            taps_copy(n, here, here, device(axis, off(axis, by)))

    def taps_last(axis, value):
        here = taps_z.at[core * 4 + at[axis]]
        here[...] = value
        for by in (0, 1, 2, 3):
            if by:
                taps_copy(2, here, here, device(axis, off(axis, by)))
            taps_copy(2, here, here, device(axis, off(axis, by), other))

    def sum_4(ref, n):
        return (ref[n] + ref[n + 1]) + (ref[n + 2] + ref[n + 3])

    def taps_sum(n):
        whole(taps_a.at[n, pl.ds(0, 3)], taps_recv.at[n])
        return sum_4(taps_a.at[n], 0)

    def taps_end():
        whole(taps_z.at[pl.ds(0, 7)], taps_recv.at[2])
        halves = sum_4(taps_z, 0), sum_4(taps_z, 4)
        for t in range(KW):
            block = halves[0][t] if t < 5 else halves[1][t - 4]
            for n in range(D // HD):
                dk_out[t : t + 1, n * HD : (n + 1) * HD] = block[n : n + 1, :]

    def taps(n):
        cols = pl.ds(mult(n * BF, BF), BF)
        sub = dot(att2[mine, :], wout_vm[:, cols]).astype(BF16).astype(F32)
        for t in range(KW):
            total = jnp.sum(sub * gp[pl.ds(12 - t, BF), cols], axis=0, keepdims=True)
            taps_c[t, pl.ds(2 * n, 1), :] = total[:, :HD]
            taps_c[t, pl.ds(2 * n + 1, 1), :] = total[:, HD:]

    def back(t, n):
        arrived(t)
        swap_half(n).start()
        own_half(n)

    def weight(n):
        swap_half(n).wait_recv()
        product(li_t, n * HALF, HALF)

    def d_input(n, carry):
        cols = pl.ds(mult(n * BF, BF), BF)
        din_vm[:, cols] = dot_nt(dqkv[...], wqkv_vm[cols, :]).astype(BF16)
        return carry

    lax.fori_loop(0, 3, lambda d, c: (d_query(d), c)[1], 0)
    arrived(BA)
    swap_att.start()
    lax.fori_loop(3, 5, lambda d, c: (d_query(d), c)[1], 0)

    swap_half(OUT).wait_recv()
    swap_att.wait_recv()
    turn_in(att2, att_t)
    product(att_t, OUT * HALF, HALF)
    rings[0][0].begin()
    lax.fori_loop(0, D // BF, lambda n, c: (taps(n), c)[1], 0)
    swap_taps.start()
    lax.fori_loop(5, NC, lambda d, c: (d_query(d), c)[1], 0)
    local(BQ).start()
    back(BV, VAL)
    rings[0][0].relay()
    swap_taps.wait_recv()
    taps_on(0, "x", taps_c[pl.ds(core * 4, 5)] + taps_p[...])

    def d_key(j):
        two = pl.ds(mult(j * 2 * BF, 2 * BF), 2 * BF)
        dk_s[pl.ds(j * 2, 2)] = (dot(ds_ref[two, :], q_aug[:, pl.ds(0, HD)]) * inv_root).astype(BF16).reshape(2, BF, HD)

        @pl.when(j > 0)
        def _():
            remote(BK, j * 2).start()

        remote(BK, j * 2 + 1).start()

    lax.fori_loop(0, 2, lambda j, c: (d_key(j), c)[1], 0)
    weight(VAL)
    rings[1][0].begin()
    lax.fori_loop(2, NC // 2, lambda j, c: (d_key(j), c)[1], 0)
    local(BK).start()
    back(BQ, QUE)
    get_wq.wait()
    weight(QUE)
    rings[2][0].begin()
    rings[3][0].begin()
    rings[1][0].relay()
    taps_on(1, "y", taps_sum(0))
    back(BK, KEY)
    lax.fori_loop(0, 2, d_input, 0)
    weight(KEY)
    for p in (5, 6, 4):
        rings[p][0].begin()
    rings[2][0].relay()
    rings[3][0].relay()
    taps_last("z", taps_sum(1))
    on(0, 0)
    lax.fori_loop(2, 4, d_input, 0)
    on(1, 0)
    on(5, 0)
    on(6, 0)
    on(2, 0)
    on(3, 0)
    on(4, 0)
    for p in (0, 1, 5, 6, 2, 3, 4):
        on(p, 1)
    taps_end()
    whole(att2.at[pl.ds(0, 32), :], halo_send)
    for t in range(8):
        drain(send_sem.at[t], (NC - 1) * BF * HD * 2)
    for swap in (swap_li, swap_att, swap_taps, *(swap_half(n) for n in range(4))):
        swap.wait_send()
    for n in (0, 1):
        whole(taps_a.at[n, pl.ds(0, 3)], taps_send.at[n])
    whole(taps_z.at[pl.ds(0, 7)], taps_send.at[2])
    for r in rings:
        r[0].sent()
        r[1].sent()
    for p in (0, 1, 5, 6, 2, 3, 4):
        rings[p][2].end()
    for r in rings:
        r[2].sent()


def collect_kernel(*refs):
    ins, outs, sems = refs[:4], refs[4:8], refs[8]
    copies = [pltpu.make_async_copy(a, b, sems.at[n]) for n, (a, b) in enumerate(zip(ins, outs))]
    for c in copies:
        c.start()
    for c in copies:
        c.wait()


def backward(lengths, li, q, k, v, g, conv, wout, wqkv):
    def vm(shape, dtype=BF16):
        return pltpu.VMEM(shape, dtype)

    buffers = []
    for p, (_, width, order) in enumerate(PARTS):
        leads = []
        for stage in range(3):
            sizes = (("zl", 2), ("y", 4), ("zh", 2), ("x", 4))
            leads.append([n for axis, n in sizes if axis[0] not in order[: stage + 1]])
        halves = [(*leads[0], 16, width // 2)] * 2
        sides = 2 if p in RINGS else 3
        buffers += [vm(shape) for shape in (*halves, (sides, *leads[0], 16, width))]
        buffers.append(vm((3, *leads[1], 16, width)))
        block, kind = ((16, width // 2), BF16) if width > HD else ((8, width), F32)
        buffers.append(vm((*leads[1], 2, *block), kind))
        buffers.append(vm((7, *block), kind))
    dma = pltpu.SemaphoreType.DMA
    outs = (
        jax.ShapeDtypeStruct((BF, D), BF16),
        jax.ShapeDtypeStruct((8, 3 * D), F32),
        jax.ShapeDtypeStruct((8, D), F32),
        jax.ShapeDtypeStruct((KW, D), F32),
    )
    results = pl.pallas_call(
        backward_kernel,
        out_shape=tuple(pltpu.VMEM(o.shape, o.dtype) for o in outs),
        in_specs=[pl.BlockSpec(memory_space=pltpu.SMEM)] + [ANY] * 8,
        out_specs=(VM,) * 4,
        scratch_shapes=[
            vm((T, 2 * HD)), vm((T, 2 * HD)), vm((T, 2 * HD)), vm((T, HD)), vm((T, 2 * HD)),
            vm((HD, T)), vm((HD + 16, T)), vm((T, BF), F32), vm((T, T)), vm((T, T)),
            vm((NC, BF, HD)), vm((NC, BF, HD), F32), vm((NC, BF, HD)), vm((NC, BF, HD)),
            vm((NC, BF, HD)), vm((NC, BF, HD)), vm((BF, 3 * D)),
            vm((BF, D)), vm((BF + 16, D), F32), vm((BF, D)), vm((16, D)), vm((16, D)),
            vm((D, D)), vm((D, 3 * D)),
            vm((2 * BF, D)), vm((2 * BF, D)), vm((2 * BF, CW)), vm((D, 2 * BF)), vm((D, 2 * BF)),
            vm((2, 4, 2, 4, 16, CW)),
            vm((KW, 8, HD), F32), vm((5, 8, HD), F32), vm((2, 4, 5, 8, HD), F32), vm((8, 5, 8, HD), F32),
            vm((KW, D), F32), *buffers,
            dma((8,)), dma((8,)), dma((NC,)), dma(()), dma((2,)), dma((6,)), dma((7,)), dma((7,)),
            dma((NP,)), dma((NP * 3,)), dma((2 * NP,)), dma((2 * NP,)), dma((NP,)), dma((NP,)),
            dma((3,)), dma((3,)),
        ],
        compiler_params=pltpu.CompilerParams(
            collective_id=0, has_side_effects=True, vmem_limit_bytes=60 * 1024 * 1024
        ),
    )(lengths, li, q, k, v, g, conv, wout, wqkv)
    results = [pltpu.with_memory_space_constraint(r, pltpu.VMEM) for r in results]
    return pl.pallas_call(
        collect_kernel,
        out_shape=outs,
        in_specs=[VM] * 4,
        out_specs=(ANY,) * 4,
        scratch_shapes=[dma((4,))],
    )(*results)


def shards(layer_in, queries, keys, values, lengths, w_qkv, w_out, conv_kernel, grad_out):
    d_input, d_wqkv, d_wout, d_kernel = backward(
        lengths, layer_in[0], queries[0], keys[0], values[0], grad_out[0], conv_kernel, w_out, w_qkv
    )
    return d_input[None], d_wqkv, d_wout, d_kernel


def solution(mesh):
    frames = P("rec", "ctx", None)
    in_specs = (frames, frames, frames, frames, P("rec"), P(), P(), P(), frames)
    out_specs = (frames, P(("ctx", "rec"), None), P(("ctx", "rec"), None), P())
    return jax.shard_map(
        shards, mesh=mesh, in_specs=in_specs, out_specs=out_specs, check_vma=False
    )
```

```python
import math

import jax
import jax.numpy as jnp
from jax import lax
from jax.experimental import pallas as pl
from jax.experimental.pallas import tpu as pltpu
from jax.sharding import PartitionSpec as P

HD = 128
KW = 9
NC = 8
BF = 256
T = NC * BF
D = 1024
F32 = jnp.float32
BF16 = jnp.bfloat16
MESH = pl.DeviceIdType.MESH
KB = 512
NEG = -1e30
NT = (((1,), (1,)), ((), ()))
ANY = pl.BlockSpec(memory_space=pl.ANY)
VM = pl.BlockSpec(memory_space=pltpu.VMEM)

TQ, TK, TV, TD, BA, BQ, BK, BV = range(8)


def mult(value, of):
    return pl.multiple_of(value, of)


def dot(a, b):
    return jnp.dot(a, b, preferred_element_type=F32)


def dot_nt(a, b):
    return lax.dot_general(a, b, NT, preferred_element_type=F32)


HALF = 512
CW = 4 * HALF
OUT, VAL, QUE, KEY = range(4)
PARTS = (
    (0, 512, ("x", "y", "z")),
    (512, 512, ("x", "z", "y")),
    (1024, 256, ("y", "x", "z")),
    (1280, 256, ("z", "x", "y")),
    (1536, 128, ("x", "y", "z")),
    (1664, 128, ("y", "x", "z")),
    (1792, 256, ("z", "y", "x")),
)
RINGS = (0, 1, 2, 3)
NP = len(PARTS)


def backward_kernel(
    len_hbm, li_ref, q_ref, k_ref, v_ref, g_ref, conv_ref, wout_ref, wqkv_ref,
    din_vm, dwq_out, dwo_out, dk_out,
    q_aug, k_aug, v_aug, do_in, do_aug, k_t, v_t, s_ref, e_ref, ds_ref,
    att_s, linv_s, dq_s, dk_s, dv_s, dat_s, dqkv,
    g_vm, gp, dsub, halo_lo, halo_hi, wout_vm, wqkv_vm,
    li2, att2, r2, li_t, att_t, grads, taps_c, taps_p, taps_a, taps_z, conv_vm, len_ref, *rest,
):
    bufs = rest[: NP * 6]
    (send_sem, recv_sem, q_recv, halo_send, halo_recv, local_sem, core_send, core_recv,
     ring_send, ring_recv, step_send, step_recv, last_send, last_recv,
     taps_send, taps_recv) = rest[NP * 6 :]
    me = lax.axis_index("ctx")
    rec = lax.axis_index("rec")
    z, y = lax.div(me, 4), lax.rem(me, 4)
    inv_root = 1.0 / math.sqrt(HD)
    c_exp = math.log2(math.e) / math.sqrt(HD)

    def peer(d):
        return lax.rem(z + lax.div(d, 4), 2) * 4 + lax.rem(y + lax.rem(d, 4), 4)

    def origin(d):
        return lax.rem(z + 2 - lax.div(d, 4), 2) * 4 + lax.rem(y + 4 - lax.rem(d, 4), 4)

    def head_cols(h):
        return pl.ds(mult(h * HD, HD), HD)

    def slot(d):
        return pl.ds(mult(d * BF, BF), BF)

    fwd_src = {TQ: q_ref, TK: k_ref, TV: v_ref}
    fwd_dst = {TQ: q_aug, TK: k_aug, TV: v_aug, TD: do_in}
    back_src = {BA: att_s, BQ: dq_s, BK: dk_s, BV: dv_s}
    back_base = {BQ: 0, BK: D, BV: 2 * D}

    def ends(t, d):
        if t <= TD:
            p = peer(d)
            src = dat_s.at[d] if t == TD else fwd_src[t].at[:, head_cols(p)]
            dst = fwd_dst[t].at[slot(d), pl.ds(0, HD)]
        else:
            p = origin(d)
            src = back_src[t].at[d]
            if t == BA:
                dst = att2.at[pl.ds(0, BF), head_cols(me)]
            else:
                dst = dqkv.at[:, pl.ds(mult(back_base[t] + me * HD, HD), HD)]
        return p, src, dst

    def remote(t, d):
        p, src, dst = ends(t, d)
        return pltpu.make_async_remote_copy(
            src_ref=src, dst_ref=dst, send_sem=send_sem,
            recv_sem=q_recv.at[d] if t == TQ else recv_sem.at[t],
            device_id=(p, rec), device_id_type=MESH,
        )

    def local(t):
        _, src, dst = ends(t, 0)
        return pltpu.make_async_copy(src, dst, q_recv.at[0] if t == TQ else recv_sem.at[t])

    def whole(ref, sem):
        pltpu.make_async_copy(ref, ref, sem).wait()

    def drain(sem, count):
        whole(e_ref.at[pl.ds(0, count // (2 * T)), :], sem)

    def arrived(t):
        if t <= TD:
            whole(fwd_dst[t].at[:, pl.ds(0, HD)], recv_sem.at[t])
        elif t == BA:
            whole(att2.at[pl.ds(0, BF), :], recv_sem.at[t])
        else:
            whole(dqkv.at[:, pl.ds(back_base[t], D)], recv_sem.at[t])

    def each_peer(body):
        def step(d, carry):
            body(d)
            return carry

        lax.fori_loop(1, NC, step, 0)

    def each_slot(body):
        def step(d, carry):
            body(d)
            return carry

        lax.fori_loop(0, NC, step, 0)

    get_g = pltpu.make_async_copy(g_ref, g_vm, local_sem.at[0])
    get_w = pltpu.make_async_copy(wout_ref, wout_vm, local_sem.at[1])
    get_g.start()
    get_w.start()
    for t in (TK, TQ, TV):
        local(t).start()
    mine, theirs = pl.ds(0, BF), pl.ds(BF, BF)
    get_li = pltpu.make_async_copy(li_ref, li2.at[mine, :], local_sem.at[2])
    get_li.start()
    get_wq = pltpu.make_async_copy(wqkv_ref, wqkv_vm, local_sem.at[3])
    get_conv = pltpu.make_async_copy(conv_ref, conv_vm, local_sem.at[5])
    get_conv.start()
    get_len = pltpu.make_async_copy(len_hbm, len_ref, local_sem.at[4])
    get_len.start()

    core = lax.rem(rec, 2)
    other = 1 - core
    at = {"x": lax.rem(lax.div(rec, 2), 4), "y": y, "z": lax.div(rec, 8) * 2 + z}

    def device(moved, to, on_core=core):
        p = {**at, **({moved: to} if moved else {})}
        return (
            lax.rem(p["z"], 2) * 4 + p["y"],
            lax.div(p["z"], 2) * 8 + p["x"] * 2 + on_core,
        )

    def off(axis, by):
        return lax.rem(at[axis] + by, 4)

    partner = device(None, None, other)
    far = lax.rem(lax.div(rec, 8) + 1, 2)
    greet = [partner] + [device("x", off("x", by)) for by in (1, 2, 3)]
    greet += [device("z", far * 2 + zl) for zl in (0, 1)]
    greet += [device(a, off(a, by), other) for a in "xyz" for by in (1, 2, 3)]

    barrier = pltpu.get_barrier_semaphore()
    each_peer(
        lambda d: pl.semaphore_signal(barrier, inc=1, device_id=(peer(d), rec), device_id_type=MESH)
    )
    for who in greet:
        pl.semaphore_signal(barrier, inc=1, device_id=who, device_id_type=MESH)
    pl.semaphore_wait(barrier, NC - 1 + len(greet))

    right, left = lax.rem(me + 1, NC), lax.rem(me + NC - 1, NC)
    to_right = pltpu.make_async_remote_copy(
        src_ref=g_ref.at[pl.ds(BF - 16, 16), :], dst_ref=halo_lo, send_sem=halo_send,
        recv_sem=halo_recv.at[0], device_id=(right, rec), device_id_type=MESH,
    )
    to_left = pltpu.make_async_remote_copy(
        src_ref=g_ref.at[pl.ds(0, 16), :], dst_ref=halo_hi, send_sem=halo_send,
        recv_sem=halo_recv.at[1], device_id=(left, rec), device_id_type=MESH,
    )
    to_right.start()
    to_left.start()
    for t in (TK, TQ, TV):
        each_peer(lambda d: remote(t, d).start())

    def to_partner(n, src, dst):
        return pltpu.make_async_remote_copy(
            src_ref=src, dst_ref=dst, send_sem=core_send.at[n // 6], recv_sem=core_recv.at[n],
            device_id=partner, device_id_type=MESH,
        )

    def half(ref, base, c):
        return ref.at[:, pl.ds(mult(base + c * HALF, HALF), HALF)]

    group = {OUT: (dsub, 0), VAL: (dqkv, 2 * D), QUE: (dqkv, 0), KEY: (dqkv, D)}

    def swap_half(n):
        ref, base = group[n]
        return to_partner(n, half(ref, base, other), r2.at[theirs, pl.ds(n * HALF, HALF)])

    def own_half(n):
        ref, base = group[n]
        r2[mine, pl.ds(n * HALF, HALF)] = half(ref, base, core)[...]

    swap_li = to_partner(4, li_ref, li2.at[theirs, :])
    swap_att = to_partner(5, att2.at[mine, :], att2.at[theirs, :])
    swap_taps = to_partner(6, taps_c.at[pl.ds(other * 4, 5)], taps_p)
    swap_li.start()

    get_len.wait()
    length = len_ref[0]
    lane = lax.broadcasted_iota(jnp.int32, (BF, HD), 1)
    row = lax.broadcasted_iota(jnp.int32, (BF, HD), 0)

    def extra(d):
        masked = (lane == 0) & (row + origin(d) * BF >= length)
        k_aug[slot(d), pl.ds(HD, HD)] = jnp.where(masked, NEG, 0.0).astype(BF16)
        q_aug[slot(d), pl.ds(HD, HD)] = jnp.where(lane == 0, 1.0, 0.0).astype(BF16)
        v_aug[slot(d), pl.ds(HD, HD)] = jnp.where(lane < 2, 1.0, 0.0).astype(BF16)

    each_slot(extra)
    first = lax.broadcasted_iota(jnp.int32, (16, T), 0) == 0
    v_t[pl.ds(HD, 16), :] = jnp.where(first, 1.0, 0.0).astype(BF16)

    get_g.wait()
    get_conv.wait()
    gp[pl.ds(8, BF), :] = g_vm[...].astype(F32)
    to_right.wait_recv()
    to_left.wait_recv()
    low = halo_lo[...].astype(F32)[8:16, :]
    gp[pl.ds(0, 8), :] = jnp.where(me > 0, low, 0.0)
    high = halo_hi[...].astype(F32)[0:8, :]
    gp[pl.ds(8 + BF, 8), :] = jnp.where(me < NC - 1, high, 0.0)

    def conv_grad(n):
        cols = pl.ds(mult(n * HD, HD), HD)
        total = gp[pl.ds(8, BF), cols]
        for t in range(KW):
            total = total + conv_vm[pl.ds(t, 1), cols] * gp[pl.ds(12 - t, BF), cols]
        dsub[:, cols] = total.astype(BF16)

    each_slot(conv_grad)
    swap_half(OUT).start()
    own_half(OUT)
    get_wq.start()

    get_w.wait()

    def datt(d):
        rows = pl.ds(mult(peer(d) * HD, HD), HD)
        dat_s[d] = dot_nt(dsub[...], wout_vm[rows, :]).astype(BF16)

        @pl.when(d > 0)
        def _():
            remote(TD, d).start()

    each_slot(datt)
    local(TD).start()

    def turn_in(src, dst):
        def step(n, carry):
            cols = pl.ds(mult(n * BF, BF), BF)
            dst[cols, :] = src[:, cols].T
            return carry

        lax.fori_loop(0, D // BF, step, 0)

    get_li.wait()
    swap_li.wait_recv()
    turn_in(li2, li_t)

    arrived(TK)
    local(TQ).wait()

    def scores(d):
        @pl.when(d > 0)
        def _():
            remote(TQ, d).wait_recv()

        qd = q_aug[slot(d), :]
        top = None
        for b in range(T // KB):
            rows = pl.ds(b * KB, KB)
            s = dot_nt(k_aug[rows, :], qd)
            s_ref[rows, :] = s
            m = jnp.max(s, axis=0, keepdims=True)
            top = m if top is None else jnp.maximum(top, m)
        for b in range(T // KB):
            rows = pl.ds(b * KB, KB)
            e_ref[rows, slot(d)] = jnp.exp2((s_ref[rows, :] - top) * c_exp).astype(BF16)

    each_slot(scores)
    arrived(TV)

    def turn(d):
        k_t[:, slot(d)] = k_aug[slot(d), pl.ds(0, HD)].T
        v_t[pl.ds(0, HD), slot(d)] = v_aug[slot(d), pl.ds(0, HD)].T

    each_slot(turn)

    def attend(d):
        acc = dot(v_t[...], e_ref[:, slot(d)])
        inv = 1.0 / acc[HD : HD + 1, :]
        att_s[d] = (acc[:HD, :] * inv).T.astype(BF16)
        linv_s[d] = jnp.broadcast_to(inv, (HD, BF)).T

        @pl.when(d > 0)
        def _():
            remote(BA, d).start()

    each_slot(attend)
    local(BA).start()

    arrived(TD)

    def backward_in(d):
        do = (do_in[slot(d), :].astype(F32) * linv_s[d]).astype(BF16)
        delta = -jnp.sum(do.astype(F32) * att_s[d].astype(F32), axis=1, keepdims=True)
        hi = delta.astype(BF16).astype(F32)
        do_aug[slot(d), pl.ds(0, HD)] = do
        do_aug[slot(d), pl.ds(HD, HD)] = jnp.where(
            lane == 0, hi, jnp.where(lane == 1, delta - hi, 0.0)
        ).astype(BF16)

    each_slot(backward_in)

    def d_value(j):
        two = pl.ds(mult(j * 2 * BF, 2 * BF), 2 * BF)
        dv_s[pl.ds(j * 2, 2)] = dot(e_ref[two, :], do_aug[:, pl.ds(0, HD)]).astype(BF16).reshape(2, BF, HD)

        @pl.when(j > 0)
        def _():
            remote(BV, j * 2).start()

        remote(BV, j * 2 + 1).start()

    lax.fori_loop(0, NC // 2, lambda j, c: (d_value(j), c)[1], 0)
    local(BV).start()

    def d_query(d):
        dod = do_aug[slot(d), :]
        acc = jnp.zeros((HD, BF), F32)
        for b in range(T // KB):
            rows = pl.ds(b * KB, KB)
            dp = dot_nt(v_aug[rows, :], dod)
            ds = (e_ref[rows, slot(d)].astype(F32) * dp).astype(BF16)
            ds_ref[rows, slot(d)] = ds
            acc = acc + dot(k_t[:, rows], ds)
        dq_s[d] = (acc * inv_root).T.astype(BF16)

        @pl.when(d > 0)
        def _():
            remote(BQ, d).start()

    def product(lhs, start, width):
        def step(zl, carry):
            rows = pl.ds(mult(zl * HALF, HALF), HALF)
            g = dot(lhs[rows, :], r2[:, pl.ds(start, width)]).astype(BF16)
            grads[zl, :, :, :, :, pl.ds(start, width)] = g.reshape(4, 2, 4, 16, width)
            return carry

        lax.fori_loop(0, 2, step, 0)

    def region(fixed, start, width):
        zl = zh = slice(None)
        if "z" in fixed:
            zl, zh = lax.rem(fixed["z"], 2), lax.div(fixed["z"], 2)
        return grads.at[
            zl, fixed.get("y", slice(None)), zh, fixed.get("x", slice(None)), :, pl.ds(start, width)
        ]

    class Stage:
        def __init__(self, part, stage):
            self.start, self.width, order = PARTS[part]
            self.part = part
            self.axis = order[stage]
            self.fixed = {a: at[a] for a in order[:stage]}
            self.stage = stage

        def piece(self, by, start=0, width=None):
            width = self.width if width is None else width
            fixed = {**self.fixed, self.axis: off(self.axis, by)}
            return region(fixed, self.start + start, width)

        def copy(self, src, dst, by, recv):
            return pltpu.make_async_remote_copy(
                src_ref=src, dst_ref=dst, send_sem=self.send, recv_sem=recv,
                device_id=device(self.axis, off(self.axis, by)), device_id_type=MESH,
            )

        def keep(self, total):
            if self.stage == 0:
                self.piece(0)[...] = total.astype(BF16)
            else:
                pair = bufs[self.part * 6 + 4]
                for c in (0, 1):
                    rows = total[..., c * 8 : c * 8 + 8, :]
                    if self.width > HD:
                        h = self.width // 2
                        rows = jnp.concatenate([rows[..., :h], rows[..., h:]], axis=-2)
                    pair[..., c, :, :] = rows.astype(pair.dtype)

    class Ring(Stage):
        def __init__(self, part):
            super().__init__(part, 0)
            self.ra, self.rb, self.ends = bufs[part * 6 : part * 6 + 3]
            h = self.width // 2
            lead = (slice(None),) * (len(self.ra.shape) - 1)
            low_a, low_b = (0, *lead, pl.ds(0, h)), (0, *lead, pl.ds(h, h))
            high_a, high_b = (1, *lead, pl.ds(0, h)), (1, *lead, pl.ds(h, h))
            self.send = ring_send
            recv = [ring_recv.at[part * 3 + n] for n in range(3)]
            self.copies = [
                self.copy(self.piece(2, 0, h), self.ra, 1, recv[0]),
                self.copy(self.piece(2, h, h), self.rb, 3, recv[1]),
                self.copy(self.piece(1, h, h), self.ends.at[low_b], 1, recv[2]),
                self.copy(self.piece(3, 0, h), self.ends.at[high_a], 3, recv[2]),
                self.copy(self.piece(1, 0, h), self.ends.at[low_a], 1, recv[2]),
                self.copy(self.piece(3, h, h), self.ends.at[high_b], 3, recv[2]),
            ]
            self.recv = recv[2]

        def begin(self):
            for c in self.copies[:4]:
                c.start()

        def relay(self):
            h = self.width // 2
            for n, by, buf, start in ((0, 1, self.ra, 0), (1, 3, self.rb, h)):
                self.copies[n].wait_recv()
                here = self.piece(by, start, h)
                here[...] = (here[...].astype(F32) + buf[...].astype(F32)).astype(BF16)
                self.copies[4 + n].start()

        def end(self):
            whole(self.ends, self.recv)
            here = self.piece(0)[...].astype(F32)
            self.keep(here + (self.ends[0].astype(F32) + self.ends[1].astype(F32)))

    class Direct(Stage):
        def __init__(self, part, stage):
            super().__init__(part, stage)
            self.buf = bufs[part * 6 + (3 if stage else 2)]
            n = part if stage else NP + part
            self.send, self.recv = step_send.at[min(stage, 1)], step_recv.at[n]
            self.copies = [
                self.copy(self.piece(by), self.buf.at[by - 1], by, self.recv) for by in (1, 2, 3)
            ]

        def begin(self):
            for c in self.copies:
                c.start()

        def end(self):
            whole(self.buf, self.recv)
            here = self.piece(0)[...].astype(F32)
            b = [self.buf[n].astype(F32) for n in range(3)]
            self.keep((here + b[0]) + (b[1] + b[2]))

    class Last(Stage):
        def __init__(self, part):
            super().__init__(part, 2)
            self.pair, self.buf = bufs[part * 6 + 4 : part * 6 + 6]
            self.send, self.recv = last_send, last_recv.at[part]
            self.copies = []
            for n, (turned, by) in enumerate((t, b) for t in (0, 1) for b in range(4) if t + b):
                to = lax.rem(core + turned, 2)
                who = device(self.axis, off(self.axis, by), to)
                self.copies.append(
                    pltpu.make_async_remote_copy(
                        src_ref=self.rows(by, to), dst_ref=self.buf.at[n],
                        send_sem=self.send, recv_sem=self.recv,
                        device_id=who, device_id_type=MESH,
                    )
                )

        def rows(self, by, to):
            chip = off(self.axis, by)
            if self.axis == "z":
                return self.pair.at[lax.rem(chip, 2), lax.div(chip, 2), to]
            return self.pair.at[chip, to]

        def begin(self):
            for c in self.copies:
                c.start()

        def end(self):
            whole(self.buf, self.recv)
            b = [self.buf[n].astype(F32) for n in range(7)]
            here = self.rows(0, core)[...].astype(F32)
            n, inside = divmod(self.start, HALF)
            out, base = ((dwo_out, 0), (dwq_out, 2 * D), (dwq_out, 0), (dwq_out, D))[n]
            for who, block in (
                (core, (here + b[0]) + (b[1] + b[2])),
                (other, (b[3] + b[4]) + (b[5] + b[6])),
            ):
                first = base + who * HALF + inside
                if self.width > HD:
                    h = self.width // 2
                    out[:, pl.ds(mult(first, HD), h)] = block[:8]
                    out[:, pl.ds(mult(first + h, HD), h)] = block[8:]
                else:
                    out[:, pl.ds(mult(first, HD), HD)] = block

    rings = [
        (Ring(p) if p in RINGS else Direct(p, 0), Direct(p, 1), Last(p)) for p in range(NP)
    ]

    def on(p, stage):
        rings[p][stage].end()
        rings[p][stage + 1].begin()

    def taps_copy(n, src, dst, who):
        pltpu.make_async_remote_copy(
            src_ref=src, dst_ref=dst, send_sem=taps_send.at[n], recv_sem=taps_recv.at[n],
            device_id=who, device_id_type=MESH,
        ).start()

    def taps_on(n, axis, value):
        here = taps_a.at[n, at[axis]]
        here[...] = value
        for by in (1, 2, 3):
            taps_copy(n, here, here, device(axis, off(axis, by)))

    def taps_last(axis, value):
        here = taps_z.at[core * 4 + at[axis]]
        here[...] = value
        for by in (0, 1, 2, 3):
            if by:
                taps_copy(2, here, here, device(axis, off(axis, by)))
            taps_copy(2, here, here, device(axis, off(axis, by), other))

    def sum_4(ref, n):
        return (ref[n] + ref[n + 1]) + (ref[n + 2] + ref[n + 3])

    def taps_sum(n):
        whole(taps_a.at[n, pl.ds(0, 3)], taps_recv.at[n])
        return sum_4(taps_a.at[n], 0)

    def taps_end():
        whole(taps_z.at[pl.ds(0, 7)], taps_recv.at[2])
        halves = sum_4(taps_z, 0), sum_4(taps_z, 4)
        for t in range(KW):
            block = halves[0][t] if t < 5 else halves[1][t - 4]
            for n in range(D // HD):
                dk_out[t : t + 1, n * HD : (n + 1) * HD] = block[n : n + 1, :]

    def taps(n):
        cols = pl.ds(mult(n * BF, BF), BF)
        sub = dot(att2[mine, :], wout_vm[:, cols]).astype(BF16).astype(F32)
        for t in range(KW):
            total = jnp.sum(sub * gp[pl.ds(12 - t, BF), cols], axis=0, keepdims=True)
            taps_c[t, pl.ds(2 * n, 1), :] = total[:, :HD]
            taps_c[t, pl.ds(2 * n + 1, 1), :] = total[:, HD:]

    def back(t, n):
        arrived(t)
        swap_half(n).start()
        own_half(n)

    def weight(n):
        swap_half(n).wait_recv()
        product(li_t, n * HALF, HALF)

    def d_input(n, carry):
        cols = pl.ds(mult(n * BF, BF), BF)
        din_vm[:, cols] = dot_nt(dqkv[...], wqkv_vm[cols, :]).astype(BF16)
        return carry

    lax.fori_loop(0, 3, lambda d, c: (d_query(d), c)[1], 0)
    arrived(BA)
    swap_att.start()
    lax.fori_loop(3, 5, lambda d, c: (d_query(d), c)[1], 0)

    swap_half(OUT).wait_recv()
    swap_att.wait_recv()
    turn_in(att2, att_t)
    product(att_t, OUT * HALF, HALF)
    rings[0][0].begin()
    lax.fori_loop(5, NC, lambda d, c: (d_query(d), c)[1], 0)
    local(BQ).start()

    def d_key(j):
        two = pl.ds(mult(j * 2 * BF, 2 * BF), 2 * BF)
        dk_s[pl.ds(j * 2, 2)] = (dot(ds_ref[two, :], q_aug[:, pl.ds(0, HD)]) * inv_root).astype(BF16).reshape(2, BF, HD)

        @pl.when(j > 0)
        def _():
            remote(BK, j * 2).start()

        remote(BK, j * 2 + 1).start()

    lax.fori_loop(0, 2, lambda j, c: (d_key(j), c)[1], 0)
    back(BV, VAL)
    rings[0][0].relay()
    weight(VAL)
    rings[1][0].begin()
    lax.fori_loop(2, NC // 2, lambda j, c: (d_key(j), c)[1], 0)
    local(BK).start()
    back(BQ, QUE)
    lax.fori_loop(0, D // BF, lambda n, c: (taps(n), c)[1], 0)
    swap_taps.start()
    weight(QUE)
    rings[2][0].begin()
    rings[3][0].begin()
    swap_taps.wait_recv()
    taps_on(0, "x", taps_c[pl.ds(core * 4, 5)] + taps_p[...])
    get_wq.wait()
    back(BK, KEY)
    lax.fori_loop(0, 2, d_input, 0)
    rings[1][0].relay()
    rings[2][0].relay()
    rings[3][0].relay()
    weight(KEY)
    for p in (5, 6, 4):
        rings[p][0].begin()
    on(0, 0)
    lax.fori_loop(2, 4, d_input, 0)
    on(1, 0)
    taps_on(1, "y", taps_sum(0))
    on(2, 0)
    on(3, 0)
    on(5, 0)
    on(4, 0)
    on(6, 0)
    on(0, 1)
    on(2, 1)
    on(3, 1)
    on(5, 1)
    on(1, 1)
    taps_last("z", taps_sum(1))
    on(4, 1)
    on(6, 1)
    whole(att2.at[pl.ds(0, 32), :], halo_send)
    drain(send_sem, 8 * (NC - 1) * BF * HD * 2)
    drain(core_send.at[0], 4 * BF * D * 2)
    swap_taps.wait_send()
    for n in (0, 1):
        whole(taps_a.at[n, pl.ds(0, 3)], taps_send.at[n])
    whole(taps_z.at[pl.ds(0, 7)], taps_send.at[2])
    ring_width = sum(PARTS[p][1] for p in RINGS)
    drain(ring_send, 3 * BF * ring_width * 2)
    drain(step_send.at[0], 3 * BF * (CW - ring_width) * 2)
    drain(step_send.at[1], 3 * BF // 4 * CW * 2)
    for p in (0, 2, 3, 5, 1, 4, 6):
        rings[p][2].end()
    taps_end()
    whole(do_in.at[pl.ds(0, 7 * 8 * (CW + 2 * HD) * 2 // (2 * HD)), :], last_send)


def collect_kernel(*refs):
    ins, outs, sems = refs[:4], refs[4:8], refs[8]
    copies = [pltpu.make_async_copy(a, b, sems.at[n]) for n, (a, b) in enumerate(zip(ins, outs))]
    for c in copies:
        c.start()
    for c in copies:
        c.wait()


def backward(lengths, li, q, k, v, g, conv, wout, wqkv):
    def vm(shape, dtype=BF16):
        return pltpu.VMEM(shape, dtype)

    buffers = []
    for p, (_, width, order) in enumerate(PARTS):
        leads = []
        for stage in range(3):
            sizes = (("zl", 2), ("y", 4), ("zh", 2), ("x", 4))
            leads.append([n for axis, n in sizes if axis[0] not in order[: stage + 1]])
        halves = [(*leads[0], 16, width // 2)] * 2
        sides = 2 if p in RINGS else 3
        buffers += [vm(shape) for shape in (*halves, (sides, *leads[0], 16, width))]
        buffers.append(vm((3, *leads[1], 16, width)))
        block, kind = ((16, width // 2), BF16) if width > HD else ((8, width), F32)
        buffers.append(vm((*leads[1], 2, *block), kind))
        buffers.append(vm((7, *block), kind))
    dma = pltpu.SemaphoreType.DMA
    outs = (
        jax.ShapeDtypeStruct((BF, D), BF16),
        jax.ShapeDtypeStruct((8, 3 * D), F32),
        jax.ShapeDtypeStruct((8, D), F32),
        jax.ShapeDtypeStruct((KW, D), F32),
    )
    results = pl.pallas_call(
        backward_kernel,
        out_shape=tuple(pltpu.VMEM(o.shape, o.dtype) for o in outs),
        in_specs=[ANY] * 9,
        out_specs=(VM,) * 4,
        scratch_shapes=[
            vm((T, 2 * HD)), vm((T, 2 * HD)), vm((T, 2 * HD)), vm((T, HD)), vm((T, 2 * HD)),
            vm((HD, T)), vm((HD + 16, T)), vm((T, BF), F32), vm((T, T)), vm((T, T)),
            vm((NC, BF, HD)), vm((NC, BF, HD), F32), vm((NC, BF, HD)), vm((NC, BF, HD)),
            vm((NC, BF, HD)), vm((NC, BF, HD)), vm((BF, 3 * D)),
            vm((BF, D)), vm((BF + 16, D), F32), vm((BF, D)), vm((16, D)), vm((16, D)),
            vm((D, D)), vm((D, 3 * D)),
            vm((2 * BF, D)), vm((2 * BF, D)), vm((2 * BF, CW)), vm((D, 2 * BF)), vm((D, 2 * BF)),
            vm((2, 4, 2, 4, 16, CW)),
            vm((KW, 8, HD), F32), vm((5, 8, HD), F32), vm((2, 4, 5, 8, HD), F32), vm((8, 5, 8, HD), F32),
            vm((KW, D), F32), pltpu.SMEM((1,), jnp.int32), *buffers,
            dma(()), dma((8,)), dma((NC,)), dma(()), dma((2,)), dma((6,)), dma((2,)), dma((7,)),
            dma(()), dma((len(RINGS) * 3,)), dma((2,)), dma((2 * NP,)), dma(()), dma((NP,)),
            dma((3,)), dma((3,)),
        ],
        compiler_params=pltpu.CompilerParams(
            collective_id=0, has_side_effects=True, vmem_limit_bytes=60 * 1024 * 1024
        ),
    )(lengths, li, q, k, v, g, conv, wout, wqkv)
    results = [pltpu.with_memory_space_constraint(r, pltpu.VMEM) for r in results]
    return pl.pallas_call(
        collect_kernel,
        out_shape=outs,
        in_specs=[VM] * 4,
        out_specs=(ANY,) * 4,
        scratch_shapes=[dma((4,))],
    )(*results)


def shards(layer_in, queries, keys, values, lengths, w_qkv, w_out, conv_kernel, grad_out):
    d_input, d_wqkv, d_wout, d_kernel = backward(
        lengths, layer_in[0], queries[0], keys[0], values[0], grad_out[0], conv_kernel, w_out, w_qkv
    )
    return d_input[None], d_wqkv, d_wout, d_kernel


def solution(mesh):
    frames = P("rec", "ctx", None)
    in_specs = (frames, frames, frames, frames, P("rec"), P(), P(), P(), frames)
    out_specs = (frames, P(("ctx", "rec"), None), P(("ctx", "rec"), None), P())
    return jax.shard_map(
        shards, mesh=mesh, in_specs=in_specs, out_specs=out_specs, check_vma=False
    )
```

```python
import math

import jax
import jax.numpy as jnp
from jax import lax
from jax.experimental import pallas as pl
from jax.experimental.pallas import tpu as pltpu
from jax.sharding import PartitionSpec as P

HD = 128
KW = 9
NC = 8
BF = 256
T = NC * BF
D = 1024
F32 = jnp.float32
BF16 = jnp.bfloat16
MESH = pl.DeviceIdType.MESH
KB = 512
NEG = -1e30
NT = (((1,), (1,)), ((), ()))
ANY = pl.BlockSpec(memory_space=pl.ANY)
VM = pl.BlockSpec(memory_space=pltpu.VMEM)

TQ, TK, TV, TD, BA, BQ, BK, BV = range(8)


def mult(value, of):
    return pl.multiple_of(value, of)


def dot(a, b):
    return jnp.dot(a, b, preferred_element_type=F32)


def dot_nt(a, b):
    return lax.dot_general(a, b, NT, preferred_element_type=F32)


HALF = 512
CW = 4 * HALF
OUT, VAL, QUE, KEY = range(4)
PARTS = (
    (0, 512, ("x", "y", "z")),
    (512, 512, ("x", "z", "y")),
    (1024, 256, ("y", "z", "x")),
    (1280, 256, ("z", "y", "x")),
    (1536, 256, ("x", "y", "z")),
    (1792, 128, ("y", "x", "z")),
    (1920, 128, ("z", "x", "y")),
)
RINGS = (0, 1, 2, 3, 4)
NP = len(PARTS)


def backward_kernel(
    len_hbm, li_ref, q_ref, k_ref, v_ref, g_ref, conv_ref, wout_ref, wqkv_ref,
    din_vm, dwq_out, dwo_out, dk_out,
    q_aug, k_aug, v_aug, do_in, do_aug, k_t, v_t, s_ref, e_ref, ds_ref,
    att_s, linv_s, dq_s, dk_s, dv_s, dat_s, dqkv,
    g_vm, gp, dsub, halo_lo, halo_hi, wout_vm, wqkv_vm,
    li2, att2, r2, li_t, att_t, grads, taps_c, taps_p, taps_a, taps_z, conv_vm, len_ref, *rest,
):
    bufs = rest[: NP * 6]
    (send_sem, recv_sem, q_recv, halo_send, halo_recv, local_sem, core_send, core_recv,
     ring_send, ring_recv, step_send, step_recv, last_send, last_recv,
     taps_send, taps_recv) = rest[NP * 6 :]
    me = lax.axis_index("ctx")
    rec = lax.axis_index("rec")
    z, y = lax.div(me, 4), lax.rem(me, 4)
    inv_root = 1.0 / math.sqrt(HD)
    c_exp = math.log2(math.e) / math.sqrt(HD)

    def peer(d):
        return lax.rem(z + lax.div(d, 4), 2) * 4 + lax.rem(y + lax.rem(d, 4), 4)

    def origin(d):
        return lax.rem(z + 2 - lax.div(d, 4), 2) * 4 + lax.rem(y + 4 - lax.rem(d, 4), 4)

    def head_cols(h):
        return pl.ds(mult(h * HD, HD), HD)

    def slot(d):
        return pl.ds(mult(d * BF, BF), BF)

    fwd_src = {TQ: q_ref, TK: k_ref, TV: v_ref}
    fwd_dst = {TQ: q_aug, TK: k_aug, TV: v_aug, TD: do_in}
    back_src = {BA: att_s, BQ: dq_s, BK: dk_s, BV: dv_s}
    back_base = {BQ: 0, BK: D, BV: 2 * D}

    def ends(t, d):
        if t <= TD:
            p = peer(d)
            src = dat_s.at[d] if t == TD else fwd_src[t].at[:, head_cols(p)]
            dst = fwd_dst[t].at[slot(d), pl.ds(0, HD)]
        else:
            p = origin(d)
            src = back_src[t].at[d]
            if t == BA:
                dst = att2.at[pl.ds(0, BF), head_cols(me)]
            else:
                dst = dqkv.at[:, pl.ds(mult(back_base[t] + me * HD, HD), HD)]
        return p, src, dst

    def remote(t, d):
        p, src, dst = ends(t, d)
        return pltpu.make_async_remote_copy(
            src_ref=src, dst_ref=dst, send_sem=send_sem,
            recv_sem=q_recv.at[d] if t == TQ else recv_sem.at[t],
            device_id=(p, rec), device_id_type=MESH,
        )

    def local(t):
        _, src, dst = ends(t, 0)
        return pltpu.make_async_copy(src, dst, q_recv.at[0] if t == TQ else recv_sem.at[t])

    def whole(ref, sem):
        pltpu.make_async_copy(ref, ref, sem).wait()

    def drain(sem, count):
        whole(e_ref.at[pl.ds(0, count // (2 * T)), :], sem)

    def arrived(t):
        if t <= TD:
            whole(fwd_dst[t].at[:, pl.ds(0, HD)], recv_sem.at[t])
        elif t == BA:
            whole(att2.at[pl.ds(0, BF), :], recv_sem.at[t])
        else:
            whole(dqkv.at[:, pl.ds(back_base[t], D)], recv_sem.at[t])

    def each_peer(body):
        def step(d, carry):
            body(d)
            return carry

        lax.fori_loop(1, NC, step, 0)

    def each_slot(body):
        def step(d, carry):
            body(d)
            return carry

        lax.fori_loop(0, NC, step, 0)

    get_g = pltpu.make_async_copy(g_ref, g_vm, local_sem.at[0])
    get_w = pltpu.make_async_copy(wout_ref, wout_vm, local_sem.at[1])
    get_g.start()
    get_w.start()
    for t in (TK, TQ, TV):
        local(t).start()
    mine, theirs = pl.ds(0, BF), pl.ds(BF, BF)
    get_li = pltpu.make_async_copy(li_ref, li2.at[mine, :], local_sem.at[2])
    get_li.start()
    get_wq = pltpu.make_async_copy(wqkv_ref, wqkv_vm, local_sem.at[3])
    get_conv = pltpu.make_async_copy(conv_ref, conv_vm, local_sem.at[5])
    get_conv.start()
    get_len = pltpu.make_async_copy(len_hbm, len_ref, local_sem.at[4])
    get_len.start()

    core = lax.rem(rec, 2)
    other = 1 - core
    at = {"x": lax.rem(lax.div(rec, 2), 4), "y": y, "z": lax.div(rec, 8) * 2 + z}

    def device(moved, to, on_core=core):
        p = {**at, **({moved: to} if moved else {})}
        return (
            lax.rem(p["z"], 2) * 4 + p["y"],
            lax.div(p["z"], 2) * 8 + p["x"] * 2 + on_core,
        )

    def off(axis, by):
        return lax.rem(at[axis] + by, 4)

    partner = device(None, None, other)
    far = lax.rem(lax.div(rec, 8) + 1, 2)
    greet = [partner] + [device("x", off("x", by)) for by in (1, 2, 3)]
    greet += [device("z", far * 2 + zl) for zl in (0, 1)]
    greet += [device(a, off(a, by), other) for a in "xyz" for by in (1, 2, 3)]

    barrier = pltpu.get_barrier_semaphore()
    each_peer(
        lambda d: pl.semaphore_signal(barrier, inc=1, device_id=(peer(d), rec), device_id_type=MESH)
    )
    for who in greet:
        pl.semaphore_signal(barrier, inc=1, device_id=who, device_id_type=MESH)
    pl.semaphore_wait(barrier, NC - 1 + len(greet))

    right, left = lax.rem(me + 1, NC), lax.rem(me + NC - 1, NC)
    to_right = pltpu.make_async_remote_copy(
        src_ref=g_ref.at[pl.ds(BF - 16, 16), :], dst_ref=halo_lo, send_sem=halo_send,
        recv_sem=halo_recv.at[0], device_id=(right, rec), device_id_type=MESH,
    )
    to_left = pltpu.make_async_remote_copy(
        src_ref=g_ref.at[pl.ds(0, 16), :], dst_ref=halo_hi, send_sem=halo_send,
        recv_sem=halo_recv.at[1], device_id=(left, rec), device_id_type=MESH,
    )
    to_right.start()
    to_left.start()
    for t in (TK, TQ, TV):
        each_peer(lambda d: remote(t, d).start())

    def to_partner(n, src, dst):
        return pltpu.make_async_remote_copy(
            src_ref=src, dst_ref=dst, send_sem=core_send.at[n // 6], recv_sem=core_recv.at[n],
            device_id=partner, device_id_type=MESH,
        )

    def half(ref, base, c):
        return ref.at[:, pl.ds(mult(base + c * HALF, HALF), HALF)]

    group = {OUT: (dsub, 0), VAL: (dqkv, 2 * D), QUE: (dqkv, 0), KEY: (dqkv, D)}

    def swap_half(n):
        ref, base = group[n]
        return to_partner(n, half(ref, base, other), r2.at[theirs, pl.ds(n * HALF, HALF)])

    def own_half(n):
        ref, base = group[n]
        r2[mine, pl.ds(n * HALF, HALF)] = half(ref, base, core)[...]

    swap_li = to_partner(4, li_ref, li2.at[theirs, :])
    swap_att = to_partner(5, att2.at[mine, :], att2.at[theirs, :])
    swap_taps = to_partner(6, taps_c.at[pl.ds(other * 4, 5)], taps_p)
    swap_li.start()

    get_len.wait()
    length = len_ref[0]
    lane = lax.broadcasted_iota(jnp.int32, (BF, HD), 1)
    row = lax.broadcasted_iota(jnp.int32, (BF, HD), 0)

    def extra(d):
        masked = (lane == 0) & (row + origin(d) * BF >= length)
        k_aug[slot(d), pl.ds(HD, HD)] = jnp.where(masked, NEG, 0.0).astype(BF16)
        q_aug[slot(d), pl.ds(HD, HD)] = jnp.where(lane == 0, 1.0, 0.0).astype(BF16)
        v_aug[slot(d), pl.ds(HD, HD)] = jnp.where(lane < 2, 1.0, 0.0).astype(BF16)

    each_slot(extra)
    first = lax.broadcasted_iota(jnp.int32, (16, T), 0) == 0
    v_t[pl.ds(HD, 16), :] = jnp.where(first, 1.0, 0.0).astype(BF16)

    get_g.wait()
    get_conv.wait()
    gp[pl.ds(8, BF), :] = g_vm[...].astype(F32)
    to_right.wait_recv()
    to_left.wait_recv()
    low = halo_lo[...].astype(F32)[8:16, :]
    gp[pl.ds(0, 8), :] = jnp.where(me > 0, low, 0.0)
    high = halo_hi[...].astype(F32)[0:8, :]
    gp[pl.ds(8 + BF, 8), :] = jnp.where(me < NC - 1, high, 0.0)

    def conv_grad(n):
        cols = pl.ds(mult(n * HD, HD), HD)
        total = gp[pl.ds(8, BF), cols]
        for t in range(KW):
            total = total + conv_vm[pl.ds(t, 1), cols] * gp[pl.ds(12 - t, BF), cols]
        dsub[:, cols] = total.astype(BF16)

    each_slot(conv_grad)
    swap_half(OUT).start()
    own_half(OUT)
    get_wq.start()

    get_w.wait()

    def datt(d):
        rows = pl.ds(mult(peer(d) * HD, HD), HD)
        dat_s[d] = dot_nt(dsub[...], wout_vm[rows, :]).astype(BF16)

        @pl.when(d > 0)
        def _():
            remote(TD, d).start()

    each_slot(datt)
    local(TD).start()

    def turn_in(src, dst):
        def step(n, carry):
            cols = pl.ds(mult(n * BF, BF), BF)
            dst[cols, :] = src[:, cols].T
            return carry

        lax.fori_loop(0, D // BF, step, 0)

    get_li.wait()
    swap_li.wait_recv()
    turn_in(li2, li_t)

    arrived(TK)
    local(TQ).wait()

    def scores(d):
        @pl.when(d > 0)
        def _():
            remote(TQ, d).wait_recv()

        qd = q_aug[slot(d), :]
        top = None
        for b in range(T // KB):
            rows = pl.ds(b * KB, KB)
            s = dot_nt(k_aug[rows, :], qd)
            s_ref[rows, :] = s
            m = jnp.max(s, axis=0, keepdims=True)
            top = m if top is None else jnp.maximum(top, m)
        for b in range(T // KB):
            rows = pl.ds(b * KB, KB)
            e_ref[rows, slot(d)] = jnp.exp2((s_ref[rows, :] - top) * c_exp).astype(BF16)

    each_slot(scores)
    arrived(TV)

    def turn(d):
        k_t[:, slot(d)] = k_aug[slot(d), pl.ds(0, HD)].T
        v_t[pl.ds(0, HD), slot(d)] = v_aug[slot(d), pl.ds(0, HD)].T

    each_slot(turn)

    def attend(d):
        acc = dot(v_t[...], e_ref[:, slot(d)])
        inv = 1.0 / acc[HD : HD + 1, :]
        att_s[d] = (acc[:HD, :] * inv).T.astype(BF16)
        linv_s[d] = jnp.broadcast_to(inv, (HD, BF)).T

        @pl.when(d > 0)
        def _():
            remote(BA, d).start()

    each_slot(attend)
    local(BA).start()

    arrived(TD)

    def backward_in(d):
        do = (do_in[slot(d), :].astype(F32) * linv_s[d]).astype(BF16)
        delta = -jnp.sum(do.astype(F32) * att_s[d].astype(F32), axis=1, keepdims=True)
        hi = delta.astype(BF16).astype(F32)
        do_aug[slot(d), pl.ds(0, HD)] = do
        do_aug[slot(d), pl.ds(HD, HD)] = jnp.where(
            lane == 0, hi, jnp.where(lane == 1, delta - hi, 0.0)
        ).astype(BF16)

    each_slot(backward_in)

    def d_value(j):
        two = pl.ds(mult(j * 2 * BF, 2 * BF), 2 * BF)
        dv_s[pl.ds(j * 2, 2)] = dot(e_ref[two, :], do_aug[:, pl.ds(0, HD)]).astype(BF16).reshape(2, BF, HD)

        @pl.when(j > 0)
        def _():
            remote(BV, j * 2).start()

        remote(BV, j * 2 + 1).start()

    lax.fori_loop(0, NC // 2, lambda j, c: (d_value(j), c)[1], 0)
    local(BV).start()

    def d_query(d):
        dod = do_aug[slot(d), :]
        acc = jnp.zeros((HD, BF), F32)
        for b in range(T // KB):
            rows = pl.ds(b * KB, KB)
            dp = dot_nt(v_aug[rows, :], dod)
            ds = (e_ref[rows, slot(d)].astype(F32) * dp).astype(BF16)
            ds_ref[rows, slot(d)] = ds
            acc = acc + dot(k_t[:, rows], ds)
        dq_s[d] = (acc * inv_root).T.astype(BF16)

        @pl.when(d > 0)
        def _():
            remote(BQ, d).start()

    def product(lhs, start, width):
        def step(zl, carry):
            rows = pl.ds(mult(zl * HALF, HALF), HALF)
            g = dot(lhs[rows, :], r2[:, pl.ds(start, width)]).astype(BF16)
            grads[zl, :, :, :, :, pl.ds(start, width)] = g.reshape(4, 2, 4, 16, width)
            return carry

        lax.fori_loop(0, 2, step, 0)

    def region(fixed, start, width):
        zl = zh = slice(None)
        if "z" in fixed:
            zl, zh = lax.rem(fixed["z"], 2), lax.div(fixed["z"], 2)
        return grads.at[
            zl, fixed.get("y", slice(None)), zh, fixed.get("x", slice(None)), :, pl.ds(start, width)
        ]

    class Stage:
        def __init__(self, part, stage):
            self.start, self.width, order = PARTS[part]
            self.part = part
            self.axis = order[stage]
            self.fixed = {a: at[a] for a in order[:stage]}
            self.stage = stage

        def piece(self, by, start=0, width=None):
            width = self.width if width is None else width
            fixed = {**self.fixed, self.axis: off(self.axis, by)}
            return region(fixed, self.start + start, width)

        def copy(self, src, dst, by, recv):
            return pltpu.make_async_remote_copy(
                src_ref=src, dst_ref=dst, send_sem=self.send, recv_sem=recv,
                device_id=device(self.axis, off(self.axis, by)), device_id_type=MESH,
            )

        def keep(self, total):
            if self.stage == 0:
                self.piece(0)[...] = total.astype(BF16)
            else:
                pair = bufs[self.part * 6 + 4]
                for c in (0, 1):
                    rows = total[..., c * 8 : c * 8 + 8, :]
                    if self.width > HD:
                        h = self.width // 2
                        rows = jnp.concatenate([rows[..., :h], rows[..., h:]], axis=-2)
                    pair[..., c, :, :] = rows.astype(pair.dtype)

    class Ring(Stage):
        def __init__(self, part):
            super().__init__(part, 0)
            self.ra, self.rb, self.ends = bufs[part * 6 : part * 6 + 3]
            h = self.width // 2
            lead = (slice(None),) * (len(self.ra.shape) - 1)
            low_a, low_b = (0, *lead, pl.ds(0, h)), (0, *lead, pl.ds(h, h))
            high_a, high_b = (1, *lead, pl.ds(0, h)), (1, *lead, pl.ds(h, h))
            self.send = ring_send
            recv = [ring_recv.at[part * 3 + n] for n in range(3)]
            self.copies = [
                self.copy(self.piece(2, 0, h), self.ra, 1, recv[0]),
                self.copy(self.piece(2, h, h), self.rb, 3, recv[1]),
                self.copy(self.piece(1, h, h), self.ends.at[low_b], 1, recv[2]),
                self.copy(self.piece(3, 0, h), self.ends.at[high_a], 3, recv[2]),
                self.copy(self.piece(1, 0, h), self.ends.at[low_a], 1, recv[2]),
                self.copy(self.piece(3, h, h), self.ends.at[high_b], 3, recv[2]),
            ]
            self.recv = recv[2]

        def begin(self):
            for c in self.copies[:4]:
                c.start()

        def relay(self):
            h = self.width // 2
            for n, by, buf, start in ((0, 1, self.ra, 0), (1, 3, self.rb, h)):
                self.copies[n].wait_recv()
                here = self.piece(by, start, h)
                here[...] = (here[...].astype(F32) + buf[...].astype(F32)).astype(BF16)
                self.copies[4 + n].start()

        def end(self):
            whole(self.ends, self.recv)
            here = self.piece(0)[...].astype(F32)
            self.keep(here + (self.ends[0].astype(F32) + self.ends[1].astype(F32)))

    class Direct(Stage):
        def __init__(self, part, stage):
            super().__init__(part, stage)
            self.buf = bufs[part * 6 + (3 if stage else 2)]
            n = part if stage else NP + part
            self.send, self.recv = step_send.at[min(stage, 1)], step_recv.at[n]
            self.copies = [
                self.copy(self.piece(by), self.buf.at[by - 1], by, self.recv) for by in (1, 2, 3)
            ]

        def begin(self):
            for c in self.copies:
                c.start()

        def end(self):
            whole(self.buf, self.recv)
            here = self.piece(0)[...].astype(F32)
            b = [self.buf[n].astype(F32) for n in range(3)]
            self.keep((here + b[0]) + (b[1] + b[2]))

    class Last(Stage):
        def __init__(self, part):
            super().__init__(part, 2)
            self.pair, self.buf = bufs[part * 6 + 4 : part * 6 + 6]
            self.send, self.recv = last_send, last_recv.at[part]
            self.copies = []
            for n, (turned, by) in enumerate((t, b) for t in (0, 1) for b in range(4) if t + b):
                to = lax.rem(core + turned, 2)
                who = device(self.axis, off(self.axis, by), to)
                self.copies.append(
                    pltpu.make_async_remote_copy(
                        src_ref=self.rows(by, to), dst_ref=self.buf.at[n],
                        send_sem=self.send, recv_sem=self.recv,
                        device_id=who, device_id_type=MESH,
                    )
                )

        def rows(self, by, to):
            chip = off(self.axis, by)
            if self.axis == "z":
                return self.pair.at[lax.rem(chip, 2), lax.div(chip, 2), to]
            return self.pair.at[chip, to]

        def begin(self):
            for c in self.copies:
                c.start()

        def end(self):
            whole(self.buf, self.recv)
            b = [self.buf[n].astype(F32) for n in range(7)]
            here = self.rows(0, core)[...].astype(F32)
            n, inside = divmod(self.start, HALF)
            out, base = ((dwo_out, 0), (dwq_out, 2 * D), (dwq_out, 0), (dwq_out, D))[n]
            for who, block in (
                (core, (here + b[0]) + (b[1] + b[2])),
                (other, (b[3] + b[4]) + (b[5] + b[6])),
            ):
                first = base + who * HALF + inside
                if self.width > HD:
                    h = self.width // 2
                    out[:, pl.ds(mult(first, HD), h)] = block[:8]
                    out[:, pl.ds(mult(first + h, HD), h)] = block[8:]
                else:
                    out[:, pl.ds(mult(first, HD), HD)] = block

    rings = [
        (Ring(p) if p in RINGS else Direct(p, 0), Direct(p, 1), Last(p)) for p in range(NP)
    ]

    def on(p, stage):
        rings[p][stage].end()
        rings[p][stage + 1].begin()

    def taps_copy(n, src, dst, who):
        pltpu.make_async_remote_copy(
            src_ref=src, dst_ref=dst, send_sem=taps_send.at[n], recv_sem=taps_recv.at[n],
            device_id=who, device_id_type=MESH,
        ).start()

    def taps_on(n, axis, value):
        here = taps_a.at[n, at[axis]]
        here[...] = value
        for by in (1, 2, 3):
            taps_copy(n, here, here, device(axis, off(axis, by)))

    def taps_last(axis, value):
        here = taps_z.at[core * 4 + at[axis]]
        here[...] = value
        for by in (0, 1, 2, 3):
            if by:
                taps_copy(2, here, here, device(axis, off(axis, by)))
            taps_copy(2, here, here, device(axis, off(axis, by), other))

    def sum_4(ref, n):
        return (ref[n] + ref[n + 1]) + (ref[n + 2] + ref[n + 3])

    def taps_sum(n):
        whole(taps_a.at[n, pl.ds(0, 3)], taps_recv.at[n])
        return sum_4(taps_a.at[n], 0)

    def taps_end():
        whole(taps_z.at[pl.ds(0, 7)], taps_recv.at[2])
        halves = sum_4(taps_z, 0), sum_4(taps_z, 4)
        for t in range(KW):
            block = halves[0][t] if t < 5 else halves[1][t - 4]
            for n in range(D // HD):
                dk_out[t : t + 1, n * HD : (n + 1) * HD] = block[n : n + 1, :]

    def taps(n):
        cols = pl.ds(mult(n * BF, BF), BF)
        sub = dot(att2[mine, :], wout_vm[:, cols]).astype(BF16).astype(F32)
        for t in range(KW):
            total = jnp.sum(sub * gp[pl.ds(12 - t, BF), cols], axis=0, keepdims=True)
            taps_c[t, pl.ds(2 * n, 1), :] = total[:, :HD]
            taps_c[t, pl.ds(2 * n + 1, 1), :] = total[:, HD:]

    def back(t, n):
        arrived(t)
        swap_half(n).start()
        own_half(n)

    def weight(n):
        swap_half(n).wait_recv()
        product(li_t, n * HALF, HALF)

    def d_input(n, carry):
        cols = pl.ds(mult(n * BF, BF), BF)
        din_vm[:, cols] = dot_nt(dqkv[...], wqkv_vm[cols, :]).astype(BF16)
        return carry

    lax.fori_loop(0, 3, lambda d, c: (d_query(d), c)[1], 0)
    arrived(BA)
    swap_att.start()
    lax.fori_loop(3, 5, lambda d, c: (d_query(d), c)[1], 0)

    swap_half(OUT).wait_recv()
    swap_att.wait_recv()
    turn_in(att2, att_t)
    product(att_t, OUT * HALF, HALF)
    rings[0][0].begin()
    lax.fori_loop(5, NC, lambda d, c: (d_query(d), c)[1], 0)
    local(BQ).start()

    def d_key(j):
        two = pl.ds(mult(j * 2 * BF, 2 * BF), 2 * BF)
        dk_s[pl.ds(j * 2, 2)] = (dot(ds_ref[two, :], q_aug[:, pl.ds(0, HD)]) * inv_root).astype(BF16).reshape(2, BF, HD)

        @pl.when(j > 0)
        def _():
            remote(BK, j * 2).start()

        remote(BK, j * 2 + 1).start()

    lax.fori_loop(0, NC // 2, lambda j, c: (d_key(j), c)[1], 0)
    local(BK).start()
    back(BV, VAL)
    rings[0][0].relay()
    weight(VAL)
    rings[1][0].begin()
    back(BQ, QUE)
    lax.fori_loop(0, D // BF, lambda n, c: (taps(n), c)[1], 0)
    swap_taps.start()
    weight(QUE)
    rings[2][0].begin()
    rings[3][0].begin()
    swap_taps.wait_recv()
    taps_on(0, "x", taps_c[pl.ds(core * 4, 5)] + taps_p[...])
    get_wq.wait()
    back(BK, KEY)
    lax.fori_loop(0, 2, d_input, 0)
    rings[1][0].relay()
    rings[2][0].relay()
    rings[3][0].relay()
    weight(KEY)
    for p in (5, 6, 4):
        rings[p][0].begin()
    on(0, 0)
    lax.fori_loop(2, 4, d_input, 0)
    on(1, 0)
    taps_on(1, "y", taps_sum(0))
    rings[4][0].relay()
    on(2, 0)
    on(3, 0)
    on(5, 0)
    on(6, 0)
    on(4, 0)
    on(0, 1)
    on(5, 1)
    on(6, 1)
    on(2, 1)
    on(3, 1)
    on(1, 1)
    taps_last("z", taps_sum(1))
    on(4, 1)
    whole(att2.at[pl.ds(0, 32), :], halo_send)
    drain(send_sem, 8 * (NC - 1) * BF * HD * 2)
    drain(core_send.at[0], 4 * BF * D * 2)
    swap_taps.wait_send()
    for n in (0, 1):
        whole(taps_a.at[n, pl.ds(0, 3)], taps_send.at[n])
    whole(taps_z.at[pl.ds(0, 7)], taps_send.at[2])
    ring_width = sum(PARTS[p][1] for p in RINGS)
    drain(ring_send, 3 * BF * ring_width * 2)
    drain(step_send.at[0], 3 * BF * (CW - ring_width) * 2)
    drain(step_send.at[1], 3 * BF // 4 * CW * 2)
    for p in (0, 5, 6, 2, 3, 1, 4):
        rings[p][2].end()
    taps_end()
    whole(do_in.at[pl.ds(0, 7 * 8 * (CW + 2 * HD) * 2 // (2 * HD)), :], last_send)


def collect_kernel(*refs):
    ins, outs, sems = refs[:4], refs[4:8], refs[8]
    copies = [pltpu.make_async_copy(a, b, sems.at[n]) for n, (a, b) in enumerate(zip(ins, outs))]
    for c in copies:
        c.start()
    for c in copies:
        c.wait()


def backward(lengths, li, q, k, v, g, conv, wout, wqkv):
    def vm(shape, dtype=BF16):
        return pltpu.VMEM(shape, dtype)

    buffers = []
    for p, (_, width, order) in enumerate(PARTS):
        leads = []
        for stage in range(3):
            sizes = (("zl", 2), ("y", 4), ("zh", 2), ("x", 4))
            leads.append([n for axis, n in sizes if axis[0] not in order[: stage + 1]])
        halves = [(*leads[0], 16, width // 2)] * 2
        sides = 2 if p in RINGS else 3
        buffers += [vm(shape) for shape in (*halves, (sides, *leads[0], 16, width))]
        buffers.append(vm((3, *leads[1], 16, width)))
        block, kind = ((16, width // 2), BF16) if width > HD else ((8, width), F32)
        buffers.append(vm((*leads[1], 2, *block), kind))
        buffers.append(vm((7, *block), kind))
    dma = pltpu.SemaphoreType.DMA
    outs = (
        jax.ShapeDtypeStruct((BF, D), BF16),
        jax.ShapeDtypeStruct((8, 3 * D), F32),
        jax.ShapeDtypeStruct((8, D), F32),
        jax.ShapeDtypeStruct((KW, D), F32),
    )
    results = pl.pallas_call(
        backward_kernel,
        out_shape=tuple(pltpu.VMEM(o.shape, o.dtype) for o in outs),
        in_specs=[ANY] * 9,
        out_specs=(VM,) * 4,
        scratch_shapes=[
            vm((T, 2 * HD)), vm((T, 2 * HD)), vm((T, 2 * HD)), vm((T, HD)), vm((T, 2 * HD)),
            vm((HD, T)), vm((HD + 16, T)), vm((T, BF), F32), vm((T, T)), vm((T, T)),
            vm((NC, BF, HD)), vm((NC, BF, HD), F32), vm((NC, BF, HD)), vm((NC, BF, HD)),
            vm((NC, BF, HD)), vm((NC, BF, HD)), vm((BF, 3 * D)),
            vm((BF, D)), vm((BF + 16, D), F32), vm((BF, D)), vm((16, D)), vm((16, D)),
            vm((D, D)), vm((D, 3 * D)),
            vm((2 * BF, D)), vm((2 * BF, D)), vm((2 * BF, CW)), vm((D, 2 * BF)), vm((D, 2 * BF)),
            vm((2, 4, 2, 4, 16, CW)),
            vm((KW, 8, HD), F32), vm((5, 8, HD), F32), vm((2, 4, 5, 8, HD), F32), vm((8, 5, 8, HD), F32),
            vm((KW, D), F32), pltpu.SMEM((1,), jnp.int32), *buffers,
            dma(()), dma((8,)), dma((NC,)), dma(()), dma((2,)), dma((6,)), dma((2,)), dma((7,)),
            dma(()), dma((len(RINGS) * 3,)), dma((2,)), dma((2 * NP,)), dma(()), dma((NP,)),
            dma((3,)), dma((3,)),
        ],
        compiler_params=pltpu.CompilerParams(
            collective_id=0, has_side_effects=True, vmem_limit_bytes=60 * 1024 * 1024
        ),
    )(lengths, li, q, k, v, g, conv, wout, wqkv)
    results = [pltpu.with_memory_space_constraint(r, pltpu.VMEM) for r in results]
    return pl.pallas_call(
        collect_kernel,
        out_shape=outs,
        in_specs=[VM] * 4,
        out_specs=(ANY,) * 4,
        scratch_shapes=[dma((4,))],
    )(*results)


def shards(layer_in, queries, keys, values, lengths, w_qkv, w_out, conv_kernel, grad_out):
    d_input, d_wqkv, d_wout, d_kernel = backward(
        lengths, layer_in[0], queries[0], keys[0], values[0], grad_out[0], conv_kernel, w_out, w_qkv
    )
    return d_input[None], d_wqkv, d_wout, d_kernel


def solution(mesh):
    frames = P("rec", "ctx", None)
    in_specs = (frames, frames, frames, frames, P("rec"), P(), P(), P(), frames)
    out_specs = (frames, P(("ctx", "rec"), None), P(("ctx", "rec"), None), P())
    return jax.shard_map(
        shards, mesh=mesh, in_specs=in_specs, out_specs=out_specs, check_vma=False
    )
```

```python
import math

import jax
import jax.numpy as jnp
from jax import lax
from jax.experimental import pallas as pl
from jax.experimental.pallas import tpu as pltpu
from jax.sharding import PartitionSpec as P

HD = 128
KW = 9
NC = 8
BF = 256
T = NC * BF
D = 1024
F32 = jnp.float32
BF16 = jnp.bfloat16
MESH = pl.DeviceIdType.MESH
KB = 512
NEG = -1e30
NT = (((1,), (1,)), ((), ()))
ANY = pl.BlockSpec(memory_space=pl.ANY)
VM = pl.BlockSpec(memory_space=pltpu.VMEM)

TQ, TK, TV, TD, BA, BQ, BK, BV = range(8)


def mult(value, of):
    return pl.multiple_of(value, of)


def dot(a, b):
    return jnp.dot(a, b, preferred_element_type=F32)


def dot_nt(a, b):
    return lax.dot_general(a, b, NT, preferred_element_type=F32)


HALF = 512
CW = 4 * HALF
OUT, VAL, QUE, KEY = range(4)
PARTS = (
    (0, 512, ("x", "y", "z")),
    (512, 512, ("x", "z", "y")),
    (1024, 256, ("y", "z", "x")),
    (1280, 256, ("z", "y", "x")),
    (1536, 256, ("x", "y", "z")),
    (1792, 128, ("y", "x", "z")),
    (1920, 128, ("z", "x", "y")),
)
PLANE = 4
RINGS = (0, 1, 2, 3, 4)
NP = len(PARTS)


def backward_kernel(
    len_hbm, li_ref, q_ref, k_ref, v_ref, g_ref, conv_ref, wout_ref, wqkv_ref,
    din_vm, dwq_out, dwo_out, dk_out,
    q_aug, k_aug, v_aug, do_in, do_aug, k_t, v_t, s_ref, e_ref, ds_ref,
    att_s, linv_s, dq_s, dk_s, dv_s, dat_s, dqkv,
    g_vm, gp, dsub, halo_lo, halo_hi, wout_vm, wqkv_vm,
    li2, att2, r2, li_t, att_t, grads, taps_c, taps_p, taps_a, taps_z, conv_vm, len_ref, *rest,
):
    bufs = rest[: NP * 6]
    (send_sem, recv_sem, q_recv, halo_send, halo_recv, local_sem, core_send, core_recv,
     ring_send, ring_recv, step_send, step_recv, last_send, last_recv,
     taps_send, taps_recv, plane_send, plane_recv) = rest[NP * 6 :]
    me = lax.axis_index("ctx")
    rec = lax.axis_index("rec")
    z, y = lax.div(me, 4), lax.rem(me, 4)
    inv_root = 1.0 / math.sqrt(HD)
    c_exp = math.log2(math.e) / math.sqrt(HD)

    def peer(d):
        return lax.rem(z + lax.div(d, 4), 2) * 4 + lax.rem(y + lax.rem(d, 4), 4)

    def origin(d):
        return lax.rem(z + 2 - lax.div(d, 4), 2) * 4 + lax.rem(y + 4 - lax.rem(d, 4), 4)

    def head_cols(h):
        return pl.ds(mult(h * HD, HD), HD)

    def slot(d):
        return pl.ds(mult(d * BF, BF), BF)

    fwd_src = {TQ: q_ref, TK: k_ref, TV: v_ref}
    fwd_dst = {TQ: q_aug, TK: k_aug, TV: v_aug, TD: do_in}
    back_src = {BA: att_s, BQ: dq_s, BK: dk_s, BV: dv_s}
    back_base = {BQ: 0, BK: D, BV: 2 * D}

    def ends(t, d):
        if t <= TD:
            p = peer(d)
            src = dat_s.at[d] if t == TD else fwd_src[t].at[:, head_cols(p)]
            dst = fwd_dst[t].at[slot(d), pl.ds(0, HD)]
        else:
            p = origin(d)
            src = back_src[t].at[d]
            if t == BA:
                dst = att2.at[pl.ds(0, BF), head_cols(me)]
            else:
                dst = dqkv.at[:, pl.ds(mult(back_base[t] + me * HD, HD), HD)]
        return p, src, dst

    def remote(t, d):
        p, src, dst = ends(t, d)
        return pltpu.make_async_remote_copy(
            src_ref=src, dst_ref=dst, send_sem=send_sem,
            recv_sem=q_recv.at[d] if t == TQ else recv_sem.at[t],
            device_id=(p, rec), device_id_type=MESH,
        )

    def local(t):
        _, src, dst = ends(t, 0)
        return pltpu.make_async_copy(src, dst, q_recv.at[0] if t == TQ else recv_sem.at[t])

    def whole(ref, sem):
        pltpu.make_async_copy(ref, ref, sem).wait()

    def drain(sem, count):
        whole(e_ref.at[pl.ds(0, count // (2 * T)), :], sem)

    def arrived(t):
        if t <= TD:
            whole(fwd_dst[t].at[:, pl.ds(0, HD)], recv_sem.at[t])
        elif t == BA:
            whole(att2.at[pl.ds(0, BF), :], recv_sem.at[t])
        else:
            whole(dqkv.at[:, pl.ds(back_base[t], D)], recv_sem.at[t])

    def each_peer(body):
        def step(d, carry):
            body(d)
            return carry

        lax.fori_loop(1, NC, step, 0)

    def each_slot(body):
        def step(d, carry):
            body(d)
            return carry

        lax.fori_loop(0, NC, step, 0)

    core = lax.rem(rec, 2)
    other = 1 - core
    at = {"x": lax.rem(lax.div(rec, 2), 4), "y": y, "z": lax.div(rec, 8) * 2 + z}

    def device(moved, to, on_core=core):
        p = {**at, **({moved: to} if moved else {})}
        return (
            lax.rem(p["z"], 2) * 4 + p["y"],
            lax.div(p["z"], 2) * 8 + p["x"] * 2 + on_core,
        )

    def off(axis, by):
        return lax.rem(at[axis] + by, 4)

    partner = device(None, None, other)
    far = lax.rem(lax.div(rec, 8) + 1, 2)
    greet = [partner] + [device("x", off("x", by)) for by in (1, 2, 3)]
    greet += [device("z", far * 2 + zl) for zl in (0, 1)]
    greet += [device(a, off(a, by), other) for a in "xyz" for by in (1, 2, 3)]

    def on_plane(chip_z, by, on_core):
        return (
            lax.rem(chip_z, 2) * 4 + off("y", by),
            lax.div(chip_z, 2) * 8 + at["x"] * 2 + on_core,
        )

    greet += [
        on_plane(chip_z, by, on_core)
        for by in (1, 2, 3)
        for chip_z, on_core in (
            (lax.div(rec, 8) * 2 + 1 - z, other),
            *((far * 2 + zl, c) for zl in (0, 1) for c in (core, other)),
        )
    ]

    barrier = pltpu.get_barrier_semaphore()
    each_peer(
        lambda d: pl.semaphore_signal(barrier, inc=1, device_id=(peer(d), rec), device_id_type=MESH)
    )
    for who in greet:
        pl.semaphore_signal(barrier, inc=1, device_id=who, device_id_type=MESH)
    get_g = pltpu.make_async_copy(g_ref, g_vm, local_sem.at[0])
    get_w = pltpu.make_async_copy(wout_ref, wout_vm, local_sem.at[1])
    get_g.start()
    get_w.start()
    for t in (TK, TQ, TV):
        local(t).start()
    mine, theirs = pl.ds(0, BF), pl.ds(BF, BF)
    get_li = pltpu.make_async_copy(li_ref, li2.at[mine, :], local_sem.at[2])
    get_li.start()
    get_wq = pltpu.make_async_copy(wqkv_ref, wqkv_vm, local_sem.at[3])
    get_conv = pltpu.make_async_copy(conv_ref, conv_vm, local_sem.at[5])
    get_conv.start()
    get_len = pltpu.make_async_copy(len_hbm, len_ref, local_sem.at[4])
    get_len.start()

    pl.semaphore_wait(barrier, NC - 1 + len(greet))

    right, left = lax.rem(me + 1, NC), lax.rem(me + NC - 1, NC)
    to_right = pltpu.make_async_remote_copy(
        src_ref=g_ref.at[pl.ds(BF - 16, 16), :], dst_ref=halo_lo, send_sem=halo_send,
        recv_sem=halo_recv.at[0], device_id=(right, rec), device_id_type=MESH,
    )
    to_left = pltpu.make_async_remote_copy(
        src_ref=g_ref.at[pl.ds(0, 16), :], dst_ref=halo_hi, send_sem=halo_send,
        recv_sem=halo_recv.at[1], device_id=(left, rec), device_id_type=MESH,
    )
    to_right.start()
    to_left.start()
    for t in (TK, TQ, TV):
        each_peer(lambda d: remote(t, d).start())

    def to_partner(n, src, dst):
        return pltpu.make_async_remote_copy(
            src_ref=src, dst_ref=dst, send_sem=core_send.at[n // 6], recv_sem=core_recv.at[n],
            device_id=partner, device_id_type=MESH,
        )

    def half(ref, base, c):
        return ref.at[:, pl.ds(mult(base + c * HALF, HALF), HALF)]

    group = {OUT: (dsub, 0), VAL: (dqkv, 2 * D), QUE: (dqkv, 0), KEY: (dqkv, D)}

    def swap_half(n):
        ref, base = group[n]
        return to_partner(n, half(ref, base, other), r2.at[theirs, pl.ds(n * HALF, HALF)])

    def own_half(n):
        ref, base = group[n]
        r2[mine, pl.ds(n * HALF, HALF)] = half(ref, base, core)[...]

    swap_li = to_partner(4, li_ref, li2.at[theirs, :])
    swap_att = to_partner(5, att2.at[mine, :], att2.at[theirs, :])
    swap_taps = to_partner(6, taps_c.at[pl.ds(other * 4, 5)], taps_p)
    swap_li.start()

    get_len.wait()
    length = len_ref[0]
    lane = lax.broadcasted_iota(jnp.int32, (BF, HD), 1)
    row = lax.broadcasted_iota(jnp.int32, (BF, HD), 0)

    def extra(d):
        masked = (lane == 0) & (row + origin(d) * BF >= length)
        k_aug[slot(d), pl.ds(HD, HD)] = jnp.where(masked, NEG, 0.0).astype(BF16)
        q_aug[slot(d), pl.ds(HD, HD)] = jnp.where(lane == 0, 1.0, 0.0).astype(BF16)
        v_aug[slot(d), pl.ds(HD, HD)] = jnp.where(lane < 2, 1.0, 0.0).astype(BF16)

    each_slot(extra)
    first = lax.broadcasted_iota(jnp.int32, (16, T), 0) == 0
    v_t[pl.ds(HD, 16), :] = jnp.where(first, 1.0, 0.0).astype(BF16)

    get_g.wait()
    get_conv.wait()
    gp[pl.ds(8, BF), :] = g_vm[...].astype(F32)
    to_right.wait_recv()
    to_left.wait_recv()
    low = halo_lo[...].astype(F32)[8:16, :]
    gp[pl.ds(0, 8), :] = jnp.where(me > 0, low, 0.0)
    high = halo_hi[...].astype(F32)[0:8, :]
    gp[pl.ds(8 + BF, 8), :] = jnp.where(me < NC - 1, high, 0.0)

    def conv_grad(n):
        cols = pl.ds(mult(n * HD, HD), HD)
        total = gp[pl.ds(8, BF), cols]
        for t in range(KW):
            total = total + conv_vm[pl.ds(t, 1), cols] * gp[pl.ds(12 - t, BF), cols]
        dsub[:, cols] = total.astype(BF16)

    each_slot(conv_grad)
    swap_half(OUT).start()
    own_half(OUT)
    get_wq.start()

    get_w.wait()

    def datt(d):
        rows = pl.ds(mult(peer(d) * HD, HD), HD)
        dat_s[d] = dot_nt(dsub[...], wout_vm[rows, :]).astype(BF16)

        @pl.when(d > 0)
        def _():
            remote(TD, d).start()

    each_slot(datt)
    local(TD).start()

    def turn_in(src, dst):
        def step(n, carry):
            cols = pl.ds(mult(n * BF, BF), BF)
            dst[cols, :] = src[:, cols].T
            return carry

        lax.fori_loop(0, D // BF, step, 0)

    get_li.wait()
    swap_li.wait_recv()
    turn_in(li2, li_t)

    arrived(TK)
    local(TQ).wait()

    def scores(d):
        @pl.when(d > 0)
        def _():
            remote(TQ, d).wait_recv()

        qd = q_aug[slot(d), :]
        top = None
        for b in range(T // KB):
            rows = pl.ds(b * KB, KB)
            s = dot_nt(k_aug[rows, :], qd)
            s_ref[rows, :] = s
            m = jnp.max(s, axis=0, keepdims=True)
            top = m if top is None else jnp.maximum(top, m)
        for b in range(T // KB):
            rows = pl.ds(b * KB, KB)
            e_ref[rows, slot(d)] = jnp.exp2((s_ref[rows, :] - top) * c_exp).astype(BF16)

    each_slot(scores)
    arrived(TV)

    def turn(d):
        k_t[:, slot(d)] = k_aug[slot(d), pl.ds(0, HD)].T
        v_t[pl.ds(0, HD), slot(d)] = v_aug[slot(d), pl.ds(0, HD)].T

    each_slot(turn)

    def attend(d):
        acc = dot(v_t[...], e_ref[:, slot(d)])
        inv = 1.0 / acc[HD : HD + 1, :]
        att_s[d] = (acc[:HD, :] * inv).T.astype(BF16)
        linv_s[d] = jnp.broadcast_to(inv, (HD, BF)).T

        @pl.when(d > 0)
        def _():
            remote(BA, d).start()

    each_slot(attend)
    local(BA).start()

    arrived(TD)

    def backward_in(d):
        do = (do_in[slot(d), :].astype(F32) * linv_s[d]).astype(BF16)
        delta = -jnp.sum(do.astype(F32) * att_s[d].astype(F32), axis=1, keepdims=True)
        hi = delta.astype(BF16).astype(F32)
        do_aug[slot(d), pl.ds(0, HD)] = do
        do_aug[slot(d), pl.ds(HD, HD)] = jnp.where(
            lane == 0, hi, jnp.where(lane == 1, delta - hi, 0.0)
        ).astype(BF16)

    each_slot(backward_in)

    def d_value(j):
        two = pl.ds(mult(j * 2 * BF, 2 * BF), 2 * BF)
        dv_s[pl.ds(j * 2, 2)] = dot(e_ref[two, :], do_aug[:, pl.ds(0, HD)]).astype(BF16).reshape(2, BF, HD)

        @pl.when(j > 0)
        def _():
            remote(BV, j * 2).start()

        remote(BV, j * 2 + 1).start()

    lax.fori_loop(0, NC // 2, lambda j, c: (d_value(j), c)[1], 0)
    local(BV).start()

    def d_query(d):
        dod = do_aug[slot(d), :]
        acc = jnp.zeros((HD, BF), F32)
        for b in range(T // KB):
            rows = pl.ds(b * KB, KB)
            dp = dot_nt(v_aug[rows, :], dod)
            ds = (e_ref[rows, slot(d)].astype(F32) * dp).astype(BF16)
            ds_ref[rows, slot(d)] = ds
            acc = acc + dot(k_t[:, rows], ds)
        dq_s[d] = (acc * inv_root).T.astype(BF16)

        @pl.when(d > 0)
        def _():
            remote(BQ, d).start()

    def product(lhs, start, width):
        def step(zl, carry):
            rows = pl.ds(mult(zl * HALF, HALF), HALF)
            g = dot(lhs[rows, :], r2[:, pl.ds(start, width)]).astype(BF16)
            grads[zl, :, :, :, :, pl.ds(start, width)] = g.reshape(4, 2, 4, 16, width)
            return carry

        lax.fori_loop(0, 2, step, 0)

    def region(fixed, start, width):
        zl = zh = slice(None)
        if "z" in fixed:
            zl, zh = lax.rem(fixed["z"], 2), lax.div(fixed["z"], 2)
        return grads.at[
            zl, fixed.get("y", slice(None)), zh, fixed.get("x", slice(None)), :, pl.ds(start, width)
        ]

    def by_core(total):
        blocks = []
        for c in (0, 1):
            rows = total[..., c * 8 : c * 8 + 8, :]
            h = rows.shape[-1] // 2
            if h >= HD:
                rows = jnp.concatenate([rows[..., :h], rows[..., h:]], axis=-2).astype(BF16)
            blocks.append(rows)
        return jnp.stack(blocks, axis=-3)

    def put_out(part, parts_of):
        start, width, _ = PARTS[part]
        n, inside = divmod(start, HALF)
        out, base = ((dwo_out, 0), (dwq_out, 2 * D), (dwq_out, 0), (dwq_out, D))[n]
        for who, block in zip((core, other), parts_of):
            first = base + who * HALF + inside
            if width > HD:
                h = width // 2
                out[:, pl.ds(mult(first, HD), h)] = block[:8]
                out[:, pl.ds(mult(first + h, HD), h)] = block[8:]
            else:
                out[:, pl.ds(mult(first, HD), HD)] = block

    class Stage:
        def __init__(self, part, stage):
            self.start, self.width, order = PARTS[part]
            self.part = part
            self.axis = order[stage]
            self.fixed = {a: at[a] for a in order[:stage]}
            self.stage = stage

        def piece(self, by, start=0, width=None):
            width = self.width if width is None else width
            fixed = {**self.fixed, self.axis: off(self.axis, by)}
            return region(fixed, self.start + start, width)

        def copy(self, src, dst, by, recv):
            return pltpu.make_async_remote_copy(
                src_ref=src, dst_ref=dst, send_sem=self.send, recv_sem=recv,
                device_id=device(self.axis, off(self.axis, by)), device_id_type=MESH,
            )

        def keep(self, total):
            if self.part == PLANE:
                bufs[self.part * 6 + 4][...] = by_core(total)
            elif self.stage == 0:
                self.piece(0)[...] = total.astype(BF16)
            else:
                bufs[self.part * 6 + 4][...] = by_core(total)

    class Ring(Stage):
        def __init__(self, part):
            super().__init__(part, 0)
            self.ra, self.rb, self.ends = bufs[part * 6 : part * 6 + 3]
            h = self.width // 2
            lead = (slice(None),) * (len(self.ra.shape) - 1)
            low_a, low_b = (0, *lead, pl.ds(0, h)), (0, *lead, pl.ds(h, h))
            high_a, high_b = (1, *lead, pl.ds(0, h)), (1, *lead, pl.ds(h, h))
            self.send = ring_send
            recv = [ring_recv.at[part * 3 + n] for n in range(3)]
            self.copies = [
                self.copy(self.piece(2, 0, h), self.ra, 1, recv[0]),
                self.copy(self.piece(2, h, h), self.rb, 3, recv[1]),
                self.copy(self.piece(1, h, h), self.ends.at[low_b], 1, recv[2]),
                self.copy(self.piece(3, 0, h), self.ends.at[high_a], 3, recv[2]),
                self.copy(self.piece(1, 0, h), self.ends.at[low_a], 1, recv[2]),
                self.copy(self.piece(3, h, h), self.ends.at[high_b], 3, recv[2]),
            ]
            self.recv = recv[2]

        def begin(self):
            for c in self.copies[:4]:
                c.start()

        def relay(self):
            h = self.width // 2
            for n, by, buf, start in ((0, 1, self.ra, 0), (1, 3, self.rb, h)):
                self.copies[n].wait_recv()
                here = self.piece(by, start, h)
                here[...] = (here[...].astype(F32) + buf[...].astype(F32)).astype(BF16)
                self.copies[4 + n].start()

        def end(self):
            whole(self.ends, self.recv)
            here = self.piece(0)[...].astype(F32)
            self.keep(here + (self.ends[0].astype(F32) + self.ends[1].astype(F32)))

    class Direct(Stage):
        def __init__(self, part, stage):
            super().__init__(part, stage)
            self.buf = bufs[part * 6 + (3 if stage else 2)]
            n = part if stage else NP + part
            self.send, self.recv = step_send.at[min(stage, 1)], step_recv.at[n]
            self.copies = [
                self.copy(self.piece(by), self.buf.at[by - 1], by, self.recv) for by in (1, 2, 3)
            ]

        def begin(self):
            for c in self.copies:
                c.start()

        def end(self):
            whole(self.buf, self.recv)
            here = self.piece(0)[...].astype(F32)
            b = [self.buf[n].astype(F32) for n in range(3)]
            self.keep((here + b[0]) + (b[1] + b[2]))

    class Last(Stage):
        def __init__(self, part):
            super().__init__(part, 2)
            self.pair, self.buf = bufs[part * 6 + 4 : part * 6 + 6]
            self.send, self.recv = last_send, last_recv.at[part]
            self.copies = []
            for n, (turned, by) in enumerate((t, b) for t in (0, 1) for b in range(4) if t + b):
                to = lax.rem(core + turned, 2)
                who = device(self.axis, off(self.axis, by), to)
                self.copies.append(
                    pltpu.make_async_remote_copy(
                        src_ref=self.rows(by, to), dst_ref=self.buf.at[n],
                        send_sem=self.send, recv_sem=self.recv,
                        device_id=who, device_id_type=MESH,
                    )
                )

        def rows(self, by, to):
            chip = off(self.axis, by)
            if self.axis == "z":
                return self.pair.at[lax.rem(chip, 2), lax.div(chip, 2), to]
            return self.pair.at[chip, to]

        def begin(self):
            for c in self.copies:
                c.start()

        def end(self):
            whole(self.buf, self.recv)
            b = [self.buf[n].astype(F32) for n in range(7)]
            here = self.rows(0, core)[...].astype(F32)
            put_out(
                self.part,
                ((here + b[0]) + (b[1] + b[2]), (b[3] + b[4]) + (b[5] + b[6])),
            )

    class Plane(Stage):
        def __init__(self, part):
            super().__init__(part, 1)
            self.pair, self.buf = bufs[part * 6 + 4 : part * 6 + 6]
            self.copies = []
            moves = [(t, dz, dy) for t in (0, 1) for dz in range(4) for dy in range(4)]
            for n, (turned, dz, dy) in enumerate(moves[1:]):
                to = lax.rem(core + turned, 2)
                self.copies.append(
                    pltpu.make_async_remote_copy(
                        src_ref=self.rows(dz, dy, to), dst_ref=self.buf.at[n],
                        send_sem=plane_send, recv_sem=plane_recv,
                        device_id=on_plane(off("z", dz), dy, to), device_id_type=MESH,
                    )
                )

        def rows(self, dz, dy, to):
            chip = off("z", dz)
            return self.pair.at[lax.rem(chip, 2), off("y", dy), lax.div(chip, 2), to]

        def begin(self):
            for c in self.copies:
                c.start()

        def end(self):
            whole(self.buf, plane_recv)
            mine_sum = self.rows(0, 0, core)[...].astype(F32)
            for n in range(15):
                mine_sum = mine_sum + self.buf[n].astype(F32)
            their_sum = self.buf[15].astype(F32)
            for n in range(16, 31):
                their_sum = their_sum + self.buf[n].astype(F32)
            put_out(self.part, (mine_sum, their_sum))

    rings = [
        (Ring(p), Plane(p))
        if p == PLANE
        else (Ring(p) if p in RINGS else Direct(p, 0), Direct(p, 1), Last(p))
        for p in range(NP)
    ]

    def on(p, stage):
        rings[p][stage].end()
        rings[p][stage + 1].begin()

    def taps_copy(n, src, dst, who):
        pltpu.make_async_remote_copy(
            src_ref=src, dst_ref=dst, send_sem=taps_send.at[n], recv_sem=taps_recv.at[n],
            device_id=who, device_id_type=MESH,
        ).start()

    def taps_on(n, axis, value):
        here = taps_a.at[n, at[axis]]
        here[...] = value
        for by in (1, 2, 3):
            taps_copy(n, here, here, device(axis, off(axis, by)))

    def taps_last(axis, value):
        here = taps_z.at[core * 4 + at[axis]]
        here[...] = value
        for by in (0, 1, 2, 3):
            if by:
                taps_copy(2, here, here, device(axis, off(axis, by)))
            taps_copy(2, here, here, device(axis, off(axis, by), other))

    def sum_4(ref, n):
        return (ref[n] + ref[n + 1]) + (ref[n + 2] + ref[n + 3])

    def taps_sum(n):
        whole(taps_a.at[n, pl.ds(0, 3)], taps_recv.at[n])
        return sum_4(taps_a.at[n], 0)

    def taps_end():
        whole(taps_z.at[pl.ds(0, 7)], taps_recv.at[2])
        halves = sum_4(taps_z, 0), sum_4(taps_z, 4)
        for t in range(KW):
            block = halves[0][t] if t < 5 else halves[1][t - 4]
            for n in range(D // HD):
                dk_out[t : t + 1, n * HD : (n + 1) * HD] = block[n : n + 1, :]

    def taps(n):
        cols = pl.ds(mult(n * BF, BF), BF)
        sub = dot(att2[mine, :], wout_vm[:, cols]).astype(BF16).astype(F32)
        for t in range(KW):
            total = jnp.sum(sub * gp[pl.ds(12 - t, BF), cols], axis=0, keepdims=True)
            taps_c[t, pl.ds(2 * n, 1), :] = total[:, :HD]
            taps_c[t, pl.ds(2 * n + 1, 1), :] = total[:, HD:]

    def back(t, n):
        arrived(t)
        swap_half(n).start()
        own_half(n)

    def weight(n):
        swap_half(n).wait_recv()
        product(li_t, n * HALF, HALF)

    def d_input(n, carry):
        cols = pl.ds(mult(n * BF, BF), BF)
        din_vm[:, cols] = dot_nt(dqkv[...], wqkv_vm[cols, :]).astype(BF16)
        return carry

    lax.fori_loop(0, 2, lambda d, c: (d_query(d), c)[1], 0)
    arrived(BA)
    swap_att.start()
    lax.fori_loop(2, 4, lambda d, c: (d_query(d), c)[1], 0)

    swap_half(OUT).wait_recv()
    swap_att.wait_recv()
    turn_in(att2, att_t)
    product(att_t, OUT * HALF, HALF)
    rings[0][0].begin()
    lax.fori_loop(4, NC, lambda d, c: (d_query(d), c)[1], 0)
    local(BQ).start()

    def d_key(j):
        two = pl.ds(mult(j * 2 * BF, 2 * BF), 2 * BF)
        dk_s[pl.ds(j * 2, 2)] = (dot(ds_ref[two, :], q_aug[:, pl.ds(0, HD)]) * inv_root).astype(BF16).reshape(2, BF, HD)

        @pl.when(j > 0)
        def _():
            remote(BK, j * 2).start()

        remote(BK, j * 2 + 1).start()

    lax.fori_loop(0, 2, lambda j, c: (d_key(j), c)[1], 0)
    back(BV, VAL)
    rings[0][0].relay()
    lax.fori_loop(2, NC // 2, lambda j, c: (d_key(j), c)[1], 0)
    local(BK).start()
    weight(VAL)
    rings[1][0].begin()
    back(BQ, QUE)
    lax.fori_loop(0, D // BF, lambda n, c: (taps(n), c)[1], 0)
    swap_taps.start()
    weight(QUE)
    rings[2][0].begin()
    rings[3][0].begin()
    swap_taps.wait_recv()
    taps_on(0, "x", taps_c[pl.ds(core * 4, 5)] + taps_p[...])
    get_wq.wait()
    rings[1][0].relay()
    back(BK, KEY)
    lax.fori_loop(0, 2, d_input, 0)
    swap_half(KEY).wait_recv()
    product(li_t, KEY * HALF, HALF // 2)
    rings[4][0].begin()
    rings[2][0].relay()
    rings[3][0].relay()
    product(li_t, KEY * HALF + HALF // 2, HALF // 2)
    rings[5][0].begin()
    rings[6][0].begin()
    taps_on(1, "y", taps_sum(0))
    on(0, 0)
    lax.fori_loop(2, 4, d_input, 0)
    on(1, 0)
    rings[4][0].relay()
    on(2, 0)
    on(3, 0)
    on(5, 0)
    on(6, 0)
    taps_last("z", taps_sum(1))
    on(0, 1)
    on(4, 0)
    on(5, 1)
    on(6, 1)
    on(1, 1)
    on(2, 1)
    on(3, 1)
    whole(att2.at[pl.ds(0, 32), :], halo_send)
    drain(send_sem, 8 * (NC - 1) * BF * HD * 2)
    drain(core_send.at[0], 4 * BF * D * 2)
    swap_taps.wait_send()
    for n in (0, 1):
        whole(taps_a.at[n, pl.ds(0, 3)], taps_send.at[n])
    whole(taps_z.at[pl.ds(0, 7)], taps_send.at[2])
    ring_width = sum(PARTS[p][1] for p in RINGS)
    drain(ring_send, 3 * BF * ring_width * 2)
    drain(step_send.at[0], 3 * BF * (CW - ring_width) * 2)
    rows = 3 * BF // 4 * (CW - PARTS[PLANE][1]) * 2 // (4 * HD)
    whole(q_aug.at[pl.ds(0, rows), :], step_send.at[1])
    for p in (0, 5, 6, 1):
        rings[p][2].end()
    rings[4][1].end()
    for p in (2, 3):
        rings[p][2].end()
    taps_end()
    whole(do_in.at[pl.ds(0, 7 * 8 * CW * 2 // (2 * HD)), :], last_send)
    whole(do_in.at[pl.ds(0, 31 * 16), :], plane_send)


def collect_kernel(*refs):
    ins, outs, sems = refs[:4], refs[4:8], refs[8]
    copies = [pltpu.make_async_copy(a, b, sems.at[n]) for n, (a, b) in enumerate(zip(ins, outs))]
    for c in copies:
        c.start()
    for c in copies:
        c.wait()


def backward(lengths, li, q, k, v, g, conv, wout, wqkv):
    def vm(shape, dtype=BF16):
        return pltpu.VMEM(shape, dtype)

    buffers = []
    for p, (_, width, order) in enumerate(PARTS):
        leads = []
        for stage in range(3):
            sizes = (("zl", 2), ("y", 4), ("zh", 2), ("x", 4))
            leads.append([n for axis, n in sizes if axis[0] not in order[: stage + 1]])
        halves = [(*leads[0], 16, width // 2)] * 2
        sides = 2 if p in RINGS else 3
        buffers += [vm(shape) for shape in (*halves, (sides, *leads[0], 16, width))]
        buffers.append(vm((3, *leads[1], 16, width)))
        block, kind = ((16, width // 2), BF16) if width > HD else ((8, width), F32)
        lead, count = (leads[0], 31) if p == PLANE else (leads[1], 7)
        buffers.append(vm((*lead, 2, *block), kind))
        buffers.append(vm((count, *block), kind))
    dma = pltpu.SemaphoreType.DMA
    outs = (
        jax.ShapeDtypeStruct((BF, D), BF16),
        jax.ShapeDtypeStruct((8, 3 * D), F32),
        jax.ShapeDtypeStruct((8, D), F32),
        jax.ShapeDtypeStruct((KW, D), F32),
    )
    results = pl.pallas_call(
        backward_kernel,
        out_shape=tuple(pltpu.VMEM(o.shape, o.dtype) for o in outs),
        in_specs=[ANY] * 9,
        out_specs=(VM,) * 4,
        scratch_shapes=[
            vm((T, 2 * HD)), vm((T, 2 * HD)), vm((T, 2 * HD)), vm((T, HD)), vm((T, 2 * HD)),
            vm((HD, T)), vm((HD + 16, T)), vm((T, BF), F32), vm((T, T)), vm((T, T)),
            vm((NC, BF, HD)), vm((NC, BF, HD), F32), vm((NC, BF, HD)), vm((NC, BF, HD)),
            vm((NC, BF, HD)), vm((NC, BF, HD)), vm((BF, 3 * D)),
            vm((BF, D)), vm((BF + 16, D), F32), vm((BF, D)), vm((16, D)), vm((16, D)),
            vm((D, D)), vm((D, 3 * D)),
            vm((2 * BF, D)), vm((2 * BF, D)), vm((2 * BF, CW)), vm((D, 2 * BF)), vm((D, 2 * BF)),
            vm((2, 4, 2, 4, 16, CW)),
            vm((KW, 8, HD), F32), vm((5, 8, HD), F32), vm((2, 4, 5, 8, HD), F32), vm((8, 5, 8, HD), F32),
            vm((KW, D), F32), pltpu.SMEM((1,), jnp.int32), *buffers,
            dma(()), dma((8,)), dma((NC,)), dma(()), dma((2,)), dma((6,)), dma((2,)), dma((7,)),
            dma(()), dma((len(RINGS) * 3,)), dma((2,)), dma((2 * NP,)), dma(()), dma((NP,)),
            dma((3,)), dma((3,)), dma(()), dma(()),
        ],
        compiler_params=pltpu.CompilerParams(
            collective_id=0, has_side_effects=True, vmem_limit_bytes=60 * 1024 * 1024
        ),
    )(lengths, li, q, k, v, g, conv, wout, wqkv)
    results = [pltpu.with_memory_space_constraint(r, pltpu.VMEM) for r in results]
    return pl.pallas_call(
        collect_kernel,
        out_shape=outs,
        in_specs=[VM] * 4,
        out_specs=(ANY,) * 4,
        scratch_shapes=[dma((4,))],
    )(*results)


def shards(layer_in, queries, keys, values, lengths, w_qkv, w_out, conv_kernel, grad_out):
    d_input, d_wqkv, d_wout, d_kernel = backward(
        lengths, layer_in[0], queries[0], keys[0], values[0], grad_out[0], conv_kernel, w_out, w_qkv
    )
    return d_input[None], d_wqkv, d_wout, d_kernel


def solution(mesh):
    frames = P("rec", "ctx", None)
    in_specs = (frames, frames, frames, frames, P("rec"), P(), P(), P(), frames)
    out_specs = (frames, P(("ctx", "rec"), None), P(("ctx", "rec"), None), P())
    return jax.shard_map(
        shards, mesh=mesh, in_specs=in_specs, out_specs=out_specs, check_vma=False
    )
```

```python
import math

import jax
import jax.numpy as jnp
from jax import lax
from jax.experimental import pallas as pl
from jax.experimental.pallas import tpu as pltpu
from jax.sharding import PartitionSpec as P

HD = 128
KW = 9
NC = 8
BF = 256
T = NC * BF
D = 1024
F32 = jnp.float32
BF16 = jnp.bfloat16
MESH = pl.DeviceIdType.MESH
KB = 512
NEG = -1e30
NT = (((1,), (1,)), ((), ()))
ANY = pl.BlockSpec(memory_space=pl.ANY)
VM = pl.BlockSpec(memory_space=pltpu.VMEM)

TQ, TK, TV, TD, BA, BQ, BK, BV = range(8)


def mult(value, of):
    return pl.multiple_of(value, of)


def dot(a, b):
    return jnp.dot(a, b, preferred_element_type=F32)


def dot_nt(a, b):
    return lax.dot_general(a, b, NT, preferred_element_type=F32)


HALF = 512
CW = 4 * HALF
OUT, VAL, QUE, KEY = range(4)
PARTS = (
    (0, 512, ("x", "y", "z")),
    (512, 512, ("x", "z", "y")),
    (1024, 256, ("y", "z", "x")),
    (1280, 256, ("z", "x", "y")),
    (1536, 256, ("x", "y", "z")),
    (1792, 128, ("y", "x", "z")),
    (1920, 128, ("z", "x", "y")),
)
PLANE = 4
RINGS = (0, 1, 2, 3, 4)
NP = len(PARTS)


def backward_kernel(
    len_hbm, li_ref, q_ref, k_ref, v_ref, g_ref, conv_ref, wout_ref, wqkv_ref,
    din_vm, dwq_out, dwo_out, dk_out,
    q_aug, k_aug, v_aug, do_in, do_aug, k_t, v_t, s_ref, e_ref, ds_ref,
    att_s, linv_s, dq_s, dk_s, dv_s, dat_s, dqkv,
    g_vm, gp, dsub, halo_lo, halo_hi, wout_vm, wqkv_vm,
    li2, att2, r2, li_t, att_t, grads, taps_c, taps_p, taps_a, taps_z, conv_vm, len_ref, *rest,
):
    bufs = rest[: NP * 6]
    (send_sem, recv_sem, q_recv, halo_send, halo_recv, local_sem, core_send, core_recv,
     ring_send, ring_recv, step_send, step_recv, last_send, last_recv,
     taps_send, taps_recv, plane_send, plane_recv) = rest[NP * 6 :]
    me = lax.axis_index("ctx")
    rec = lax.axis_index("rec")
    z, y = lax.div(me, 4), lax.rem(me, 4)
    inv_root = 1.0 / math.sqrt(HD)
    c_exp = math.log2(math.e) / math.sqrt(HD)

    def peer(d):
        return lax.rem(z + lax.div(d, 4), 2) * 4 + lax.rem(y + lax.rem(d, 4), 4)

    def origin(d):
        return lax.rem(z + 2 - lax.div(d, 4), 2) * 4 + lax.rem(y + 4 - lax.rem(d, 4), 4)

    def head_cols(h):
        return pl.ds(mult(h * HD, HD), HD)

    def slot(d):
        return pl.ds(mult(d * BF, BF), BF)

    fwd_src = {TQ: q_ref, TK: k_ref, TV: v_ref}
    fwd_dst = {TQ: q_aug, TK: k_aug, TV: v_aug, TD: do_in}
    back_src = {BA: att_s, BQ: dq_s, BK: dk_s, BV: dv_s}
    back_base = {BQ: 0, BK: D, BV: 2 * D}

    def ends(t, d):
        if t <= TD:
            p = peer(d)
            src = dat_s.at[d] if t == TD else fwd_src[t].at[:, head_cols(p)]
            dst = fwd_dst[t].at[slot(d), pl.ds(0, HD)]
        else:
            p = origin(d)
            src = back_src[t].at[d]
            if t == BA:
                dst = att2.at[pl.ds(0, BF), head_cols(me)]
            else:
                dst = dqkv.at[:, pl.ds(mult(back_base[t] + me * HD, HD), HD)]
        return p, src, dst

    def remote(t, d):
        p, src, dst = ends(t, d)
        return pltpu.make_async_remote_copy(
            src_ref=src, dst_ref=dst, send_sem=send_sem,
            recv_sem=q_recv.at[d] if t == TQ else recv_sem.at[t],
            device_id=(p, rec), device_id_type=MESH,
        )

    def local(t):
        _, src, dst = ends(t, 0)
        return pltpu.make_async_copy(src, dst, q_recv.at[0] if t == TQ else recv_sem.at[t])

    def whole(ref, sem):
        pltpu.make_async_copy(ref, ref, sem).wait()

    def drain(sem, count):
        whole(e_ref.at[pl.ds(0, count // (2 * T)), :], sem)

    def arrived(t):
        if t <= TD:
            whole(fwd_dst[t].at[:, pl.ds(0, HD)], recv_sem.at[t])
        elif t == BA:
            whole(att2.at[pl.ds(0, BF), :], recv_sem.at[t])
        else:
            whole(dqkv.at[:, pl.ds(back_base[t], D)], recv_sem.at[t])

    def each_peer(body):
        def step(d, carry):
            body(d)
            return carry

        lax.fori_loop(1, NC, step, 0)

    def each_slot(body):
        def step(d, carry):
            body(d)
            return carry

        lax.fori_loop(0, NC, step, 0)

    core = lax.rem(rec, 2)
    other = 1 - core
    at = {"x": lax.rem(lax.div(rec, 2), 4), "y": y, "z": lax.div(rec, 8) * 2 + z}

    def device(moved, to, on_core=core):
        p = {**at, **({moved: to} if moved else {})}
        return (
            lax.rem(p["z"], 2) * 4 + p["y"],
            lax.div(p["z"], 2) * 8 + p["x"] * 2 + on_core,
        )

    def off(axis, by):
        return lax.rem(at[axis] + by, 4)

    partner = device(None, None, other)
    far = lax.rem(lax.div(rec, 8) + 1, 2)
    greet = [partner] + [device("x", off("x", by)) for by in (1, 2, 3)]
    greet += [device("z", far * 2 + zl) for zl in (0, 1)]
    greet += [device(a, off(a, by), other) for a in "xyz" for by in (1, 2, 3)]

    def on_plane(chip_z, by, on_core):
        return (
            lax.rem(chip_z, 2) * 4 + off("y", by),
            lax.div(chip_z, 2) * 8 + at["x"] * 2 + on_core,
        )

    greet += [
        on_plane(chip_z, by, on_core)
        for by in (1, 2, 3)
        for chip_z, on_core in (
            (lax.div(rec, 8) * 2 + 1 - z, other),
            *((far * 2 + zl, c) for zl in (0, 1) for c in (core, other)),
        )
    ]

    barrier = pltpu.get_barrier_semaphore()
    each_peer(
        lambda d: pl.semaphore_signal(barrier, inc=1, device_id=(peer(d), rec), device_id_type=MESH)
    )
    for who in greet:
        pl.semaphore_signal(barrier, inc=1, device_id=who, device_id_type=MESH)
    get_g = pltpu.make_async_copy(g_ref, g_vm, local_sem.at[0])
    get_w = pltpu.make_async_copy(wout_ref, wout_vm, local_sem.at[1])
    get_g.start()
    get_w.start()
    for t in (TK, TQ, TV):
        local(t).start()
    mine, theirs = pl.ds(0, BF), pl.ds(BF, BF)
    get_li = pltpu.make_async_copy(li_ref, li2.at[mine, :], local_sem.at[2])
    get_li.start()
    get_wq = pltpu.make_async_copy(wqkv_ref, wqkv_vm, local_sem.at[3])
    get_conv = pltpu.make_async_copy(conv_ref, conv_vm, local_sem.at[5])
    get_conv.start()
    get_len = pltpu.make_async_copy(len_hbm, len_ref, local_sem.at[4])
    get_len.start()

    pl.semaphore_wait(barrier, NC - 1 + len(greet))

    right, left = lax.rem(me + 1, NC), lax.rem(me + NC - 1, NC)
    to_right = pltpu.make_async_remote_copy(
        src_ref=g_ref.at[pl.ds(BF - 16, 16), :], dst_ref=halo_lo, send_sem=halo_send,
        recv_sem=halo_recv.at[0], device_id=(right, rec), device_id_type=MESH,
    )
    to_left = pltpu.make_async_remote_copy(
        src_ref=g_ref.at[pl.ds(0, 16), :], dst_ref=halo_hi, send_sem=halo_send,
        recv_sem=halo_recv.at[1], device_id=(left, rec), device_id_type=MESH,
    )
    to_right.start()
    to_left.start()
    for t in (TK, TQ, TV):
        each_peer(lambda d: remote(t, d).start())

    def to_partner(n, src, dst):
        return pltpu.make_async_remote_copy(
            src_ref=src, dst_ref=dst, send_sem=core_send.at[n // 6], recv_sem=core_recv.at[n],
            device_id=partner, device_id_type=MESH,
        )

    def half(ref, base, c):
        return ref.at[:, pl.ds(mult(base + c * HALF, HALF), HALF)]

    group = {OUT: (dsub, 0), VAL: (dqkv, 2 * D), QUE: (dqkv, 0), KEY: (dqkv, D)}

    def swap_half(n):
        ref, base = group[n]
        return to_partner(n, half(ref, base, other), r2.at[theirs, pl.ds(n * HALF, HALF)])

    def own_half(n):
        ref, base = group[n]
        r2[mine, pl.ds(n * HALF, HALF)] = half(ref, base, core)[...]

    swap_li = to_partner(4, li_ref, li2.at[theirs, :])
    swap_att = to_partner(5, att2.at[mine, :], att2.at[theirs, :])
    swap_taps = to_partner(6, taps_c.at[pl.ds(other * 4, 5)], taps_p)
    swap_li.start()

    get_len.wait()
    length = len_ref[0]
    lane = lax.broadcasted_iota(jnp.int32, (BF, HD), 1)
    row = lax.broadcasted_iota(jnp.int32, (BF, HD), 0)

    def extra(d):
        masked = (lane == 0) & (row + origin(d) * BF >= length)
        k_aug[slot(d), pl.ds(HD, HD)] = jnp.where(masked, NEG, 0.0).astype(BF16)
        q_aug[slot(d), pl.ds(HD, HD)] = jnp.where(lane == 0, 1.0, 0.0).astype(BF16)
        v_aug[slot(d), pl.ds(HD, HD)] = jnp.where(lane < 2, 1.0, 0.0).astype(BF16)

    each_slot(extra)
    first = lax.broadcasted_iota(jnp.int32, (16, T), 0) == 0
    v_t[pl.ds(HD, 16), :] = jnp.where(first, 1.0, 0.0).astype(BF16)

    get_g.wait()
    get_conv.wait()
    gp[pl.ds(8, BF), :] = g_vm[...].astype(F32)
    to_right.wait_recv()
    to_left.wait_recv()
    low = halo_lo[...].astype(F32)[8:16, :]
    gp[pl.ds(0, 8), :] = jnp.where(me > 0, low, 0.0)
    high = halo_hi[...].astype(F32)[0:8, :]
    gp[pl.ds(8 + BF, 8), :] = jnp.where(me < NC - 1, high, 0.0)

    def conv_grad(n):
        cols = pl.ds(mult(n * HD, HD), HD)
        total = gp[pl.ds(8, BF), cols]
        for t in range(KW):
            total = total + conv_vm[pl.ds(t, 1), cols] * gp[pl.ds(12 - t, BF), cols]
        dsub[:, cols] = total.astype(BF16)

    each_slot(conv_grad)
    swap_half(OUT).start()
    own_half(OUT)
    get_wq.start()

    get_w.wait()

    def datt(d):
        rows = pl.ds(mult(peer(d) * HD, HD), HD)
        dat_s[d] = dot_nt(dsub[...], wout_vm[rows, :]).astype(BF16)

        @pl.when(d > 0)
        def _():
            remote(TD, d).start()

    each_slot(datt)
    local(TD).start()

    def turn_in(src, dst):
        def step(n, carry):
            cols = pl.ds(mult(n * BF, BF), BF)
            dst[cols, :] = src[:, cols].T
            return carry

        lax.fori_loop(0, D // BF, step, 0)

    get_li.wait()
    swap_li.wait_recv()
    turn_in(li2, li_t)

    arrived(TK)
    local(TQ).wait()

    def scores(d):
        @pl.when(d > 0)
        def _():
            remote(TQ, d).wait_recv()

        qd = q_aug[slot(d), :]
        top = None
        for b in range(T // KB):
            rows = pl.ds(b * KB, KB)
            s = dot_nt(k_aug[rows, :], qd)
            s_ref[rows, :] = s
            m = jnp.max(s, axis=0, keepdims=True)
            top = m if top is None else jnp.maximum(top, m)
        for b in range(T // KB):
            rows = pl.ds(b * KB, KB)
            e_ref[rows, slot(d)] = jnp.exp2((s_ref[rows, :] - top) * c_exp).astype(BF16)

    each_slot(scores)
    arrived(TV)

    def turn(d):
        k_t[:, slot(d)] = k_aug[slot(d), pl.ds(0, HD)].T
        v_t[pl.ds(0, HD), slot(d)] = v_aug[slot(d), pl.ds(0, HD)].T

    each_slot(turn)

    def attend(d):
        acc = dot(v_t[...], e_ref[:, slot(d)])
        inv = 1.0 / acc[HD : HD + 1, :]
        att_s[d] = (acc[:HD, :] * inv).T.astype(BF16)
        linv_s[d] = jnp.broadcast_to(inv, (HD, BF)).T

        @pl.when(d > 0)
        def _():
            remote(BA, d).start()

    each_slot(attend)
    local(BA).start()

    arrived(TD)

    def backward_in(d):
        do = (do_in[slot(d), :].astype(F32) * linv_s[d]).astype(BF16)
        delta = -jnp.sum(do.astype(F32) * att_s[d].astype(F32), axis=1, keepdims=True)
        hi = delta.astype(BF16).astype(F32)
        do_aug[slot(d), pl.ds(0, HD)] = do
        do_aug[slot(d), pl.ds(HD, HD)] = jnp.where(
            lane == 0, hi, jnp.where(lane == 1, delta - hi, 0.0)
        ).astype(BF16)

    each_slot(backward_in)

    def d_value(j):
        two = pl.ds(mult(j * 2 * BF, 2 * BF), 2 * BF)
        dv_s[pl.ds(j * 2, 2)] = dot(e_ref[two, :], do_aug[:, pl.ds(0, HD)]).astype(BF16).reshape(2, BF, HD)

        @pl.when(j > 0)
        def _():
            remote(BV, j * 2).start()

        remote(BV, j * 2 + 1).start()

    lax.fori_loop(0, NC // 2, lambda j, c: (d_value(j), c)[1], 0)
    local(BV).start()

    def d_query(d):
        dod = do_aug[slot(d), :]
        acc = jnp.zeros((HD, BF), F32)
        for b in range(T // KB):
            rows = pl.ds(b * KB, KB)
            dp = dot_nt(v_aug[rows, :], dod)
            ds = (e_ref[rows, slot(d)].astype(F32) * dp).astype(BF16)
            ds_ref[rows, slot(d)] = ds
            acc = acc + dot(k_t[:, rows], ds)
        dq_s[d] = (acc * inv_root).T.astype(BF16)

        @pl.when(d > 0)
        def _():
            remote(BQ, d).start()

    def product(lhs, start, width):
        def step(zl, carry):
            rows = pl.ds(mult(zl * HALF, HALF), HALF)
            g = dot(lhs[rows, :], r2[:, pl.ds(start, width)]).astype(BF16)
            grads[zl, :, :, :, :, pl.ds(start, width)] = g.reshape(4, 2, 4, 16, width)
            return carry

        lax.fori_loop(0, 2, step, 0)

    def region(fixed, start, width):
        zl = zh = slice(None)
        if "z" in fixed:
            zl, zh = lax.rem(fixed["z"], 2), lax.div(fixed["z"], 2)
        return grads.at[
            zl, fixed.get("y", slice(None)), zh, fixed.get("x", slice(None)), :, pl.ds(start, width)
        ]

    def by_core(total):
        blocks = []
        for c in (0, 1):
            rows = total[..., c * 8 : c * 8 + 8, :]
            h = rows.shape[-1] // 2
            if h >= HD:
                rows = jnp.concatenate([rows[..., :h], rows[..., h:]], axis=-2).astype(BF16)
            blocks.append(rows)
        return jnp.stack(blocks, axis=-3)

    def put_out(part, parts_of):
        start, width, _ = PARTS[part]
        n, inside = divmod(start, HALF)
        out, base = ((dwo_out, 0), (dwq_out, 2 * D), (dwq_out, 0), (dwq_out, D))[n]
        for who, block in zip((core, other), parts_of):
            first = base + who * HALF + inside
            if width > HD:
                h = width // 2
                out[:, pl.ds(mult(first, HD), h)] = block[:8]
                out[:, pl.ds(mult(first + h, HD), h)] = block[8:]
            else:
                out[:, pl.ds(mult(first, HD), HD)] = block

    class Stage:
        def __init__(self, part, stage):
            self.start, self.width, order = PARTS[part]
            self.part = part
            self.axis = order[stage]
            self.fixed = {a: at[a] for a in order[:stage]}
            self.stage = stage

        def piece(self, by, start=0, width=None):
            width = self.width if width is None else width
            fixed = {**self.fixed, self.axis: off(self.axis, by)}
            return region(fixed, self.start + start, width)

        def copy(self, src, dst, by, recv):
            return pltpu.make_async_remote_copy(
                src_ref=src, dst_ref=dst, send_sem=self.send, recv_sem=recv,
                device_id=device(self.axis, off(self.axis, by)), device_id_type=MESH,
            )

        def keep(self, total):
            if self.part == PLANE:
                bufs[self.part * 6 + 4][...] = by_core(total)
            elif self.stage == 0:
                self.piece(0)[...] = total.astype(BF16)
            else:
                bufs[self.part * 6 + 4][...] = by_core(total)

    class Ring(Stage):
        def __init__(self, part):
            super().__init__(part, 0)
            self.ra, self.rb, self.ends = bufs[part * 6 : part * 6 + 3]
            h = self.width // 2
            lead = (slice(None),) * (len(self.ra.shape) - 1)
            low_a, low_b = (0, *lead, pl.ds(0, h)), (0, *lead, pl.ds(h, h))
            high_a, high_b = (1, *lead, pl.ds(0, h)), (1, *lead, pl.ds(h, h))
            self.send = ring_send
            recv = [ring_recv.at[part * 3 + n] for n in range(3)]
            self.copies = [
                self.copy(self.piece(2, 0, h), self.ra, 1, recv[0]),
                self.copy(self.piece(2, h, h), self.rb, 3, recv[1]),
                self.copy(self.piece(1, h, h), self.ends.at[low_b], 1, recv[2]),
                self.copy(self.piece(3, 0, h), self.ends.at[high_a], 3, recv[2]),
                self.copy(self.piece(1, 0, h), self.ends.at[low_a], 1, recv[2]),
                self.copy(self.piece(3, h, h), self.ends.at[high_b], 3, recv[2]),
            ]
            self.recv = recv[2]

        def begin(self):
            for c in self.copies[:4]:
                c.start()

        def relay(self):
            h = self.width // 2
            for n, by, buf, start in ((0, 1, self.ra, 0), (1, 3, self.rb, h)):
                self.copies[n].wait_recv()
                here = self.piece(by, start, h)
                here[...] = (here[...].astype(F32) + buf[...].astype(F32)).astype(BF16)
                self.copies[4 + n].start()

        def end(self):
            whole(self.ends, self.recv)
            here = self.piece(0)[...].astype(F32)
            self.keep(here + (self.ends[0].astype(F32) + self.ends[1].astype(F32)))

    class Direct(Stage):
        def __init__(self, part, stage):
            super().__init__(part, stage)
            self.buf = bufs[part * 6 + (3 if stage else 2)]
            n = part if stage else NP + part
            self.send, self.recv = step_send.at[min(stage, 1)], step_recv.at[n]
            self.copies = [
                self.copy(self.piece(by), self.buf.at[by - 1], by, self.recv) for by in (1, 2, 3)
            ]

        def begin(self):
            for c in self.copies:
                c.start()

        def end(self):
            whole(self.buf, self.recv)
            here = self.piece(0)[...].astype(F32)
            b = [self.buf[n].astype(F32) for n in range(3)]
            self.keep((here + b[0]) + (b[1] + b[2]))

    class Last(Stage):
        def __init__(self, part):
            super().__init__(part, 2)
            self.pair, self.buf = bufs[part * 6 + 4 : part * 6 + 6]
            self.send, self.recv = last_send, last_recv.at[part]
            self.copies = []
            for n, (turned, by) in enumerate((t, b) for t in (0, 1) for b in range(4) if t + b):
                to = lax.rem(core + turned, 2)
                who = device(self.axis, off(self.axis, by), to)
                self.copies.append(
                    pltpu.make_async_remote_copy(
                        src_ref=self.rows(by, to), dst_ref=self.buf.at[n],
                        send_sem=self.send, recv_sem=self.recv,
                        device_id=who, device_id_type=MESH,
                    )
                )

        def rows(self, by, to):
            chip = off(self.axis, by)
            if self.axis == "z":
                return self.pair.at[lax.rem(chip, 2), lax.div(chip, 2), to]
            return self.pair.at[chip, to]

        def begin(self):
            for c in self.copies:
                c.start()

        def end(self):
            whole(self.buf, self.recv)
            b = [self.buf[n].astype(F32) for n in range(7)]
            here = self.rows(0, core)[...].astype(F32)
            put_out(
                self.part,
                ((here + b[0]) + (b[1] + b[2]), (b[3] + b[4]) + (b[5] + b[6])),
            )

    class Plane(Stage):
        def __init__(self, part):
            super().__init__(part, 1)
            self.pair, self.buf = bufs[part * 6 + 4 : part * 6 + 6]
            self.copies = []
            moves = [(t, dz, dy) for t in (0, 1) for dz in range(4) for dy in range(4)]
            for n, (turned, dz, dy) in enumerate(moves[1:]):
                to = lax.rem(core + turned, 2)
                self.copies.append(
                    pltpu.make_async_remote_copy(
                        src_ref=self.rows(dz, dy, to), dst_ref=self.buf.at[n],
                        send_sem=plane_send, recv_sem=plane_recv,
                        device_id=on_plane(off("z", dz), dy, to), device_id_type=MESH,
                    )
                )

        def rows(self, dz, dy, to):
            chip = off("z", dz)
            return self.pair.at[lax.rem(chip, 2), off("y", dy), lax.div(chip, 2), to]

        def begin(self):
            for c in self.copies:
                c.start()

        def end(self):
            whole(self.buf, plane_recv)
            mine_sum = self.rows(0, 0, core)[...].astype(F32)
            for n in range(15):
                mine_sum = mine_sum + self.buf[n].astype(F32)
            their_sum = self.buf[15].astype(F32)
            for n in range(16, 31):
                their_sum = their_sum + self.buf[n].astype(F32)
            put_out(self.part, (mine_sum, their_sum))

    rings = [
        (Ring(p), Plane(p))
        if p == PLANE
        else (Ring(p) if p in RINGS else Direct(p, 0), Direct(p, 1), Last(p))
        for p in range(NP)
    ]

    def on(p, stage):
        rings[p][stage].end()
        rings[p][stage + 1].begin()

    def taps_copy(n, src, dst, who):
        pltpu.make_async_remote_copy(
            src_ref=src, dst_ref=dst, send_sem=taps_send.at[n], recv_sem=taps_recv.at[n],
            device_id=who, device_id_type=MESH,
        ).start()

    def taps_on(n, axis, value):
        here = taps_a.at[n, at[axis]]
        here[...] = value
        for by in (1, 2, 3):
            taps_copy(n, here, here, device(axis, off(axis, by)))

    def taps_last(axis, value):
        here = taps_z.at[core * 4 + at[axis]]
        here[...] = value
        for by in (0, 1, 2, 3):
            if by:
                taps_copy(2, here, here, device(axis, off(axis, by)))
            taps_copy(2, here, here, device(axis, off(axis, by), other))

    def sum_4(ref, n):
        return (ref[n] + ref[n + 1]) + (ref[n + 2] + ref[n + 3])

    def taps_sum(n):
        whole(taps_a.at[n, pl.ds(0, 3)], taps_recv.at[n])
        return sum_4(taps_a.at[n], 0)

    def taps_end():
        whole(taps_z.at[pl.ds(0, 7)], taps_recv.at[2])
        halves = sum_4(taps_z, 0), sum_4(taps_z, 4)
        for t in range(KW):
            block = halves[0][t] if t < 5 else halves[1][t - 4]
            for n in range(D // HD):
                dk_out[t : t + 1, n * HD : (n + 1) * HD] = block[n : n + 1, :]

    def taps(n):
        cols = pl.ds(mult(n * BF, BF), BF)
        sub = dot(att2[mine, :], wout_vm[:, cols]).astype(BF16).astype(F32)
        for t in range(KW):
            total = jnp.sum(sub * gp[pl.ds(12 - t, BF), cols], axis=0, keepdims=True)
            taps_c[t, pl.ds(2 * n, 1), :] = total[:, :HD]
            taps_c[t, pl.ds(2 * n + 1, 1), :] = total[:, HD:]

    def back(t, n):
        arrived(t)
        swap_half(n).start()
        own_half(n)

    def weight(n):
        swap_half(n).wait_recv()
        product(li_t, n * HALF, HALF)

    def d_input(n, carry):
        cols = pl.ds(mult(n * BF, BF), BF)
        din_vm[:, cols] = dot_nt(dqkv[...], wqkv_vm[cols, :]).astype(BF16)
        return carry

    lax.fori_loop(0, 2, lambda d, c: (d_query(d), c)[1], 0)
    arrived(BA)
    swap_att.start()
    lax.fori_loop(2, 4, lambda d, c: (d_query(d), c)[1], 0)

    swap_half(OUT).wait_recv()
    swap_att.wait_recv()
    turn_in(att2, att_t)
    product(att_t, OUT * HALF, HALF)
    rings[0][0].begin()
    lax.fori_loop(4, NC, lambda d, c: (d_query(d), c)[1], 0)
    local(BQ).start()

    def d_key(j):
        two = pl.ds(mult(j * 2 * BF, 2 * BF), 2 * BF)
        dk_s[pl.ds(j * 2, 2)] = (dot(ds_ref[two, :], q_aug[:, pl.ds(0, HD)]) * inv_root).astype(BF16).reshape(2, BF, HD)

        @pl.when(j > 0)
        def _():
            remote(BK, j * 2).start()

        remote(BK, j * 2 + 1).start()

    lax.fori_loop(0, 2, lambda j, c: (d_key(j), c)[1], 0)
    back(BV, VAL)
    rings[0][0].relay()
    lax.fori_loop(2, NC // 2, lambda j, c: (d_key(j), c)[1], 0)
    local(BK).start()
    weight(VAL)
    rings[1][0].begin()
    back(BQ, QUE)
    lax.fori_loop(0, D // BF, lambda n, c: (taps(n), c)[1], 0)
    swap_taps.start()
    weight(QUE)
    rings[2][0].begin()
    rings[3][0].begin()
    swap_taps.wait_recv()
    taps_on(0, "x", taps_c[pl.ds(core * 4, 5)] + taps_p[...])
    get_wq.wait()
    rings[1][0].relay()
    back(BK, KEY)
    lax.fori_loop(0, 2, d_input, 0)
    swap_half(KEY).wait_recv()
    product(li_t, KEY * HALF, HALF // 2)
    rings[4][0].begin()
    rings[2][0].relay()
    rings[3][0].relay()
    product(li_t, KEY * HALF + HALF // 2, HALF // 2)
    rings[5][0].begin()
    rings[6][0].begin()
    taps_on(1, "y", taps_sum(0))
    on(0, 0)
    lax.fori_loop(2, 4, d_input, 0)
    on(1, 0)
    rings[4][0].relay()
    on(2, 0)
    on(3, 0)
    on(5, 0)
    on(6, 0)
    taps_last("z", taps_sum(1))
    on(0, 1)
    on(4, 0)
    on(5, 1)
    on(6, 1)
    on(1, 1)
    on(2, 1)
    on(3, 1)
    whole(att2.at[pl.ds(0, 32), :], halo_send)
    drain(send_sem, 8 * (NC - 1) * BF * HD * 2)
    drain(core_send.at[0], 4 * BF * D * 2)
    swap_taps.wait_send()
    for n in (0, 1):
        whole(taps_a.at[n, pl.ds(0, 3)], taps_send.at[n])
    whole(taps_z.at[pl.ds(0, 7)], taps_send.at[2])
    ring_width = sum(PARTS[p][1] for p in RINGS)
    drain(ring_send, 3 * BF * ring_width * 2)
    drain(step_send.at[0], 3 * BF * (CW - ring_width) * 2)
    rows = 3 * BF // 4 * (CW - PARTS[PLANE][1]) * 2 // (4 * HD)
    whole(q_aug.at[pl.ds(0, rows), :], step_send.at[1])
    for p in (0, 5, 6, 1):
        rings[p][2].end()
    rings[4][1].end()
    for p in (2, 3):
        rings[p][2].end()
    taps_end()
    whole(do_in.at[pl.ds(0, 7 * 8 * CW * 2 // (2 * HD)), :], last_send)
    whole(do_in.at[pl.ds(0, 31 * 16), :], plane_send)


def collect_kernel(*refs):
    ins, outs, sems = refs[:4], refs[4:8], refs[8]
    copies = [pltpu.make_async_copy(a, b, sems.at[n]) for n, (a, b) in enumerate(zip(ins, outs))]
    for c in copies:
        c.start()
    for c in copies:
        c.wait()


def backward(lengths, li, q, k, v, g, conv, wout, wqkv):
    def vm(shape, dtype=BF16):
        return pltpu.VMEM(shape, dtype)

    buffers = []
    for p, (_, width, order) in enumerate(PARTS):
        leads = []
        for stage in range(3):
            sizes = (("zl", 2), ("y", 4), ("zh", 2), ("x", 4))
            leads.append([n for axis, n in sizes if axis[0] not in order[: stage + 1]])
        halves = [(*leads[0], 16, width // 2)] * 2
        sides = 2 if p in RINGS else 3
        buffers += [vm(shape) for shape in (*halves, (sides, *leads[0], 16, width))]
        buffers.append(vm((3, *leads[1], 16, width)))
        block, kind = ((16, width // 2), BF16) if width > HD else ((8, width), F32)
        lead, count = (leads[0], 31) if p == PLANE else (leads[1], 7)
        buffers.append(vm((*lead, 2, *block), kind))
        buffers.append(vm((count, *block), kind))
    dma = pltpu.SemaphoreType.DMA
    outs = (
        jax.ShapeDtypeStruct((BF, D), BF16),
        jax.ShapeDtypeStruct((8, 3 * D), F32),
        jax.ShapeDtypeStruct((8, D), F32),
        jax.ShapeDtypeStruct((KW, D), F32),
    )
    results = pl.pallas_call(
        backward_kernel,
        out_shape=tuple(pltpu.VMEM(o.shape, o.dtype) for o in outs),
        in_specs=[ANY] * 9,
        out_specs=(VM,) * 4,
        scratch_shapes=[
            vm((T, 2 * HD)), vm((T, 2 * HD)), vm((T, 2 * HD)), vm((T, HD)), vm((T, 2 * HD)),
            vm((HD, T)), vm((HD + 16, T)), vm((T, BF), F32), vm((T, T)), vm((T, T)),
            vm((NC, BF, HD)), vm((NC, BF, HD), F32), vm((NC, BF, HD)), vm((NC, BF, HD)),
            vm((NC, BF, HD)), vm((NC, BF, HD)), vm((BF, 3 * D)),
            vm((BF, D)), vm((BF + 16, D), F32), vm((BF, D)), vm((16, D)), vm((16, D)),
            vm((D, D)), vm((D, 3 * D)),
            vm((2 * BF, D)), vm((2 * BF, D)), vm((2 * BF, CW)), vm((D, 2 * BF)), vm((D, 2 * BF)),
            vm((2, 4, 2, 4, 16, CW)),
            vm((KW, 8, HD), F32), vm((5, 8, HD), F32), vm((2, 4, 5, 8, HD), F32), vm((8, 5, 8, HD), F32),
            vm((KW, D), F32), pltpu.SMEM((1,), jnp.int32), *buffers,
            dma(()), dma((8,)), dma((NC,)), dma(()), dma((2,)), dma((6,)), dma((2,)), dma((7,)),
            dma(()), dma((len(RINGS) * 3,)), dma((2,)), dma((2 * NP,)), dma(()), dma((NP,)),
            dma((3,)), dma((3,)), dma(()), dma(()),
        ],
        compiler_params=pltpu.CompilerParams(
            collective_id=0, has_side_effects=True, vmem_limit_bytes=60 * 1024 * 1024
        ),
    )(lengths, li, q, k, v, g, conv, wout, wqkv)
    results = [pltpu.with_memory_space_constraint(r, pltpu.VMEM) for r in results]
    return pl.pallas_call(
        collect_kernel,
        out_shape=outs,
        in_specs=[VM] * 4,
        out_specs=(ANY,) * 4,
        scratch_shapes=[dma((4,))],
    )(*results)


def shards(layer_in, queries, keys, values, lengths, w_qkv, w_out, conv_kernel, grad_out):
    d_input, d_wqkv, d_wout, d_kernel = backward(
        lengths, layer_in[0], queries[0], keys[0], values[0], grad_out[0], conv_kernel, w_out, w_qkv
    )
    return d_input[None], d_wqkv, d_wout, d_kernel


def solution(mesh):
    frames = P("rec", "ctx", None)
    in_specs = (frames, frames, frames, frames, P("rec"), P(), P(), P(), frames)
    out_specs = (frames, P(("ctx", "rec"), None), P(("ctx", "rec"), None), P())
    return jax.shard_map(
        shards, mesh=mesh, in_specs=in_specs, out_specs=out_specs, check_vma=False
    )
```

```python
import math

import jax
import jax.numpy as jnp
from jax import lax
from jax.experimental import pallas as pl
from jax.experimental.pallas import tpu as pltpu
from jax.sharding import PartitionSpec as P

HD = 128
KW = 9
NC = 8
BF = 256
T = NC * BF
D = 1024
F32 = jnp.float32
BF16 = jnp.bfloat16
MESH = pl.DeviceIdType.MESH
KB = 512
NEG = -1e30
NT = (((1,), (1,)), ((), ()))
ANY = pl.BlockSpec(memory_space=pl.ANY)
VM = pl.BlockSpec(memory_space=pltpu.VMEM)

TQ, TK, TV, TD, BA, BQ, BK, BV = range(8)


def mult(value, of):
    return pl.multiple_of(value, of)


def dot(a, b):
    return jnp.dot(a, b, preferred_element_type=F32)


def dot_nt(a, b):
    return lax.dot_general(a, b, NT, preferred_element_type=F32)


HALF = 512
CW = 4 * HALF
OUT, VAL, QUE, KEY = range(4)
PARTS = (
    (0, 512, ("x", "y", "z")),
    (512, 512, ("x", "z", "y")),
    (1024, 256, ("y", "z", "x")),
    (1280, 256, ("z", "x", "y")),
    (1536, 256, ("x", "y", "z")),
    (1792, 128, ("y", "x", "z")),
    (1920, 128, ("z", "x", "y")),
)
PLANE = 4
RINGS = (0, 1, 2, 3, 4)
NP = len(PARTS)


def backward_kernel(
    len_hbm, li_ref, q_ref, k_ref, v_ref, g_ref, conv_ref, wout_ref, wqkv_ref,
    din_vm, dwq_out, dwo_out, dk_out,
    q_aug, k_aug, v_aug, do_in, do_aug, k_t, v_t, s_ref, e_ref, ds_ref,
    att_s, linv_s, dq_s, dk_s, dv_s, dat_s, dqkv,
    g_vm, gp, dsub, halo_lo, halo_hi, wout_vm, wqkv_vm,
    li2, att2, r2, li_t, att_t, grads, taps_c, taps_p, taps_a, taps_z, conv_vm, len_ref, *rest,
):
    bufs = rest[: NP * 6]
    (send_sem, recv_sem, q_recv, halo_send, halo_recv, local_sem, core_send, core_recv,
     ring_send, ring_recv, step_send, step_recv, last_send, last_recv,
     taps_send, taps_recv, plane_send, plane_recv) = rest[NP * 6 :]
    me = lax.axis_index("ctx")
    rec = lax.axis_index("rec")
    z, y = lax.div(me, 4), lax.rem(me, 4)
    inv_root = 1.0 / math.sqrt(HD)
    c_exp = math.log2(math.e) / math.sqrt(HD)

    def peer(d):
        return lax.rem(z + lax.div(d, 4), 2) * 4 + lax.rem(y + lax.rem(d, 4), 4)

    def origin(d):
        return lax.rem(z + 2 - lax.div(d, 4), 2) * 4 + lax.rem(y + 4 - lax.rem(d, 4), 4)

    def head_cols(h):
        return pl.ds(mult(h * HD, HD), HD)

    def slot(d):
        return pl.ds(mult(d * BF, BF), BF)

    fwd_src = {TQ: q_ref, TK: k_ref, TV: v_ref}
    fwd_dst = {TQ: q_aug, TK: k_aug, TV: v_aug, TD: do_in}
    back_src = {BA: att_s, BQ: dq_s, BK: dk_s, BV: dv_s}
    back_base = {BQ: 0, BK: D, BV: 2 * D}

    def ends(t, d):
        if t <= TD:
            p = peer(d)
            src = dat_s.at[d] if t == TD else fwd_src[t].at[:, head_cols(p)]
            dst = fwd_dst[t].at[slot(d), pl.ds(0, HD)]
        else:
            p = origin(d)
            src = back_src[t].at[d]
            if t == BA:
                dst = att2.at[pl.ds(0, BF), head_cols(me)]
            else:
                dst = dqkv.at[:, pl.ds(mult(back_base[t] + me * HD, HD), HD)]
        return p, src, dst

    def remote(t, d):
        p, src, dst = ends(t, d)
        return pltpu.make_async_remote_copy(
            src_ref=src, dst_ref=dst, send_sem=send_sem,
            recv_sem=q_recv.at[d] if t == TQ else recv_sem.at[t],
            device_id=(p, rec), device_id_type=MESH,
        )

    def local(t):
        _, src, dst = ends(t, 0)
        return pltpu.make_async_copy(src, dst, q_recv.at[0] if t == TQ else recv_sem.at[t])

    def whole(ref, sem):
        pltpu.make_async_copy(ref, ref, sem).wait()

    def drain(sem, count):
        whole(e_ref.at[pl.ds(0, count // (2 * T)), :], sem)

    def arrived(t):
        if t <= TD:
            whole(fwd_dst[t].at[:, pl.ds(0, HD)], recv_sem.at[t])
        elif t == BA:
            whole(att2.at[pl.ds(0, BF), :], recv_sem.at[t])
        else:
            whole(dqkv.at[:, pl.ds(back_base[t], D)], recv_sem.at[t])

    def each_peer(body):
        def step(d, carry):
            body(d)
            return carry

        lax.fori_loop(1, NC, step, 0)

    def each_slot(body):
        def step(d, carry):
            body(d)
            return carry

        lax.fori_loop(0, NC, step, 0)

    core = lax.rem(rec, 2)
    other = 1 - core
    at = {"x": lax.rem(lax.div(rec, 2), 4), "y": y, "z": lax.div(rec, 8) * 2 + z}

    def device(moved, to, on_core=core):
        p = {**at, **({moved: to} if moved else {})}
        return (
            lax.rem(p["z"], 2) * 4 + p["y"],
            lax.div(p["z"], 2) * 8 + p["x"] * 2 + on_core,
        )

    def off(axis, by):
        return lax.rem(at[axis] + by, 4)

    partner = device(None, None, other)
    far = lax.rem(lax.div(rec, 8) + 1, 2)
    greet = [partner] + [device("x", off("x", by)) for by in (1, 2, 3)]
    greet += [device("z", far * 2 + zl) for zl in (0, 1)]
    greet += [device(a, off(a, by), other) for a in "xyz" for by in (1, 2, 3)]

    def on_plane(chip_z, by, on_core):
        return (
            lax.rem(chip_z, 2) * 4 + off("y", by),
            lax.div(chip_z, 2) * 8 + at["x"] * 2 + on_core,
        )

    greet += [
        on_plane(chip_z, by, on_core)
        for by in (1, 2, 3)
        for chip_z, on_core in (
            (lax.div(rec, 8) * 2 + 1 - z, other),
            *((far * 2 + zl, c) for zl in (0, 1) for c in (core, other)),
        )
    ]

    barrier = pltpu.get_barrier_semaphore()
    each_peer(
        lambda d: pl.semaphore_signal(barrier, inc=1, device_id=(peer(d), rec), device_id_type=MESH)
    )
    for who in greet:
        pl.semaphore_signal(barrier, inc=1, device_id=who, device_id_type=MESH)
    get_g = pltpu.make_async_copy(g_ref, g_vm, local_sem.at[0])
    get_w = pltpu.make_async_copy(wout_ref, wout_vm, local_sem.at[1])
    get_g.start()
    get_w.start()
    for t in (TK, TQ, TV):
        local(t).start()
    mine, theirs = pl.ds(0, BF), pl.ds(BF, BF)
    get_li = pltpu.make_async_copy(li_ref, li2.at[mine, :], local_sem.at[2])
    get_li.start()
    get_wq = pltpu.make_async_copy(wqkv_ref, wqkv_vm, local_sem.at[3])
    get_conv = pltpu.make_async_copy(conv_ref, conv_vm, local_sem.at[5])
    get_conv.start()
    get_len = pltpu.make_async_copy(len_hbm, len_ref, local_sem.at[4])
    get_len.start()

    pl.semaphore_wait(barrier, NC - 1 + len(greet))

    right, left = lax.rem(me + 1, NC), lax.rem(me + NC - 1, NC)
    to_right = pltpu.make_async_remote_copy(
        src_ref=g_ref.at[pl.ds(BF - 16, 16), :], dst_ref=halo_lo, send_sem=halo_send,
        recv_sem=halo_recv.at[0], device_id=(right, rec), device_id_type=MESH,
    )
    to_left = pltpu.make_async_remote_copy(
        src_ref=g_ref.at[pl.ds(0, 16), :], dst_ref=halo_hi, send_sem=halo_send,
        recv_sem=halo_recv.at[1], device_id=(left, rec), device_id_type=MESH,
    )
    to_right.start()
    to_left.start()
    for t in (TK, TQ, TV):
        each_peer(lambda d: remote(t, d).start())

    def to_partner(n, src, dst):
        return pltpu.make_async_remote_copy(
            src_ref=src, dst_ref=dst, send_sem=core_send.at[n // 6], recv_sem=core_recv.at[n],
            device_id=partner, device_id_type=MESH,
        )

    def half(ref, base, c):
        return ref.at[:, pl.ds(mult(base + c * HALF, HALF), HALF)]

    group = {OUT: (dsub, 0), VAL: (dqkv, 2 * D), QUE: (dqkv, 0), KEY: (dqkv, D)}

    def swap_half(n):
        ref, base = group[n]
        return to_partner(n, half(ref, base, other), r2.at[theirs, pl.ds(n * HALF, HALF)])

    def own_half(n):
        ref, base = group[n]
        r2[mine, pl.ds(n * HALF, HALF)] = half(ref, base, core)[...]

    swap_li = to_partner(4, li_ref, li2.at[theirs, :])
    swap_att = to_partner(5, att2.at[mine, :], att2.at[theirs, :])
    swap_taps = to_partner(6, taps_c.at[pl.ds(other * 4, 5)], taps_p)
    swap_li.start()

    get_len.wait()
    length = len_ref[0]
    lane = lax.broadcasted_iota(jnp.int32, (BF, HD), 1)
    row = lax.broadcasted_iota(jnp.int32, (BF, HD), 0)

    def extra(d):
        masked = (lane == 0) & (row + origin(d) * BF >= length)
        k_aug[slot(d), pl.ds(HD, HD)] = jnp.where(masked, NEG, 0.0).astype(BF16)
        q_aug[slot(d), pl.ds(HD, HD)] = jnp.where(lane == 0, 1.0, 0.0).astype(BF16)
        v_aug[slot(d), pl.ds(HD, HD)] = jnp.where(lane < 2, 1.0, 0.0).astype(BF16)

    each_slot(extra)
    first = lax.broadcasted_iota(jnp.int32, (16, T), 0) == 0
    v_t[pl.ds(HD, 16), :] = jnp.where(first, 1.0, 0.0).astype(BF16)

    get_g.wait()
    get_conv.wait()
    gp[pl.ds(8, BF), :] = g_vm[...].astype(F32)
    to_right.wait_recv()
    to_left.wait_recv()
    low = halo_lo[...].astype(F32)[8:16, :]
    gp[pl.ds(0, 8), :] = jnp.where(me > 0, low, 0.0)
    high = halo_hi[...].astype(F32)[0:8, :]
    gp[pl.ds(8 + BF, 8), :] = jnp.where(me < NC - 1, high, 0.0)

    def conv_grad(n):
        cols = pl.ds(mult(n * HD, HD), HD)
        total = gp[pl.ds(8, BF), cols]
        for t in range(KW):
            total = total + conv_vm[pl.ds(t, 1), cols] * gp[pl.ds(12 - t, BF), cols]
        dsub[:, cols] = total.astype(BF16)

    each_slot(conv_grad)
    swap_half(OUT).start()
    own_half(OUT)
    get_wq.start()

    get_w.wait()

    def datt(d):
        rows = pl.ds(mult(peer(d) * HD, HD), HD)
        dat_s[d] = dot_nt(dsub[...], wout_vm[rows, :]).astype(BF16)

        @pl.when(d > 0)
        def _():
            remote(TD, d).start()

    each_slot(datt)
    local(TD).start()

    def turn_in(src, dst):
        def step(n, carry):
            cols = pl.ds(mult(n * BF, BF), BF)
            dst[cols, :] = src[:, cols].T
            return carry

        lax.fori_loop(0, D // BF, step, 0)

    get_li.wait()
    swap_li.wait_recv()
    turn_in(li2, li_t)

    arrived(TK)
    local(TQ).wait()

    def scores(d):
        @pl.when(d > 0)
        def _():
            remote(TQ, d).wait_recv()

        qd = q_aug[slot(d), :]
        top = None
        for b in range(T // KB):
            rows = pl.ds(b * KB, KB)
            s = dot_nt(k_aug[rows, :], qd)
            s_ref[rows, :] = s
            m = jnp.max(s, axis=0, keepdims=True)
            top = m if top is None else jnp.maximum(top, m)
        for b in range(T // KB):
            rows = pl.ds(b * KB, KB)
            e_ref[rows, slot(d)] = jnp.exp2((s_ref[rows, :] - top) * c_exp).astype(BF16)

    each_slot(scores)
    arrived(TV)

    def turn(d):
        k_t[:, slot(d)] = k_aug[slot(d), pl.ds(0, HD)].T
        v_t[pl.ds(0, HD), slot(d)] = v_aug[slot(d), pl.ds(0, HD)].T

    each_slot(turn)

    def attend(d):
        acc = dot(v_t[...], e_ref[:, slot(d)])
        inv = 1.0 / acc[HD : HD + 1, :]
        att_s[d] = (acc[:HD, :] * inv).T.astype(BF16)
        linv_s[d] = jnp.broadcast_to(inv, (HD, BF)).T

        @pl.when(d > 0)
        def _():
            remote(BA, d).start()

    each_slot(attend)
    local(BA).start()

    arrived(TD)

    def backward_in(d):
        do = (do_in[slot(d), :].astype(F32) * linv_s[d]).astype(BF16)
        delta = -jnp.sum(do.astype(F32) * att_s[d].astype(F32), axis=1, keepdims=True)
        hi = delta.astype(BF16).astype(F32)
        do_aug[slot(d), pl.ds(0, HD)] = do
        do_aug[slot(d), pl.ds(HD, HD)] = jnp.where(
            lane == 0, hi, jnp.where(lane == 1, delta - hi, 0.0)
        ).astype(BF16)

    each_slot(backward_in)

    def d_value(j):
        two = pl.ds(mult(j * 2 * BF, 2 * BF), 2 * BF)
        dv_s[pl.ds(j * 2, 2)] = dot(e_ref[two, :], do_aug[:, pl.ds(0, HD)]).astype(BF16).reshape(2, BF, HD)

        @pl.when(j > 0)
        def _():
            remote(BV, j * 2).start()

        remote(BV, j * 2 + 1).start()

    lax.fori_loop(0, NC // 2, lambda j, c: (d_value(j), c)[1], 0)
    local(BV).start()

    def d_query(d):
        dod = do_aug[slot(d), :]
        acc = jnp.zeros((HD, BF), F32)
        for b in range(T // KB):
            rows = pl.ds(b * KB, KB)
            dp = dot_nt(v_aug[rows, :], dod)
            ds = (e_ref[rows, slot(d)].astype(F32) * dp).astype(BF16)
            ds_ref[rows, slot(d)] = ds
            acc = acc + dot(k_t[:, rows], ds)
        dq_s[d] = (acc * inv_root).T.astype(BF16)

        @pl.when(d > 0)
        def _():
            remote(BQ, d).start()

    def product(lhs, start, width):
        def step(zl, carry):
            rows = pl.ds(mult(zl * HALF, HALF), HALF)
            g = dot(lhs[rows, :], r2[:, pl.ds(start, width)]).astype(BF16)
            grads[zl, :, :, :, :, pl.ds(start, width)] = g.reshape(4, 2, 4, 16, width)
            return carry

        lax.fori_loop(0, 2, step, 0)

    def region(fixed, start, width):
        zl = zh = slice(None)
        if "z" in fixed:
            zl, zh = lax.rem(fixed["z"], 2), lax.div(fixed["z"], 2)
        return grads.at[
            zl, fixed.get("y", slice(None)), zh, fixed.get("x", slice(None)), :, pl.ds(start, width)
        ]

    def by_core(total):
        blocks = []
        for c in (0, 1):
            rows = total[..., c * 8 : c * 8 + 8, :]
            h = rows.shape[-1] // 2
            if h >= HD:
                rows = jnp.concatenate([rows[..., :h], rows[..., h:]], axis=-2).astype(BF16)
            blocks.append(rows)
        return jnp.stack(blocks, axis=-3)

    def put_out(part, parts_of):
        start, width, _ = PARTS[part]
        n, inside = divmod(start, HALF)
        out, base = ((dwo_out, 0), (dwq_out, 2 * D), (dwq_out, 0), (dwq_out, D))[n]
        for who, block in zip((core, other), parts_of):
            first = base + who * HALF + inside
            if width > HD:
                h = width // 2
                out[:, pl.ds(mult(first, HD), h)] = block[:8]
                out[:, pl.ds(mult(first + h, HD), h)] = block[8:]
            else:
                out[:, pl.ds(mult(first, HD), HD)] = block

    class Stage:
        def __init__(self, part, stage):
            self.start, self.width, order = PARTS[part]
            self.part = part
            self.axis = order[stage]
            self.fixed = {a: at[a] for a in order[:stage]}
            self.stage = stage

        def piece(self, by, start=0, width=None):
            width = self.width if width is None else width
            fixed = {**self.fixed, self.axis: off(self.axis, by)}
            return region(fixed, self.start + start, width)

        def copy(self, src, dst, by, recv):
            return pltpu.make_async_remote_copy(
                src_ref=src, dst_ref=dst, send_sem=self.send, recv_sem=recv,
                device_id=device(self.axis, off(self.axis, by)), device_id_type=MESH,
            )

        def keep(self, total):
            if self.part == PLANE:
                bufs[self.part * 6 + 4][...] = by_core(total)
            elif self.stage == 0:
                self.piece(0)[...] = total.astype(BF16)
            else:
                bufs[self.part * 6 + 4][...] = by_core(total)

    class Ring(Stage):
        def __init__(self, part):
            super().__init__(part, 0)
            self.ra, self.rb, self.ends = bufs[part * 6 : part * 6 + 3]
            h = self.width // 2
            lead = (slice(None),) * (len(self.ra.shape) - 1)
            low_a, low_b = (0, *lead, pl.ds(0, h)), (0, *lead, pl.ds(h, h))
            high_a, high_b = (1, *lead, pl.ds(0, h)), (1, *lead, pl.ds(h, h))
            self.send = ring_send
            recv = [ring_recv.at[part * 3 + n] for n in range(3)]
            self.copies = [
                self.copy(self.piece(2, 0, h), self.ra, 1, recv[0]),
                self.copy(self.piece(2, h, h), self.rb, 3, recv[1]),
                self.copy(self.piece(1, h, h), self.ends.at[low_b], 1, recv[2]),
                self.copy(self.piece(3, 0, h), self.ends.at[high_a], 3, recv[2]),
                self.copy(self.piece(1, 0, h), self.ends.at[low_a], 1, recv[2]),
                self.copy(self.piece(3, h, h), self.ends.at[high_b], 3, recv[2]),
            ]
            self.recv = recv[2]

        def begin(self):
            for c in self.copies[:4]:
                c.start()

        def relay(self):
            h = self.width // 2
            for n, by, buf, start in ((0, 1, self.ra, 0), (1, 3, self.rb, h)):
                self.copies[n].wait_recv()
                here = self.piece(by, start, h)
                here[...] = (here[...].astype(F32) + buf[...].astype(F32)).astype(BF16)
                self.copies[4 + n].start()

        def end(self):
            whole(self.ends, self.recv)
            here = self.piece(0)[...].astype(F32)
            self.keep(here + (self.ends[0].astype(F32) + self.ends[1].astype(F32)))

    class Direct(Stage):
        def __init__(self, part, stage):
            super().__init__(part, stage)
            self.buf = bufs[part * 6 + (3 if stage else 2)]
            n = part if stage else NP + part
            self.send, self.recv = step_send.at[min(stage, 1)], step_recv.at[n]
            self.copies = [
                self.copy(self.piece(by), self.buf.at[by - 1], by, self.recv) for by in (1, 2, 3)
            ]

        def begin(self):
            for c in self.copies:
                c.start()

        def end(self):
            whole(self.buf, self.recv)
            here = self.piece(0)[...].astype(F32)
            b = [self.buf[n].astype(F32) for n in range(3)]
            self.keep((here + b[0]) + (b[1] + b[2]))

    class Last(Stage):
        def __init__(self, part):
            super().__init__(part, 2)
            self.pair, self.buf = bufs[part * 6 + 4 : part * 6 + 6]
            self.send, self.recv = last_send, last_recv.at[part]
            self.copies = []
            for n, (turned, by) in enumerate((t, b) for t in (0, 1) for b in range(4) if t + b):
                to = lax.rem(core + turned, 2)
                who = device(self.axis, off(self.axis, by), to)
                self.copies.append(
                    pltpu.make_async_remote_copy(
                        src_ref=self.rows(by, to), dst_ref=self.buf.at[n],
                        send_sem=self.send, recv_sem=self.recv,
                        device_id=who, device_id_type=MESH,
                    )
                )

        def rows(self, by, to):
            chip = off(self.axis, by)
            if self.axis == "z":
                return self.pair.at[lax.rem(chip, 2), lax.div(chip, 2), to]
            return self.pair.at[chip, to]

        def begin(self):
            for c in self.copies:
                c.start()

        def end(self):
            whole(self.buf, self.recv)
            b = [self.buf[n].astype(F32) for n in range(7)]
            here = self.rows(0, core)[...].astype(F32)
            put_out(
                self.part,
                ((here + b[0]) + (b[1] + b[2]), (b[3] + b[4]) + (b[5] + b[6])),
            )

    class Plane(Stage):
        def __init__(self, part):
            super().__init__(part, 1)
            self.pair, self.buf = bufs[part * 6 + 4 : part * 6 + 6]
            self.copies = []
            moves = [(t, dz, dy) for t in (0, 1) for dz in range(4) for dy in range(4)]
            for n, (turned, dz, dy) in enumerate(moves[1:]):
                to = lax.rem(core + turned, 2)
                self.copies.append(
                    pltpu.make_async_remote_copy(
                        src_ref=self.rows(dz, dy, to), dst_ref=self.buf.at[n],
                        send_sem=plane_send, recv_sem=plane_recv,
                        device_id=on_plane(off("z", dz), dy, to), device_id_type=MESH,
                    )
                )

        def rows(self, dz, dy, to):
            chip = off("z", dz)
            return self.pair.at[lax.rem(chip, 2), off("y", dy), lax.div(chip, 2), to]

        def begin(self):
            for c in self.copies:
                c.start()

        def end(self):
            whole(self.buf, plane_recv)
            mine_sum = self.rows(0, 0, core)[...].astype(F32)
            for n in range(15):
                mine_sum = mine_sum + self.buf[n].astype(F32)
            their_sum = self.buf[15].astype(F32)
            for n in range(16, 31):
                their_sum = their_sum + self.buf[n].astype(F32)
            put_out(self.part, (mine_sum, their_sum))

    rings = [
        (Ring(p), Plane(p))
        if p == PLANE
        else (Ring(p) if p in RINGS else Direct(p, 0), Direct(p, 1), Last(p))
        for p in range(NP)
    ]

    def on(p, stage):
        rings[p][stage].end()
        rings[p][stage + 1].begin()

    def taps_copy(n, src, dst, who):
        pltpu.make_async_remote_copy(
            src_ref=src, dst_ref=dst, send_sem=taps_send.at[n], recv_sem=taps_recv.at[n],
            device_id=who, device_id_type=MESH,
        ).start()

    def taps_on(n, axis, value):
        here = taps_a.at[n, at[axis]]
        here[...] = value
        for by in (1, 2, 3):
            taps_copy(n, here, here, device(axis, off(axis, by)))

    def taps_last(axis, value):
        here = taps_z.at[core * 4 + at[axis]]
        here[...] = value
        for by in (0, 1, 2, 3):
            if by:
                taps_copy(2, here, here, device(axis, off(axis, by)))
            taps_copy(2, here, here, device(axis, off(axis, by), other))

    def sum_4(ref, n):
        return (ref[n] + ref[n + 1]) + (ref[n + 2] + ref[n + 3])

    def taps_sum(n):
        whole(taps_a.at[n, pl.ds(0, 3)], taps_recv.at[n])
        return sum_4(taps_a.at[n], 0)

    def taps_end():
        whole(taps_z.at[pl.ds(0, 7)], taps_recv.at[2])
        halves = sum_4(taps_z, 0), sum_4(taps_z, 4)
        for t in range(KW):
            block = halves[0][t] if t < 5 else halves[1][t - 4]
            for n in range(D // HD):
                dk_out[t : t + 1, n * HD : (n + 1) * HD] = block[n : n + 1, :]

    def taps(n):
        cols = pl.ds(mult(n * BF, BF), BF)
        sub = dot(att2[mine, :], wout_vm[:, cols]).astype(BF16).astype(F32)
        for t in range(KW):
            total = jnp.sum(sub * gp[pl.ds(12 - t, BF), cols], axis=0, keepdims=True)
            taps_c[t, pl.ds(2 * n, 1), :] = total[:, :HD]
            taps_c[t, pl.ds(2 * n + 1, 1), :] = total[:, HD:]

    def back(t, n):
        arrived(t)
        swap_half(n).start()
        own_half(n)

    def weight(n):
        swap_half(n).wait_recv()
        product(li_t, n * HALF, HALF)

    def d_input(n, carry):
        cols = pl.ds(mult(n * BF, BF), BF)
        din_vm[:, cols] = dot_nt(dqkv[...], wqkv_vm[cols, :]).astype(BF16)
        return carry

    lax.fori_loop(0, 2, lambda d, c: (d_query(d), c)[1], 0)
    arrived(BA)
    swap_att.start()
    lax.fori_loop(2, 4, lambda d, c: (d_query(d), c)[1], 0)

    swap_half(OUT).wait_recv()
    swap_att.wait_recv()
    turn_in(att2, att_t)
    product(att_t, OUT * HALF, HALF)
    rings[0][0].begin()
    lax.fori_loop(4, NC, lambda d, c: (d_query(d), c)[1], 0)
    local(BQ).start()

    def d_key(j):
        two = pl.ds(mult(j * 2 * BF, 2 * BF), 2 * BF)
        dk_s[pl.ds(j * 2, 2)] = (dot(ds_ref[two, :], q_aug[:, pl.ds(0, HD)]) * inv_root).astype(BF16).reshape(2, BF, HD)

        @pl.when(j > 0)
        def _():
            remote(BK, j * 2).start()

        remote(BK, j * 2 + 1).start()

    lax.fori_loop(0, 2, lambda j, c: (d_key(j), c)[1], 0)
    back(BV, VAL)
    rings[0][0].relay()
    lax.fori_loop(2, NC // 2, lambda j, c: (d_key(j), c)[1], 0)
    local(BK).start()
    weight(VAL)
    rings[1][0].begin()
    back(BQ, QUE)
    lax.fori_loop(0, D // BF, lambda n, c: (taps(n), c)[1], 0)
    swap_taps.start()
    weight(QUE)
    rings[2][0].begin()
    rings[3][0].begin()
    swap_taps.wait_recv()
    taps_on(0, "x", taps_c[pl.ds(core * 4, 5)] + taps_p[...])
    get_wq.wait()
    rings[1][0].relay()
    back(BK, KEY)
    lax.fori_loop(0, 1, d_input, 0)
    swap_half(KEY).wait_recv()
    product(li_t, KEY * HALF, HALF // 2)
    rings[4][0].begin()
    rings[2][0].relay()
    rings[3][0].relay()
    product(li_t, KEY * HALF + HALF // 2, HALF // 2)
    rings[5][0].begin()
    rings[6][0].begin()
    taps_on(1, "y", taps_sum(0))
    on(0, 0)
    lax.fori_loop(1, 4, d_input, 0)
    on(1, 0)
    rings[4][0].relay()
    on(2, 0)
    on(3, 0)
    on(5, 0)
    on(6, 0)
    taps_last("z", taps_sum(1))
    on(0, 1)
    on(4, 0)
    on(5, 1)
    on(6, 1)
    on(1, 1)
    on(2, 1)
    on(3, 1)
    whole(att2.at[pl.ds(0, 32), :], halo_send)
    drain(send_sem, 8 * (NC - 1) * BF * HD * 2)
    drain(core_send.at[0], 4 * BF * D * 2)
    swap_taps.wait_send()
    for n in (0, 1):
        whole(taps_a.at[n, pl.ds(0, 3)], taps_send.at[n])
    whole(taps_z.at[pl.ds(0, 7)], taps_send.at[2])
    ring_width = sum(PARTS[p][1] for p in RINGS)
    drain(ring_send, 3 * BF * ring_width * 2)
    drain(step_send.at[0], 3 * BF * (CW - ring_width) * 2)
    rows = 3 * BF // 4 * (CW - PARTS[PLANE][1]) * 2 // (4 * HD)
    whole(q_aug.at[pl.ds(0, rows), :], step_send.at[1])
    for p in (0, 5, 6, 1):
        rings[p][2].end()
    rings[4][1].end()
    for p in (2, 3):
        rings[p][2].end()
    taps_end()
    whole(do_in.at[pl.ds(0, 7 * 8 * CW * 2 // (2 * HD)), :], last_send)
    whole(do_in.at[pl.ds(0, 31 * 16), :], plane_send)


def collect_kernel(*refs):
    ins, outs, sems = refs[:4], refs[4:8], refs[8]
    copies = [pltpu.make_async_copy(a, b, sems.at[n]) for n, (a, b) in enumerate(zip(ins, outs))]
    for c in copies:
        c.start()
    for c in copies:
        c.wait()


def backward(lengths, li, q, k, v, g, conv, wout, wqkv):
    def vm(shape, dtype=BF16):
        return pltpu.VMEM(shape, dtype)

    buffers = []
    for p, (_, width, order) in enumerate(PARTS):
        leads = []
        for stage in range(3):
            sizes = (("zl", 2), ("y", 4), ("zh", 2), ("x", 4))
            leads.append([n for axis, n in sizes if axis[0] not in order[: stage + 1]])
        halves = [(*leads[0], 16, width // 2)] * 2
        sides = 2 if p in RINGS else 3
        buffers += [vm(shape) for shape in (*halves, (sides, *leads[0], 16, width))]
        buffers.append(vm((3, *leads[1], 16, width)))
        block, kind = ((16, width // 2), BF16) if width > HD else ((8, width), F32)
        lead, count = (leads[0], 31) if p == PLANE else (leads[1], 7)
        buffers.append(vm((*lead, 2, *block), kind))
        buffers.append(vm((count, *block), kind))
    dma = pltpu.SemaphoreType.DMA
    outs = (
        jax.ShapeDtypeStruct((BF, D), BF16),
        jax.ShapeDtypeStruct((8, 3 * D), F32),
        jax.ShapeDtypeStruct((8, D), F32),
        jax.ShapeDtypeStruct((KW, D), F32),
    )
    results = pl.pallas_call(
        backward_kernel,
        out_shape=tuple(pltpu.VMEM(o.shape, o.dtype) for o in outs),
        in_specs=[ANY] * 9,
        out_specs=(VM,) * 4,
        scratch_shapes=[
            vm((T, 2 * HD)), vm((T, 2 * HD)), vm((T, 2 * HD)), vm((T, HD)), vm((T, 2 * HD)),
            vm((HD, T)), vm((HD + 16, T)), vm((T, BF), F32), vm((T, T)), vm((T, T)),
            vm((NC, BF, HD)), vm((NC, BF, HD), F32), vm((NC, BF, HD)), vm((NC, BF, HD)),
            vm((NC, BF, HD)), vm((NC, BF, HD)), vm((BF, 3 * D)),
            vm((BF, D)), vm((BF + 16, D), F32), vm((BF, D)), vm((16, D)), vm((16, D)),
            vm((D, D)), vm((D, 3 * D)),
            vm((2 * BF, D)), vm((2 * BF, D)), vm((2 * BF, CW)), vm((D, 2 * BF)), vm((D, 2 * BF)),
            vm((2, 4, 2, 4, 16, CW)),
            vm((KW, 8, HD), F32), vm((5, 8, HD), F32), vm((2, 4, 5, 8, HD), F32), vm((8, 5, 8, HD), F32),
            vm((KW, D), F32), pltpu.SMEM((1,), jnp.int32), *buffers,
            dma(()), dma((8,)), dma((NC,)), dma(()), dma((2,)), dma((6,)), dma((2,)), dma((7,)),
            dma(()), dma((len(RINGS) * 3,)), dma((2,)), dma((2 * NP,)), dma(()), dma((NP,)),
            dma((3,)), dma((3,)), dma(()), dma(()),
        ],
        compiler_params=pltpu.CompilerParams(
            collective_id=0, has_side_effects=True, vmem_limit_bytes=60 * 1024 * 1024
        ),
    )(lengths, li, q, k, v, g, conv, wout, wqkv)
    results = [pltpu.with_memory_space_constraint(r, pltpu.VMEM) for r in results]
    return pl.pallas_call(
        collect_kernel,
        out_shape=outs,
        in_specs=[VM] * 4,
        out_specs=(ANY,) * 4,
        scratch_shapes=[dma((4,))],
    )(*results)


def shards(layer_in, queries, keys, values, lengths, w_qkv, w_out, conv_kernel, grad_out):
    d_input, d_wqkv, d_wout, d_kernel = backward(
        lengths, layer_in[0], queries[0], keys[0], values[0], grad_out[0], conv_kernel, w_out, w_qkv
    )
    return d_input[None], d_wqkv, d_wout, d_kernel


def solution(mesh):
    frames = P("rec", "ctx", None)
    in_specs = (frames, frames, frames, frames, P("rec"), P(), P(), P(), frames)
    out_specs = (frames, P(("ctx", "rec"), None), P(("ctx", "rec"), None), P())
    return jax.shard_map(
        shards, mesh=mesh, in_specs=in_specs, out_specs=out_specs, check_vma=False
    )
```
